32 devices in a mesh: row: 2 (over x), col: 16 (over z, y, core).
Axes of the slice: x: 2, y: 2, z: 4, core: 2. Of those that a mesh axis runs over, the one named last changes fastest.
Arguments:
- features: float32 [8192, 128], P(('row', 'col')), may hold values from -6 to 6
- weight: float32 [128, 256], replicated, may hold values from -0.5 to 0.5
- out_bias: float32 [256], replicated, may hold values from -3 to 3
- cotangent: float32 [8192, 256], P(('row', 'col')), may hold values from -6 to 6
- drop_keep: int32 [8192, 256], P(('row', 'col')), may hold values 0 or 1
- tile_cols: int32 [2, 16, 32, 4], P('row', 'col'), may hold values from 0 to 3, as said below
- tile_edge_counts: int32 [2, 16, 32, 4], P('row', 'col'), may hold values from 1 to 64, as said below
- edge_pos: int32 [2, 16, 32, 256], P('row', 'col'), may hold values from 0 to 16383
- edge_keep_bits: int32 [2, 16, 32, 256], P('row', 'col'), may hold values 0 or 1
Outputs:
- hidden_out: float32 [8192, 256], P(('row', 'col'))
- grad_features: float32 [8192, 128], P(('row', 'col'))
- grad_weight: float32 [128, 256], replicated
The draws below stay inside these ranges and needn't reach their ends.
Inputs may be any that keep to these rules, and one draw needn't show every extreme that they name: `tile_cols`: the 4 source tile columns of one tile-row of a device block are distinct. A tile's edges are its first tile_edge_counts slots; the slots at and after the count are unused.
All inputs are finite; a program needn't handle non-finite values. No bound on the sum of `drop_keep` or of `edge_keep_bits` on one device may be relied on, other than what follows from the above.
Results may differ from the reference program's by a relative error of at most 0.000071.
Values sent between devices are 32-bit elements; how exact they have to be, the bound alone decides.
No kernel may reach another device: no remote copies, remote signals or barrier semaphores. Data moves between devices by JAX's collectives and lax.ppermute only.
A program may use at most 64 MiB of HBM per device.

```python
import jax
import jax.numpy as jnp
from jax import lax

FIN = 128
FH = 256
TILE_SIDE = 128
TPR = 4
EPT = 64
ND = 256
GRID_ROWS = 2
GRID_COLS = 16
NODES = 8192
DST_TILES = 32
SRC_TILES = 4
EDGE_SLOTS = 256


def draw_tile_cols(key, part):
    row_total = GRID_ROWS * GRID_COLS * DST_TILES
    scores = jax.random.randint(key, (row_total, SRC_TILES), 0, 1 << 20) * SRC_TILES + jnp.arange(SRC_TILES, dtype=jnp.int32)[None, :]
    ranked = jnp.argsort(scores, axis=1)
    return ranked[:, :TPR].astype(jnp.int32).reshape(GRID_ROWS, GRID_COLS, DST_TILES, TPR)


def draw_tile_edge_counts(key, part):
    counts = jax.random.randint(key, (GRID_ROWS, GRID_COLS, DST_TILES, TPR), 1, EPT + 1)
    return counts.at[:, :, 0, 0].set(EPT).astype(jnp.int32)


def place_ends(drawn, key, low, high):
    longest = drawn.shape.index(max(drawn.shape))
    spots = []
    for shift in (0, 1):
        where = [jax.random.randint(jax.random.fold_in(key, axis), (), 0, length) for axis, length in enumerate(drawn.shape)]
        where[longest] = (where[longest] + shift) % drawn.shape[longest]
        spots.append(tuple(where))
    return drawn.at[spots[0]].set(low).at[spots[1]].set(high)


def block_scale(rng, extent, pieces, low, high):
    def one(dim, blocks):
        draws = jax.random.uniform(jax.random.fold_in(jax.random.fold_in(rng, 6), dim), (blocks,), jnp.float32, low / len(pieces), high / len(pieces))
        return jnp.repeat(jnp.exp(draws), extent[dim] // blocks).reshape((-1,) + (1,) * (len(extent) - dim - 1))

    level = one(*pieces[0])
    for cut in pieces[1:]:
        level = level * one(*cut)
    return level


def centred(stream_key, dims, width, limit, cuts=(), held_as=jnp.bfloat16):
    array = jax.random.normal(stream_key, dims, jnp.float32) * width
    if len(cuts) > 0:
        array = block_scale(stream_key, dims, cuts, -0.22, 0.18) * array
    return jnp.clip(array, min=-limit, max=limit).astype(held_as)


def setup_inputs(seed: int = 0) -> dict:
    seeds = jax.random.split(jax.random.key(seed), 10)
    features = centred(seeds[0], (NODES, FIN), 1.0, 6.0, ((0, 32),), jnp.float32)
    weight = centred(seeds[1], (FIN, FH), FIN ** -0.5, 0.5, (), jnp.float32)
    out_bias = centred(seeds[2], (FH,), 0.5, 3.0, (), jnp.float32)
    cotangent = centred(seeds[3], (NODES, FH), 1.0, 6.0, ((0, 32),), jnp.float32)
    drop_keep = place_ends((jax.random.randint(seeds[4], (NODES, FH), 0, 10) < 9).astype(jnp.int32), jax.random.fold_in(seeds[4], 1), 0, 1)
    tile_cols = draw_tile_cols(jax.random.fold_in(seeds[9], 71), 0)
    tile_edge_counts = draw_tile_edge_counts(jax.random.fold_in(seeds[9], 71), 0)
    edge_pos = place_ends(jax.random.randint(seeds[7], (GRID_ROWS, GRID_COLS, DST_TILES, EDGE_SLOTS), 0, TILE_SIDE * TILE_SIDE), jax.random.fold_in(seeds[7], 1), 0, (TILE_SIDE * TILE_SIDE) - 1).astype(jnp.int32)
    edge_keep_bits = place_ends((jax.random.randint(seeds[8], (GRID_ROWS, GRID_COLS, DST_TILES, EDGE_SLOTS), 0, 5) < 4).astype(jnp.int32), jax.random.fold_in(seeds[8], 1), 0, 1)
    return {"features": features, "weight": weight, "out_bias": out_bias, "cotangent": cotangent, "drop_keep": drop_keep, "tile_cols": tile_cols, "tile_edge_counts": tile_edge_counts, "edge_pos": edge_pos, "edge_keep_bits": edge_keep_bits}


keep_rate = 0.9

def gelu_exact(values):
    return 0.5 * values * (1.0 + lax.erf(values * 0.7071067811865476))

def gelu_slope(values):
    return 0.5 * (1.0 + lax.erf(values * 0.7071067811865476)) + values * jnp.exp(-0.5 * values * values) * 0.3989422804014327

def edge_lists(tile_cols, tile_edge_counts, edge_pos, edge_keep_bits):
    slot_ids = jnp.arange(EDGE_SLOTS, dtype=jnp.int32)
    tile_of = slot_ids // EPT
    slot_place = slot_ids % EPT
    count_slot = tile_edge_counts[:, :, :, tile_of]
    column_slot = tile_cols[:, :, :, tile_of]
    live_mask = jnp.where((slot_place[None, None, None, :] < count_slot) & (edge_keep_bits == 1), 1.0, 0.0).astype(jnp.float32)
    tile_row = jnp.arange(DST_TILES, dtype=jnp.int32)[None, None, :, None]
    grid_row = jnp.arange(GRID_ROWS, dtype=jnp.int32)[:, None, None, None]
    grid_col = jnp.arange(GRID_COLS, dtype=jnp.int32)[None, :, None, None]
    target = grid_row * (GRID_COLS * ND) + tile_row * TILE_SIDE + edge_pos // TILE_SIDE
    source_local = column_slot * TILE_SIDE + edge_pos % TILE_SIDE
    source = (source_local // ND * GRID_COLS + grid_col) * ND + source_local % ND
    flat_count = GRID_ROWS * GRID_COLS
    return (target.reshape(flat_count, -1).astype(jnp.int32), source.reshape(flat_count, -1).astype(jnp.int32), live_mask.reshape(flat_count, -1))

def reference(features, weight, out_bias, cotangent, drop_keep, tile_cols, tile_edge_counts, edge_pos, edge_keep_bits):
    highest = lax.Precision.HIGHEST
    target, source, live_mask = edge_lists(tile_cols, tile_edge_counts, edge_pos, edge_keep_bits)
    degree = 1.0 + jax.ops.segment_sum(live_mask.ravel(), target.ravel(), num_segments=NODES)
    inv_root = lax.rsqrt(degree)[:, None]
    transformed = jnp.dot(features, weight, precision=highest, preferred_element_type=jnp.float32)
    scaled_rows = inv_root * transformed

    def forward_step(running_total, single_edge):
        target_nodes, source_nodes, surviving_mask = single_edge
        return (running_total.at[target_nodes].add(surviving_mask[:, None] * scaled_rows[source_nodes]), None)
    summed, _ = lax.scan(forward_step, jnp.zeros((NODES, FH), jnp.float32), (target, source, live_mask))
    pre_act = inv_root * (summed + scaled_rows) + out_bias[None, :]
    dropout = drop_keep.astype(jnp.float32) / keep_rate
    hidden_out = gelu_exact(pre_act) * dropout
    grad_pre = cotangent * dropout * gelu_slope(pre_act)
    backward_scaled_rows = inv_root * grad_pre

    def backward_step(running_total, single_edge):
        target_nodes, source_nodes, surviving_mask = single_edge
        return (running_total.at[source_nodes].add(surviving_mask[:, None] * backward_scaled_rows[target_nodes]), None)
    returned, _ = lax.scan(backward_step, jnp.zeros((NODES, FH), jnp.float32), (target, source, live_mask))
    grad_z = inv_root * (returned + backward_scaled_rows)
    grad_features = jnp.dot(grad_z, weight.T, precision=highest, preferred_element_type=jnp.float32)
    grad_weight = jnp.dot(features.T, grad_z, precision=highest, preferred_element_type=jnp.float32)
    return (hidden_out, grad_features, grad_weight)
```

```python
import functools

import jax
import jax.numpy as jnp
from jax import lax
from jax.experimental import pallas as pl
from jax.experimental.pallas import tpu as pltpu
from jax.sharding import PartitionSpec as P

TILE_SIDE = 128
TPR = 4
EPT = 64
KEEP_RATE = 0.9

f32 = jnp.float32
bf16 = jnp.bfloat16
i32 = jnp.int32
highest = lax.Precision.HIGHEST
NT = (((1,), (1,)), ((), ()))
TN = (((0,), (0,)), ((), ()))
MIB = 1 << 20


def gelu_exact(values):
    return 0.5 * values * (1.0 + lax.erf(values * 0.7071067811865476))


def gelu_slope(values):
    return (
        0.5 * (1.0 + lax.erf(values * 0.7071067811865476))
        + values * jnp.exp(-0.5 * values * values) * 0.3989422804014327
    )


def one_hot(index_row, size):
    places = lax.broadcasted_iota(i32, (size, index_row.shape[1]), 0)
    return jnp.where(places == index_row, 1.0, 0.0).astype(bf16)


def pack_kernel(cols_ref, counts_ref, pos_ref, keep_ref, packed_ref, degree_ref):
    rows, slots = pos_ref.shape
    slot = lax.broadcasted_iota(i32, (rows, slots), 1)
    tile = lax.shift_right_arithmetic(slot, 6)
    count = jnp.zeros((rows, slots), i32)
    col = jnp.zeros((rows, slots), i32)
    for k in range(TPR):
        count = jnp.where(tile == k, counts_ref[:, k : k + 1], count)
        col = jnp.where(tile == k, cols_ref[:, k : k + 1], col)
    live = ((slot & (EPT - 1)) < count) & (keep_ref[...] == 1)
    pos = pos_ref[...]
    source = col * TILE_SIDE + (pos & (TILE_SIDE - 1))
    target = jnp.where(live, lax.shift_right_arithmetic(pos, 7), -1)
    packed = jnp.where(live, source * TILE_SIDE + target, -1)
    packed_ref[...] = packed
    ones = jnp.ones((8, slots), bf16)
    for t in range(rows):
        hot = one_hot(target[t : t + 1, :], TILE_SIDE)
        sums = lax.dot_general(ones, hot, NT, preferred_element_type=f32)
        degree_ref[t : t + 1, :] = sums[0:1, :]


def own_block_kernel(group, me_ref, packed_ref, block_ref):
    c = pl.program_id(0)
    sources = block_ref.shape[1]
    per_group = group // TILE_SIDE
    for s in range(per_group):
        row = packed_ref[pl.ds(c * per_group + s, 1), :]
        source = lax.shift_right_arithmetic(row, 7) - me_ref[0] * group
        source = jnp.where(source < 0, source + sources, source)
        target = jnp.where(row >= 0, row & (TILE_SIDE - 1), -1)
        hot = lax.dot_general(
            one_hot(source, sources), one_hot(target, TILE_SIDE), NT, preferred_element_type=f32
        )
        block_ref[0, :, s * TILE_SIDE : (s + 1) * TILE_SIDE] = hot.astype(bf16)


def turned_block_kernel(group, grid_rows, grid_cols, me_ref, edges_ref, block_ref):
    c = pl.program_id(0)
    per_group = group // TILE_SIDE
    slots = edges_ref.shape[1] // per_group
    for k in range(grid_rows):
        r = lax.rem(me_ref[0] + k, grid_rows)
        for s in range(per_group):
            row = edges_ref[pl.ds(r * grid_cols + c, 1), s * slots : (s + 1) * slots]
            source = lax.shift_right_arithmetic(row, 7) - me_ref[0] * group
            target = row & (TILE_SIDE - 1)
            hot = lax.dot_general(
                one_hot(target, TILE_SIDE), one_hot(source, group), NT, preferred_element_type=f32
            )
            at = (k * per_group + s) * TILE_SIDE
            block_ref[0, at : at + TILE_SIDE, :] = hot.astype(bf16)


def spread_down(row):
    return jnp.broadcast_to(row, (TILE_SIDE, TILE_SIDE)).T


def halves(values):
    high = values.astype(bf16)
    low = (values - high.astype(f32)).astype(bf16)
    return high, low


def sum_kernel(scaled, *refs):
    if scaled:
        degree_ref, block_ref, value_ref, own_ref, other_ref, total_ref = refs
    else:
        block_ref, value_ref, own_ref, other_ref, total_ref = refs
    c = pl.program_id(0)
    group, width = value_ref.shape
    values = value_ref[...]
    if scaled:
        per_group = group // TILE_SIDE
        scale = jnp.concatenate(
            [
                spread_down(lax.rsqrt(1.0 + degree_ref[pl.ds(c * per_group + s, 1), :]))
                for s in range(per_group)
            ],
            axis=0,
        )
        values = values * scale[:, :1] if width != TILE_SIDE else values * scale
    both = jnp.concatenate(halves(values), axis=1)
    part = jnp.dot(block_ref[0], both, preferred_element_type=f32)

    @pl.when(c == 0)
    def _():
        total_ref[...] = part

    @pl.when(c > 0)
    def _():
        total_ref[...] += part

    @pl.when(c == pl.num_programs(0) - 1)
    def _():
        total = total_ref[...]
        total = total[:, :width] + total[:, width:]
        own_ref[...] = total[:group]
        other_ref[...] = total[group:]


def middle_kernel(
    me_ref,
    own_ref,
    got_ref,
    degree_ref,
    features_ref,
    weight_ref,
    bias_ref,
    cotangent_ref,
    drop_ref,
    hidden_ref,
    sent_ref,
    scale_ref,
    weight_grad_ref,
):
    group, width = features_ref.shape
    per_group = group // TILE_SIDE
    scale = jnp.concatenate(
        [
            spread_down(lax.rsqrt(1.0 + degree_ref[pl.ds(me_ref[0] * per_group + s, 1), :]))
            for s in range(per_group)
        ],
        axis=0,
    )[:, :width]
    scale_ref[...] = scale
    total = own_ref[...]
    for k in range(got_ref.shape[0] // group):
        total = total + got_ref[k * group : (k + 1) * group, :]
    mixed = scale * (total + scale * features_ref[...])
    weight = weight_ref[...]
    pre_act = jnp.dot(mixed, weight, precision=highest, preferred_element_type=f32) + bias_ref[...]
    dropout = drop_ref[...].astype(f32) / KEEP_RATE
    hidden_ref[...] = gelu_exact(pre_act) * dropout
    grad_pre = cotangent_ref[...] * dropout * gelu_slope(pre_act)
    sent_ref[...] = scale * lax.dot_general(
        grad_pre, weight, NT, precision=highest, preferred_element_type=f32
    )
    weight_grad_ref[...] = lax.dot_general(
        mixed, grad_pre, TN, precision=highest, preferred_element_type=f32
    )


def shards(
    features,
    weight,
    out_bias,
    cotangent,
    drop_keep,
    tile_cols,
    tile_edge_counts,
    edge_pos,
    edge_keep_bits,
):
    grid_rows, grid_cols = lax.axis_size("row"), lax.axis_size("col")
    my_row, my_col = lax.axis_index("row"), lax.axis_index("col")
    group, width = features.shape
    hidden = weight.shape[1]
    rows, slots = edge_pos.shape[2:]
    per_group = group // TILE_SIDE
    block_side = grid_rows * group
    row_id, col_id = my_row[None].astype(i32), my_col[None].astype(i32)
    smem = pl.BlockSpec(memory_space=pltpu.SMEM)
    limit = pltpu.CompilerParams(vmem_limit_bytes=48 * MIB)

    packed, degree = pl.pallas_call(
        pack_kernel,
        out_shape=(
            jax.ShapeDtypeStruct((rows, slots), i32),
            jax.ShapeDtypeStruct((rows, TILE_SIDE), f32),
        ),
        compiler_params=limit,
        cost_estimate=pl.CostEstimate(flops=2**21, bytes_accessed=2**17, transcendentals=0),
        name="pack",
    )(tile_cols[0, 0], tile_edge_counts[0, 0], edge_pos[0, 0], edge_keep_bits[0, 0])

    gathered = lax.all_gather(features, "col", axis=0, tiled=True)

    pieces = packed.reshape(1, grid_cols, per_group * slots)
    pieces = jnp.broadcast_to(pieces, (grid_rows, grid_cols, per_group * slots))
    edges = lax.all_to_all(
        pieces.reshape(grid_rows * grid_cols, per_group * slots), ("row", "col"), 0, 0, tiled=True
    )

    bit = 1
    while bit < grid_cols:
        degree = degree + lax.ppermute(degree, "col", [(p, p ^ bit) for p in range(grid_cols)])
        bit *= 2

    formation = pl.CostEstimate(
        flops=2 * rows * slots * TILE_SIDE * block_side,
        bytes_accessed=2 * rows * TILE_SIDE * block_side,
        transcendentals=0,
    )
    block_shape = jax.ShapeDtypeStruct((grid_cols, block_side, group), bf16)
    block_spec = pl.BlockSpec((1, block_side, group), lambda c: (c, 0, 0))
    own_block = pl.pallas_call(
        functools.partial(own_block_kernel, group),
        grid=(grid_cols,),
        in_specs=[smem, pl.BlockSpec((rows, slots), lambda c: (0, 0))],
        out_specs=block_spec,
        out_shape=block_shape,
        compiler_params=limit,
        cost_estimate=formation,
        name="own_block",
    )(row_id, packed)
    turned_block = pl.pallas_call(
        functools.partial(turned_block_kernel, group, grid_rows, grid_cols),
        grid=(grid_cols,),
        in_specs=[smem, pl.BlockSpec(edges.shape, lambda c: (0, 0))],
        out_specs=block_spec,
        out_shape=block_shape,
        compiler_params=limit,
        cost_estimate=formation,
        name="turned_block",
    )(row_id, edges)

    def block_sum(block, values, node_degree=None):
        scaled = node_degree is not None
        return pl.pallas_call(
            functools.partial(sum_kernel, scaled),
            grid=(grid_cols,),
            in_specs=([pl.BlockSpec((rows, TILE_SIDE), lambda c: (0, 0))] if scaled else [])
            + [block_spec, pl.BlockSpec((group, width), lambda c: (c, 0))],
            out_specs=(
                pl.BlockSpec((group, width), lambda c: (0, 0)),
                pl.BlockSpec((block_side - group, width), lambda c: (0, 0)),
            ),
            out_shape=(
                jax.ShapeDtypeStruct((group, width), f32),
                jax.ShapeDtypeStruct((block_side - group, width), f32),
            ),
            scratch_shapes=[pltpu.VMEM((block_side, 2 * width), f32)],
            compiler_params=limit,
            cost_estimate=pl.CostEstimate(
                flops=4 * rows * TILE_SIDE * block_side * width,
                bytes_accessed=2 * rows * TILE_SIDE * block_side,
                transcendentals=0,
            ),
            name="forward_sum" if scaled else "backward_sum",
        )(*([node_degree] if scaled else []), block, values)

    def to_owners(others):
        got = [
            lax.ppermute(
                others[k * group : (k + 1) * group],
                "row",
                [(p, (p + k + 1) % grid_rows) for p in range(grid_rows)],
            )
            for k in range(grid_rows - 1)
        ]
        return got[0] if len(got) == 1 else jnp.concatenate(got, axis=0)

    own, others = block_sum(turned_block, gathered, degree)
    got = to_owners(others)

    hidden_out, sent, scale, weight_grad = pl.pallas_call(
        middle_kernel,
        in_specs=[smem] + [pl.BlockSpec(memory_space=pltpu.VMEM)] * 8,
        out_shape=(
            jax.ShapeDtypeStruct((group, hidden), f32),
            jax.ShapeDtypeStruct((group, width), f32),
            jax.ShapeDtypeStruct((group, width), f32),
            jax.ShapeDtypeStruct((width, hidden), f32),
        ),
        compiler_params=limit,
        cost_estimate=pl.CostEstimate(
            flops=36 * group * width * hidden, bytes_accessed=2**20, transcendentals=2**18
        ),
        name="middle",
    )(
        col_id,
        own,
        got,
        degree,
        features,
        weight,
        out_bias.reshape(1, hidden),
        cotangent,
        drop_keep,
    )

    collected = lax.all_gather(sent, "col", axis=0, tiled=True)
    for axis, size in (("col", grid_cols), ("row", grid_rows)):
        bit = 1
        while bit < size:
            weight_grad = weight_grad + lax.ppermute(
                weight_grad, axis, [(p, p ^ bit) for p in range(size)]
            )
            bit *= 2
    own, others = block_sum(own_block, collected)
    got = to_owners(others)
    total = own
    for k in range(grid_rows - 1):
        total = total + got[k * group : (k + 1) * group]
    grad_features = scale * (total + sent)
    return (hidden_out, grad_features, weight_grad)


def solution(mesh):
    in_specs = (
        P(("row", "col"), None),
        P(),
        P(),
        P(("row", "col"), None),
        P(("row", "col"), None),
        P("row", "col", None, None),
        P("row", "col", None, None),
        P("row", "col", None, None),
        P("row", "col", None, None),
    )
    out_specs = (P(("row", "col"), None), P(("row", "col"), None), P())
    return jax.shard_map(shards, mesh=mesh, in_specs=in_specs, out_specs=out_specs, check_vma=False)
```

```python
import functools

import jax
import jax.numpy as jnp
from jax import lax
from jax.experimental import pallas as pl
from jax.experimental.pallas import tpu as pltpu
from jax.sharding import PartitionSpec as P

TILE_SIDE = 128
TPR = 4
EPT = 64
KEEP_RATE = 0.9
CORES = 2
DEPTH = 4

f32 = jnp.float32
bf16 = jnp.bfloat16
i32 = jnp.int32
highest = lax.Precision.HIGHEST
NT = (((1,), (1,)), ((), ()))
TN = (((0,), (0,)), ((), ()))
MIB = 1 << 20


class Grid:
    def __init__(self, rows, cols, group):
        self.rows, self.cols, self.group = rows, cols, group
        self.wide = cols // (DEPTH * CORES)
        self.count = rows * cols
        self.per = group // TILE_SIDE
        self.gathered = DEPTH * CORES
        self.summed = rows * self.wide

    def place(self, me):
        col = lax.rem(me, self.cols)
        core = lax.rem(col, CORES)
        rest = lax.div(col, CORES)
        return lax.div(me, self.cols), lax.rem(rest, self.wide), lax.div(rest, self.wide), core

    def col(self, z, y, core):
        return (z * self.wide + y) * CORES + core

    def number(self, x, y, z, core):
        return x * self.cols + self.col(z, y, core)

    def all_places(self):
        return [
            (x, y, z, core)
            for x in range(self.rows)
            for z in range(DEPTH)
            for y in range(self.wide)
            for core in range(CORES)
        ]

    def pairs(self, move):
        return [(self.number(*p), self.number(*move(*p))) for p in self.all_places()]


def gelu_exact(values):
    return 0.5 * values * (1.0 + lax.erf(values * 0.7071067811865476))


def gelu_slope(values):
    return (
        0.5 * (1.0 + lax.erf(values * 0.7071067811865476))
        + values * jnp.exp(-0.5 * values * values) * 0.3989422804014327
    )


def one_hot(index_row, size):
    places = lax.broadcasted_iota(i32, (size, index_row.shape[1]), 0)
    return jnp.where(places == index_row, 1.0, 0.0).astype(bf16)


def turned_times(values, table):
    return lax.dot_general(
        values.astype(f32).astype(bf16), table, TN, preferred_element_type=f32
    ).astype(i32)


def pack_kernel(grid, cols_ref, counts_ref, pos_ref, keep_ref, lists_ref, pieces_ref):
    rows, slots = pos_ref.shape
    slot = lax.broadcasted_iota(i32, (rows, slots), 1)
    tile_of = lax.broadcasted_iota(i32, (TPR, slots), 1) // EPT
    spread = jnp.where(tile_of == lax.broadcasted_iota(i32, (TPR, slots), 0), 1.0, 0.0)
    count = turned_times(counts_ref[...], spread.astype(bf16))
    live = ((slot & (EPT - 1)) < count) & (keep_ref[...] == 1)
    pos = jnp.where(live, pos_ref[...], -1)
    lists_ref[:, :slots] = pos
    lane = lax.broadcasted_iota(i32, (TPR, TILE_SIDE), 1)
    k = lax.broadcasted_iota(i32, (TPR, TILE_SIDE), 0)
    placed = [
        turned_times(cols_ref[...], jnp.where(lane == u * TPR + k, 1.0, 0.0).astype(bf16))
        for u in range(grid.wide * grid.per)
    ]
    lists_ref[:, slots:] = placed[0]
    target = lax.shift_right_arithmetic(pos, 7)
    ones = jnp.ones((8, slots), bf16)
    degrees = []
    for t in range(rows):
        hot = one_hot(target[t : t + 1, :], TILE_SIDE)
        sums = lax.dot_general(ones, hot, NT, preferred_element_type=f32)
        degrees.append(sums[0:1, :].astype(i32))
    at_cols = grid.wide * grid.per * slots
    at_degrees = at_cols + TILE_SIDE
    for z in range(DEPTH):
        for core in range(CORES):
            parts = []
            columns = 0
            for y in range(grid.wide):
                for s in range(grid.per):
                    t = grid.col(z, y, core) * grid.per + s
                    parts.append(pos[t : t + 1, :])
                    columns = columns + placed[y * grid.per + s][t : t + 1, :]
            parts.append(columns)
            shared = jnp.concatenate(parts, axis=1)
            for y in range(grid.wide):
                t = grid.col(z, y, core) * grid.per
                own = jnp.concatenate(degrees[t : t + grid.per], axis=1)
                for x in range(grid.rows):
                    n = grid.number(x, y, z, core)
                    pieces_ref[n, :, :at_degrees] = shared
                    pieces_ref[n, :, at_degrees:] = own


def roots_kernel(grid, me_ref, edges_ref, roots_ref):
    x = lax.div(me_ref[0], grid.cols)
    at = edges_ref.shape[2] - grid.group
    counts = edges_ref[pl.ds(x * grid.cols, grid.cols), :, at:]
    root = lax.rsqrt(1.0 + jnp.sum(counts, axis=0).astype(f32))
    for g in range(grid.gathered):
        roots_ref[g] = root


def slot_columns(columns, first, slots):
    tile = lax.broadcasted_iota(i32, (1, slots), 1) // EPT
    spread = jnp.broadcast_to(columns[:, first : first + 1], (1, slots))
    for k in range(1, TPR):
        spread = jnp.where(tile == k, columns[:, first + k : first + k + 1], spread)
    return spread


def forward_block_kernel(grid, slots, me_ref, edges_ref, block_ref):
    g = pl.program_id(0)
    x, y, z, core = grid.place(me_ref[0])
    from_z = z ^ lax.div(g, CORES)
    from_core = core ^ lax.rem(g, CORES)
    at_cols = grid.wide * grid.per * slots
    for to_y in range(grid.wide):
        for to_x in range(grid.rows):
            n = grid.number(to_x, y, from_z, from_core)
            columns = edges_ref[n, :, at_cols : at_cols + TILE_SIDE]
            for s in range(grid.per):
                u = to_y * grid.per + s
                pos = edges_ref[n, :, u * slots : (u + 1) * slots]
                target = lax.shift_right_arithmetic(pos, 7)
                source = slot_columns(columns, u * TPR, slots) * TILE_SIDE + (pos & (TILE_SIDE - 1))
                hot = lax.dot_general(
                    one_hot(target, TILE_SIDE),
                    one_hot(source - x * grid.group, grid.group),
                    NT,
                    preferred_element_type=f32,
                )
                at = ((to_y * grid.rows + to_x) * grid.per + s) * TILE_SIDE
                block_ref[at : at + TILE_SIDE, :] = hot.astype(bf16)


def backward_block_kernel(grid, slots, me_ref, *refs):
    lists, block_ref = refs[:-1], refs[-1]
    g = pl.program_id(0)
    x, y, z, core = grid.place(me_ref[0])
    col = grid.col(z ^ lax.div(g, CORES), y, core ^ lax.rem(g, CORES))
    side = grid.rows * grid.group
    for k, list_ref in enumerate(lists):
        for s in range(grid.per):
            row = list_ref[pl.ds(col * grid.per + s, 1), :]
            pos = row[:, :slots]
            target = lax.shift_right_arithmetic(pos, 7)
            source = slot_columns(row[:, slots:], 0, slots) * TILE_SIDE + (pos & (TILE_SIDE - 1))
            hot = lax.dot_general(
                one_hot(source, side), one_hot(target, TILE_SIDE), NT, preferred_element_type=f32
            )
            block_ref[k * side : (k + 1) * side, s * TILE_SIDE : (s + 1) * TILE_SIDE] = hot.astype(
                bf16
            )


def spread_down(row):
    return jnp.concatenate(
        [
            jnp.broadcast_to(row[:, a : a + TILE_SIDE], (TILE_SIDE, TILE_SIDE)).T
            for a in range(0, row.shape[1], TILE_SIDE)
        ],
        axis=0,
    )


def sum_kernel(grid, scaled, me_ref, *refs):
    if scaled:
        roots_ref, refs = refs[0], refs[1:]
    block_ref, refs = refs[0], refs[1:]
    values, refs = refs[: grid.gathered], refs[grid.gathered :]
    outs, both_ref = refs[:-1], refs[-1]
    width = values[0].shape[1]
    step = pl.program_id(0)

    @pl.when(step == 0)
    def _():
        x, y, z, core = grid.place(me_ref[0])
        for g, ref in enumerate(values):
            value = ref[...]
            if scaled:
                n = (z ^ (g // CORES)) * CORES + (core ^ (g % CORES))
                value = value * spread_down(roots_ref[n])
            high = value.astype(bf16)
            rows = slice(g * grid.group, (g + 1) * grid.group)
            both_ref[rows, :width] = high
            both_ref[rows, width:] = (value - high.astype(f32)).astype(bf16)

    part = jnp.dot(block_ref[...], both_ref[...], preferred_element_type=f32)
    total = part[:, :width] + part[:, width:]
    for k, out_ref in enumerate(outs):

        @pl.when(step == k)
        def _(out_ref=out_ref):
            out_ref[...] = total


def middle_kernel(
    roots_ref,
    features_ref,
    weight_ref,
    bias_ref,
    cotangent_ref,
    drop_ref,
    *refs,
):
    sums, (hidden_ref, sent_ref, scale_ref, weight_grad_ref) = refs[:-4], refs[-4:]
    scale = spread_down(roots_ref[0])
    scale_ref[...] = scale
    total = scale * features_ref[...]
    for ref in sums:
        total = total + ref[...]
    mixed = scale * total
    weight = weight_ref[...]
    pre_act = jnp.dot(mixed, weight, precision=highest, preferred_element_type=f32) + bias_ref[...]
    dropout = drop_ref[...].astype(f32) / KEEP_RATE
    hidden_ref[...] = gelu_exact(pre_act) * dropout
    grad_pre = cotangent_ref[...] * dropout * gelu_slope(pre_act)
    sent_ref[...] = scale * lax.dot_general(
        grad_pre, weight, NT, precision=highest, preferred_element_type=f32
    )
    weight_grad_ref[...] = lax.dot_general(
        mixed, grad_pre, TN, precision=highest, preferred_element_type=f32
    )


def shards(
    features,
    weight,
    out_bias,
    cotangent,
    drop_keep,
    tile_cols,
    tile_edge_counts,
    edge_pos,
    edge_keep_bits,
):
    group, width = features.shape
    hidden = weight.shape[1]
    rows, slots = edge_pos.shape[2:]
    grid = Grid(lax.axis_size("row"), lax.axis_size("col"), group)
    both_axes = ("row", "col")
    me = lax.axis_index(both_axes).astype(i32)[None]
    smem = pl.BlockSpec(memory_space=pltpu.SMEM)
    vmem = pl.BlockSpec(memory_space=pltpu.VMEM)
    limit = pltpu.CompilerParams(vmem_limit_bytes=24 * MIB)

    def gather(values):
        blocks = []
        for dz in range(DEPTH):
            block = values
            if dz:
                block = lax.ppermute(
                    values, both_axes, grid.pairs(lambda x, y, z, c, dz=dz: (x, y, z ^ dz, c))
                )
            blocks.append(block)
        others = [
            lax.ppermute(block, both_axes, grid.pairs(lambda x, y, z, c: (x, y, z, c ^ 1)))
            for block in blocks
        ]
        return [block for pair in zip(blocks, others) for block in pair]

    sum_order = [(dx, dy) for dy in range(grid.wide) for dx in range(grid.rows)]

    def to_owners(sums):
        got = [sums[0]]
        for part, (dx, dy) in list(zip(sums, sum_order))[1:]:
            got.append(
                lax.ppermute(
                    part,
                    both_axes,
                    grid.pairs(
                        lambda x, y, z, c, dx=dx, dy=dy: (
                            (x + dx) % grid.rows,
                            (y + dy) % grid.wide,
                            z,
                            c,
                        )
                    ),
                )
            )
        return got

    piece = grid.wide * grid.per * slots + TILE_SIDE + group
    lists, pieces = pl.pallas_call(
        functools.partial(pack_kernel, grid),
        out_shape=(
            jax.ShapeDtypeStruct((rows, slots + TILE_SIDE), i32),
            jax.ShapeDtypeStruct((grid.count, 1, piece), i32),
        ),
        compiler_params=limit,
        cost_estimate=pl.CostEstimate(flops=2**21, bytes_accessed=2**17, transcendentals=0),
        name="pack",
    )(tile_cols[0, 0].T, tile_edge_counts[0, 0].T, edge_pos[0, 0], edge_keep_bits[0, 0])

    gathered = gather(features)
    edges = lax.all_to_all(pieces, both_axes, 0, 0, tiled=True)
    peer_lists = [lists] + [
        lax.ppermute(
            lists,
            both_axes,
            grid.pairs(lambda x, y, z, c, dy=dy: (x, (y - dy) % grid.wide, z, c)),
        )
        for dy in range(1, grid.wide)
    ]

    own_roots = pl.pallas_call(
        functools.partial(roots_kernel, grid),
        in_specs=[smem, vmem],
        out_shape=jax.ShapeDtypeStruct((grid.gathered, 1, group), f32),
        compiler_params=limit,
        cost_estimate=pl.CostEstimate(flops=2**14, bytes_accessed=2**16, transcendentals=0),
        name="roots",
    )(me, edges)
    roots = lax.all_to_all(
        own_roots,
        "col",
        0,
        0,
        tiled=True,
        axis_index_groups=[
            [grid.col(z, y, c) for z in range(DEPTH) for c in range(CORES)]
            for y in range(grid.wide)
        ],
    )

    side, depth = grid.summed * group, grid.gathered * group
    formation = pl.CostEstimate(
        flops=2 * rows * slots * TILE_SIDE * grid.rows * group,
        bytes_accessed=2 * side * depth,
        transcendentals=0,
    )

    def block_of(kernel, name, *operands):
        return pl.pallas_call(
            functools.partial(kernel, grid, slots),
            grid=(grid.gathered,),
            in_specs=[smem]
            + [pl.BlockSpec(a.shape, lambda g, a=a: (0,) * a.ndim) for a in operands],
            out_specs=pl.BlockSpec((side, group), lambda g: (0, g)),
            out_shape=jax.ShapeDtypeStruct((side, depth), bf16),
            compiler_params=limit,
            cost_estimate=formation,
            name=name,
        )(me, *operands)

    def block_sum(name, row_block, block, values, roots=None):
        scaled = roots is not None
        whole = pl.BlockSpec((group, width), lambda k, me_ref: (0, 0))
        return pl.pallas_call(
            functools.partial(sum_kernel, grid, scaled),
            grid_spec=pltpu.PrefetchScalarGridSpec(
                num_scalar_prefetch=1,
                grid=(grid.summed,),
                in_specs=([pl.BlockSpec(roots.shape, lambda k, me_ref: (0, 0, 0))] if scaled else [])
                + [pl.BlockSpec((group, depth), lambda k, me_ref: (row_block(k, me_ref), 0))]
                + [whole] * grid.gathered,
                out_specs=(whole,) * grid.summed,
                scratch_shapes=[pltpu.VMEM((depth, 2 * width), bf16)],
            ),
            out_shape=(jax.ShapeDtypeStruct((group, width), f32),) * grid.summed,
            compiler_params=limit,
            cost_estimate=pl.CostEstimate(
                flops=4 * side * depth * width, bytes_accessed=2 * side * depth, transcendentals=0
            ),
            name=name,
        )(me, *([roots] if scaled else []), block, *values)

    def forward_row(k, me_ref):
        x, y, _, _ = grid.place(me_ref[0])
        to_x = lax.rem(x + lax.rem(k, grid.rows), grid.rows)
        to_y = lax.rem(y + lax.div(k, grid.rows), grid.wide)
        return to_y * grid.rows + to_x

    def backward_row(k, me_ref):
        x, _, _, _ = grid.place(me_ref[0])
        to_x = lax.rem(x + lax.rem(k, grid.rows), grid.rows)
        return lax.div(k, grid.rows) * grid.rows + to_x

    forward_block = block_of(forward_block_kernel, "forward_block", edges)
    sums = to_owners(block_sum("forward_sum", forward_row, forward_block, gathered, roots))

    hidden_out, sent, scale, weight_grad = pl.pallas_call(
        middle_kernel,
        out_shape=(
            jax.ShapeDtypeStruct((group, hidden), f32),
            jax.ShapeDtypeStruct((group, width), f32),
            jax.ShapeDtypeStruct((group, width), f32),
            jax.ShapeDtypeStruct((width, hidden), f32),
        ),
        compiler_params=limit,
        cost_estimate=pl.CostEstimate(
            flops=36 * group * width * hidden, bytes_accessed=2**20, transcendentals=2**18
        ),
        name="middle",
    )(own_roots, features, weight, out_bias.reshape(1, hidden), cotangent, drop_keep, *sums)

    collected = gather(sent)
    shares = lax.all_to_all(
        weight_grad.reshape(grid.count, 1, -1), both_axes, 0, 0, tiled=True
    )
    share = jnp.sum(shares, axis=0, keepdims=True)
    weight_grad = lax.all_to_all(
        jnp.broadcast_to(share, shares.shape), both_axes, 0, 0, tiled=True
    ).reshape(width, hidden)

    if side * depth * 4 > 24 * MIB:
        peer_lists = list(lax.optimization_barrier((*peer_lists, sent))[:-1])
    backward_block = block_of(backward_block_kernel, "backward_block", *peer_lists)
    sums = to_owners(block_sum("backward_sum", backward_row, backward_block, collected))
    total = sent
    for part in sums:
        total = total + part
    return (hidden_out, scale * total, weight_grad)


def solution(mesh):
    in_specs = (
        P(("row", "col"), None),
        P(),
        P(),
        P(("row", "col"), None),
        P(("row", "col"), None),
        P("row", "col", None, None),
        P("row", "col", None, None),
        P("row", "col", None, None),
        P("row", "col", None, None),
    )
    out_specs = (P(("row", "col"), None), P(("row", "col"), None), P())
    return jax.shard_map(shards, mesh=mesh, in_specs=in_specs, out_specs=out_specs, check_vma=False)
```

```python
import functools

import jax
import jax.numpy as jnp
from jax import lax
from jax.experimental import pallas as pl
from jax.experimental.pallas import tpu as pltpu
from jax.sharding import PartitionSpec as P

TILE_SIDE = 128
TPR = 4
EPT = 64
KEEP_RATE = 0.9
CORES = 2
DEPTH = 4

f32 = jnp.float32
bf16 = jnp.bfloat16
i32 = jnp.int32
highest = lax.Precision.HIGHEST
NT = (((1,), (1,)), ((), ()))
TN = (((0,), (0,)), ((), ()))
MIB = 1 << 20


class Grid:
    def __init__(self, rows, cols, group):
        self.rows, self.cols, self.group = rows, cols, group
        self.wide = cols // (DEPTH * CORES)
        self.count = rows * cols
        self.per = group // TILE_SIDE
        self.gathered = DEPTH * CORES
        self.summed = rows * self.wide

    def place(self, me):
        col = lax.rem(me, self.cols)
        core = lax.rem(col, CORES)
        rest = lax.div(col, CORES)
        return lax.div(me, self.cols), lax.rem(rest, self.wide), lax.div(rest, self.wide), core

    def col(self, z, y, core):
        return (z * self.wide + y) * CORES + core

    def number(self, x, y, z, core):
        return x * self.cols + self.col(z, y, core)

    def all_places(self):
        return [
            (x, y, z, core)
            for x in range(self.rows)
            for z in range(DEPTH)
            for y in range(self.wide)
            for core in range(CORES)
        ]

    def pairs(self, move):
        return [(self.number(*p), self.number(*move(*p))) for p in self.all_places()]


def gelu_exact(values):
    return 0.5 * values * (1.0 + lax.erf(values * 0.7071067811865476))


def gelu_slope(values):
    return (
        0.5 * (1.0 + lax.erf(values * 0.7071067811865476))
        + values * jnp.exp(-0.5 * values * values) * 0.3989422804014327
    )


def one_hot(index_row, size):
    places = lax.broadcasted_iota(i32, (size, index_row.shape[1]), 0)
    return jnp.where(places == index_row, 1.0, 0.0).astype(bf16)


def turned_times(values, table):
    return lax.dot_general(
        values.astype(f32).astype(bf16), table, TN, preferred_element_type=f32
    ).astype(i32)


def pack_kernel(grid, cols_ref, counts_ref, pos_ref, keep_ref, lists_ref, pieces_ref):
    rows, slots = pos_ref.shape
    slot = lax.broadcasted_iota(i32, (rows, slots), 1)
    tile_of = lax.broadcasted_iota(i32, (TPR, slots), 1) // EPT
    spread = jnp.where(tile_of == lax.broadcasted_iota(i32, (TPR, slots), 0), 1.0, 0.0)
    count = turned_times(counts_ref[...], spread.astype(bf16))
    live = ((slot & (EPT - 1)) < count) & (keep_ref[...] == 1)
    pos = jnp.where(live, pos_ref[...], -1)
    lists_ref[:, :slots] = pos
    lane = lax.broadcasted_iota(i32, (TPR, TILE_SIDE), 1)
    k = lax.broadcasted_iota(i32, (TPR, TILE_SIDE), 0)
    placed = [
        turned_times(cols_ref[...], jnp.where(lane == u * TPR + k, 1.0, 0.0).astype(bf16))
        for u in range(grid.per)
    ]
    lists_ref[:, slots:] = placed[0]
    target = lax.shift_right_arithmetic(pos, 7)
    ones = jnp.ones((8, slots), bf16)
    degrees = []
    for t in range(rows):
        hot = one_hot(target[t : t + 1, :], TILE_SIDE)
        sums = lax.dot_general(ones, hot, NT, preferred_element_type=f32)
        degrees.append(sums[0:1, :].astype(i32))
    at_cols = grid.wide * grid.per * slots
    at_degrees = at_cols + grid.wide * TILE_SIDE
    for z in range(DEPTH):
        for core in range(CORES):
            parts, columns = [], []
            for y in range(grid.wide):
                t = grid.col(z, y, core) * grid.per
                parts += [pos[t + s : t + s + 1, :] for s in range(grid.per)]
                columns.append(sum(placed[s][t + s : t + s + 1, :] for s in range(grid.per)))
            shared = jnp.concatenate(parts + columns, axis=1)
            for y in range(grid.wide):
                t = grid.col(z, y, core) * grid.per
                own = jnp.concatenate(degrees[t : t + grid.per], axis=1)
                for x in range(grid.rows):
                    n = grid.number(x, y, z, core)
                    pieces_ref[n, :, :at_degrees] = shared
                    pieces_ref[n, :, at_degrees:] = own


def roots_kernel(grid, me_ref, edges_ref, roots_ref):
    x = lax.div(me_ref[0], grid.cols)
    at = edges_ref.shape[2] - grid.group
    counts = edges_ref[pl.ds(x * grid.cols, grid.cols), :, at:]
    root = lax.rsqrt(1.0 + jnp.sum(counts, axis=0).astype(f32))
    for g in range(grid.gathered):
        roots_ref[g] = root


def slot_columns(columns, first, slots):
    tile = lax.broadcasted_iota(i32, (1, slots), 1) // EPT
    spread = jnp.broadcast_to(columns[:, first : first + 1], (1, slots))
    for k in range(1, TPR):
        spread = jnp.where(tile == k, columns[:, first + k : first + k + 1], spread)
    return spread


def split_values(grid, values, both_ref, scale_of=None):
    width = values[0].shape[1]
    for g, ref in enumerate(values):
        value = ref[: grid.group, :]
        if scale_of is not None:
            value = value * spread_down(scale_of(g))
        high = value.astype(bf16)
        rows = slice(g * grid.group, (g + 1) * grid.group)
        both_ref[rows, :width] = high
        both_ref[rows, width:] = (value - high.astype(f32)).astype(bf16)


def forward_kernel(grid, slots, me_ref, roots_ref, edges_ref, *refs):
    values, outs, both_ref = refs[: grid.gathered], refs[grid.gathered : -1], refs[-1]
    width = values[0].shape[1]
    step = pl.program_id(0)
    x, y, z, core = grid.place(me_ref[0])

    @pl.when(step == 0)
    def _():
        split_values(
            grid,
            values,
            both_ref,
            lambda g: roots_ref[(z ^ (g // CORES)) * CORES + (core ^ (g % CORES))],
        )

    to_x = lax.rem(x + lax.rem(step, grid.rows), grid.rows)
    to_y = lax.rem(y + lax.div(step, grid.rows), grid.wide)
    at_cols = grid.wide * grid.per * slots + to_y * TILE_SIDE
    total = jnp.zeros((grid.group, 2 * width), f32)
    for g in range(grid.gathered):
        n = grid.number(to_x, y, z ^ (g // CORES), core ^ (g % CORES))
        columns = edges_ref[n, :, pl.ds(pl.multiple_of(at_cols, TILE_SIDE), TILE_SIDE)]
        hots = []
        for s in range(grid.per):
            at = pl.multiple_of((to_y * grid.per + s) * slots, TILE_SIDE)
            pos = edges_ref[n, :, pl.ds(at, slots)]
            target = lax.shift_right_arithmetic(pos, 7)
            source = slot_columns(columns, s * TPR, slots) * TILE_SIDE + (pos & (TILE_SIDE - 1))
            hots.append(
                lax.dot_general(
                    one_hot(target, TILE_SIDE),
                    one_hot(source - x * grid.group, grid.group),
                    NT,
                    preferred_element_type=f32,
                )
            )
        block = jnp.concatenate(hots, axis=0).astype(bf16)
        rows = slice(g * grid.group, (g + 1) * grid.group)
        total = total + jnp.dot(block, both_ref[rows, :], preferred_element_type=f32)
    total = total[:, :width] + total[:, width:]
    for k, out_ref in enumerate(outs):

        @pl.when(step == k)
        def _(out_ref=out_ref):
            out_ref[...] = total


def backward_block_kernel(grid, slots, me_ref, *refs):
    lists, block_ref = refs[:-1], refs[-1]
    g = pl.program_id(0)
    x, y, z, core = grid.place(me_ref[0])
    col = grid.col(z ^ lax.div(g, CORES), y, core ^ lax.rem(g, CORES))
    side = grid.rows * grid.group
    for k, list_ref in enumerate(lists):
        for s in range(grid.per):
            row = list_ref[pl.ds(col * grid.per + s, 1), :]
            pos = row[:, :slots]
            target = lax.shift_right_arithmetic(pos, 7)
            source = slot_columns(row[:, slots:], 0, slots) * TILE_SIDE + (pos & (TILE_SIDE - 1))
            hot = lax.dot_general(
                one_hot(source, side), one_hot(target, TILE_SIDE), NT, preferred_element_type=f32
            )
            block_ref[k * side : (k + 1) * side, s * TILE_SIDE : (s + 1) * TILE_SIDE] = hot.astype(
                bf16
            )


def spread_down(row):
    return jnp.concatenate(
        [
            jnp.broadcast_to(row[:, a : a + TILE_SIDE], (TILE_SIDE, TILE_SIDE)).T
            for a in range(0, row.shape[1], TILE_SIDE)
        ],
        axis=0,
    )


def backward_sum_kernel(grid, me_ref, block_ref, *refs):
    values, outs = refs[: grid.gathered], refs[grid.gathered : -2]
    shares_ref, both_ref = refs[-2:]
    width = values[0].shape[1]
    step = pl.program_id(0)

    @pl.when(step == 0)
    def _():
        x, y, z, core = grid.place(me_ref[0])
        split_values(grid, values, both_ref)
        for g, ref in enumerate(values):
            n = (z ^ (g // CORES)) * CORES + (core ^ (g % CORES))
            shares_ref[n] = ref[grid.group :, :]
        share = shares_ref[0]
        for n in range(1, grid.gathered):
            share = share + shares_ref[n]
        for out_ref in outs:
            out_ref[grid.group :, :] = share

    part = jnp.dot(block_ref[...], both_ref[...], preferred_element_type=f32)
    total = part[:, :width] + part[:, width:]
    for k, out_ref in enumerate(outs):

        @pl.when(step == k)
        def _(out_ref=out_ref):
            out_ref[: grid.group, :] = total


def finish_kernel(grid, me_ref, scale_ref, sent_ref, *refs):
    sums, (features_grad_ref, share_ref, shares_ref) = refs[:-3], refs[-3:]
    x, y, z, core = grid.place(me_ref[0])
    total = sent_ref[: grid.group, :]
    for k, ref in enumerate(sums):
        total = total + ref[: grid.group, :]
        from_x = lax.rem(x + grid.rows - k % grid.rows, grid.rows)
        from_y = lax.rem(y + grid.wide - k // grid.rows, grid.wide)
        shares_ref[from_y * grid.rows + from_x] = ref[grid.group :, :]
    features_grad_ref[...] = scale_ref[...] * total
    share = shares_ref[0]
    for n in range(1, grid.summed):
        share = share + shares_ref[n]
    share_ref[...] = share


def join_kernel(grid, me_ref, *refs):
    quarters, out_ref = refs[:-1], refs[-1]
    _, _, z, _ = grid.place(me_ref[0])
    half = quarters[0].shape[0] // 2
    for dz, ref in enumerate(quarters):
        rows = pl.ds(pl.multiple_of((z ^ dz) * half, 8), half)
        out_ref[rows, :] = jnp.concatenate([ref[:half, :], ref[half:, :]], axis=1)


def middle_kernel(
    grid,
    me_ref,
    roots_ref,
    features_ref,
    weight_ref,
    bias_ref,
    cotangent_ref,
    drop_ref,
    *refs,
):
    sums, refs = refs[: grid.summed], refs[grid.summed :]
    (hidden_ref, scale_ref), sent_refs, weight_grad_ref = refs[:2], refs[2:-1], refs[-1]
    _, _, z, _ = grid.place(me_ref[0])
    scale = spread_down(roots_ref[0])
    scale_ref[...] = scale
    total = scale * features_ref[...]
    for ref in sums:
        total = total + ref[...]
    mixed = scale * total
    weight = weight_ref[...]
    pre_act = jnp.dot(mixed, weight, precision=highest, preferred_element_type=f32) + bias_ref[...]
    dropout = drop_ref[...].astype(f32) / KEEP_RATE
    hidden_ref[...] = gelu_exact(pre_act) * dropout
    grad_pre = cotangent_ref[...] * dropout * gelu_slope(pre_act)
    sent = scale * lax.dot_general(
        grad_pre, weight, NT, precision=highest, preferred_element_type=f32
    )
    weight_grad_ref[...] = lax.dot_general(
        mixed, grad_pre, TN, precision=highest, preferred_element_type=f32
    )
    width = features_ref.shape[1]
    quarter = width // DEPTH
    for dz, sent_ref in enumerate(sent_refs):
        share = weight_grad_ref[pl.ds(pl.multiple_of((z ^ dz) * quarter, 8), quarter), :]
        sent_ref[: grid.group, :] = sent
        sent_ref[grid.group : grid.group + quarter, :] = share[:, :width]
        sent_ref[grid.group + quarter :, :] = share[:, width:]


def shards(
    features,
    weight,
    out_bias,
    cotangent,
    drop_keep,
    tile_cols,
    tile_edge_counts,
    edge_pos,
    edge_keep_bits,
):
    group, width = features.shape
    hidden = weight.shape[1]
    rows, slots = edge_pos.shape[2:]
    grid = Grid(lax.axis_size("row"), lax.axis_size("col"), group)
    both_axes = ("row", "col")
    me = lax.axis_index(both_axes).astype(i32)[None]
    smem = pl.BlockSpec(memory_space=pltpu.SMEM)
    vmem = pl.BlockSpec(memory_space=pltpu.VMEM)
    limit = pltpu.CompilerParams(vmem_limit_bytes=24 * MIB)

    def along_z(blocks):
        return [blocks[0]] + [
            lax.ppermute(
                blocks[dz], both_axes, grid.pairs(lambda x, y, z, c, dz=dz: (x, y, z ^ dz, c))
            )
            for dz in range(1, DEPTH)
        ]

    def to_cores(blocks):
        others = [
            lax.ppermute(block, both_axes, grid.pairs(lambda x, y, z, c: (x, y, z, c ^ 1)))
            for block in blocks
        ]
        return [block for pair in zip(blocks, others) for block in pair]

    def backward_row(k, me_ref):
        x, _, _, _ = grid.place(me_ref[0])
        to_x = lax.rem(x + lax.rem(k, grid.rows), grid.rows)
        return lax.div(k, grid.rows) * grid.rows + to_x

    sum_order = [(dx, dy) for dy in range(grid.wide) for dx in range(grid.rows)]

    def to_owners(sums):
        got = [sums[0]]
        for part, (dx, dy) in list(zip(sums, sum_order))[1:]:
            got.append(
                lax.ppermute(
                    part,
                    both_axes,
                    grid.pairs(
                        lambda x, y, z, c, dx=dx, dy=dy: (
                            (x + dx) % grid.rows,
                            (y + dy) % grid.wide,
                            z,
                            c,
                        )
                    ),
                )
            )
        return got

    piece = grid.wide * grid.per * slots + grid.wide * TILE_SIDE + group
    lists, pieces = pl.pallas_call(
        functools.partial(pack_kernel, grid),
        out_shape=(
            jax.ShapeDtypeStruct((rows, slots + TILE_SIDE), i32),
            jax.ShapeDtypeStruct((grid.count, 1, piece), i32),
        ),
        compiler_params=limit,
        cost_estimate=pl.CostEstimate(flops=2**31, bytes_accessed=2**23, transcendentals=0),
        name="pack",
    )(tile_cols[0, 0].T, tile_edge_counts[0, 0].T, edge_pos[0, 0], edge_keep_bits[0, 0])

    along = along_z([features] * DEPTH)
    peer_lists = [lists] + [
        lax.ppermute(
            lists,
            both_axes,
            grid.pairs(lambda x, y, z, c, dy=dy: (x, (y - dy) % grid.wide, z, c)),
        )
        for dy in range(1, grid.wide)
    ]
    side, depth = grid.summed * group, grid.gathered * group
    backward_block = pl.pallas_call(
        functools.partial(backward_block_kernel, grid, slots),
        grid=(grid.gathered,),
        in_specs=[smem] + [pl.BlockSpec(lists.shape, lambda g: (0, 0))] * grid.wide,
        out_specs=pl.BlockSpec((side, group), lambda g: (0, g)),
        out_shape=jax.ShapeDtypeStruct((side, depth), bf16),
        compiler_params=limit,
        cost_estimate=pl.CostEstimate(flops=2**16, bytes_accessed=2**16, transcendentals=0),
        name="backward_block",
    )(me, *peer_lists)
    *along, pieces, backward_block = lax.optimization_barrier((*along, pieces, backward_block))
    edges = lax.all_to_all(pieces, both_axes, 0, 0, tiled=True)
    gathered = to_cores(along)

    own_roots = pl.pallas_call(
        functools.partial(roots_kernel, grid),
        in_specs=[smem, vmem],
        out_shape=jax.ShapeDtypeStruct((grid.gathered, 1, group), f32),
        compiler_params=limit,
        cost_estimate=pl.CostEstimate(flops=2**14, bytes_accessed=2**16, transcendentals=0),
        name="roots",
    )(me, edges)
    roots = lax.all_to_all(
        own_roots,
        "col",
        0,
        0,
        tiled=True,
        axis_index_groups=[
            [grid.col(z, y, c) for z in range(DEPTH) for c in range(CORES)]
            for y in range(grid.wide)
        ],
    )

    def whole(*shape):
        return pl.BlockSpec(shape, lambda k: (0,) * len(shape))

    sums = pl.pallas_call(
        functools.partial(forward_kernel, grid, slots),
        grid=(grid.summed,),
        in_specs=[smem, whole(*roots.shape), whole(*edges.shape)]
        + [whole(group, width)] * grid.gathered,
        out_specs=(whole(group, width),) * grid.summed,
        out_shape=(jax.ShapeDtypeStruct((group, width), f32),) * grid.summed,
        scratch_shapes=[pltpu.VMEM((depth, 2 * width), bf16)],
        compiler_params=limit,
        cost_estimate=pl.CostEstimate(
            flops=8 * side * depth * width, bytes_accessed=depth * width * 4, transcendentals=0
        ),
        name="forward",
    )(me, roots, edges, *gathered)
    sums = to_owners(sums)

    tall = group + hidden // DEPTH
    tall_shape = jax.ShapeDtypeStruct((tall, width), f32)
    hidden_out, scale, *sent = pl.pallas_call(
        functools.partial(middle_kernel, grid),
        in_specs=[smem] + [vmem] * (6 + grid.summed),
        out_shape=(
            jax.ShapeDtypeStruct((group, hidden), f32),
            jax.ShapeDtypeStruct((group, width), f32),
        )
        + (tall_shape,) * DEPTH,
        scratch_shapes=[pltpu.VMEM((width, hidden), f32)],
        compiler_params=limit,
        cost_estimate=pl.CostEstimate(
            flops=36 * group * width * hidden, bytes_accessed=2**20, transcendentals=2**18
        ),
        name="middle",
    )(me, own_roots, features, weight, out_bias.reshape(1, hidden), cotangent, drop_keep, *sums)

    collected = to_cores(along_z(sent))
    sums = pl.pallas_call(
        functools.partial(backward_sum_kernel, grid),
        grid_spec=pltpu.PrefetchScalarGridSpec(
            num_scalar_prefetch=1,
            grid=(grid.summed,),
            in_specs=[pl.BlockSpec((group, depth), lambda k, me_ref: (backward_row(k, me_ref), 0))]
            + [pl.BlockSpec((tall, width), lambda k, me_ref: (0, 0))] * grid.gathered,
            out_specs=(pl.BlockSpec((tall, width), lambda k, me_ref: (0, 0)),) * grid.summed,
            scratch_shapes=[
                pltpu.VMEM((grid.gathered, tall - group, width), f32),
                pltpu.VMEM((depth, 2 * width), bf16),
            ],
        ),
        out_shape=(tall_shape,) * grid.summed,
        compiler_params=limit,
        cost_estimate=pl.CostEstimate(
            flops=4 * side * depth * width, bytes_accessed=2 * side * depth, transcendentals=0
        ),
        name="backward_sum",
    )(me, backward_block, *collected)
    sums = to_owners(sums)
    grad_features, share = pl.pallas_call(
        functools.partial(finish_kernel, grid),
        in_specs=[smem] + [vmem] * (2 + grid.summed),
        out_shape=(
            jax.ShapeDtypeStruct((group, width), f32),
            jax.ShapeDtypeStruct((tall - group, width), f32),
        ),
        scratch_shapes=[pltpu.VMEM((grid.summed, tall - group, width), f32)],
        compiler_params=limit,
        cost_estimate=pl.CostEstimate(flops=2**18, bytes_accessed=2**19, transcendentals=0),
        name="finish",
    )(me, scale, sent[0], *sums)
    grad_weight = pl.pallas_call(
        functools.partial(join_kernel, grid),
        in_specs=[smem] + [vmem] * DEPTH,
        out_shape=jax.ShapeDtypeStruct((width, hidden), f32),
        compiler_params=limit,
        cost_estimate=pl.CostEstimate(flops=0, bytes_accessed=2**18, transcendentals=0),
        name="join",
    )(me, *along_z([share] * DEPTH))
    return (hidden_out, grad_features, grad_weight)


def solution(mesh):
    in_specs = (
        P(("row", "col"), None),
        P(),
        P(),
        P(("row", "col"), None),
        P(("row", "col"), None),
        P("row", "col", None, None),
        P("row", "col", None, None),
        P("row", "col", None, None),
        P("row", "col", None, None),
    )
    out_specs = (P(("row", "col"), None), P(("row", "col"), None), P())
    return jax.shard_map(shards, mesh=mesh, in_specs=in_specs, out_specs=out_specs, check_vma=False)
```

```python
import functools

import jax
import jax.numpy as jnp
from jax import lax
from jax.experimental import pallas as pl
from jax.experimental.pallas import tpu as pltpu
from jax.sharding import PartitionSpec as P

TILE_SIDE = 128
TPR = 4
EPT = 64
KEEP_RATE = 0.9
CORES = 2
DEPTH = 4

f32 = jnp.float32
bf16 = jnp.bfloat16
i32 = jnp.int32
highest = lax.Precision.HIGHEST
NT = (((1,), (1,)), ((), ()))
TN = (((0,), (0,)), ((), ()))
MIB = 1 << 20


class Grid:
    def __init__(self, rows, cols, group):
        self.rows, self.cols, self.group = rows, cols, group
        self.wide = cols // (DEPTH * CORES)
        self.count = rows * cols
        self.per = group // TILE_SIDE
        self.gathered = DEPTH * CORES
        self.summed = rows * self.wide

    def place(self, me):
        col = lax.rem(me, self.cols)
        core = lax.rem(col, CORES)
        rest = lax.div(col, CORES)
        return lax.div(me, self.cols), lax.rem(rest, self.wide), lax.div(rest, self.wide), core

    def col(self, z, y, core):
        return (z * self.wide + y) * CORES + core

    def number(self, x, y, z, core):
        return x * self.cols + self.col(z, y, core)

    def all_places(self):
        return [
            (x, y, z, core)
            for x in range(self.rows)
            for z in range(DEPTH)
            for y in range(self.wide)
            for core in range(CORES)
        ]

    def pairs(self, move):
        return [(self.number(*p), self.number(*move(*p))) for p in self.all_places()]


def gelu_exact(values):
    return 0.5 * values * (1.0 + lax.erf(values * 0.7071067811865476))


def gelu_slope(values):
    return (
        0.5 * (1.0 + lax.erf(values * 0.7071067811865476))
        + values * jnp.exp(-0.5 * values * values) * 0.3989422804014327
    )


def one_hot(index_row, size):
    places = lax.broadcasted_iota(i32, (size, index_row.shape[1]), 0)
    return jnp.where(places == index_row, 1.0, 0.0).astype(bf16)


def turned_times(values, table):
    return lax.dot_general(
        values.astype(f32).astype(bf16), table, TN, preferred_element_type=f32
    ).astype(i32)


def pack_kernel(grid, me_ref, *refs):
    hbm_refs, lists_ref, sent_refs, refs = refs[:4], refs[4], refs[5 : 5 + DEPTH], refs[5 + DEPTH :]
    counts_ref, vmem_refs, sem = refs[0], refs[1:5], refs[5]
    copies = [
        pltpu.make_async_copy(a, b, sem.at[n]) for n, (a, b) in enumerate(zip(hbm_refs, vmem_refs))
    ]
    for copy in copies:
        copy.start()
    for copy in copies:
        copy.wait()
    cols_ref, tile_counts_ref, pos_ref, keep_ref = vmem_refs
    rows, slots = pos_ref.shape
    slot = lax.broadcasted_iota(i32, (rows, slots), 1)
    tile_of = lax.broadcasted_iota(i32, (TPR, slots), 1) // EPT
    spread = jnp.where(tile_of == lax.broadcasted_iota(i32, (TPR, slots), 0), 1.0, 0.0)
    count = turned_times(tile_counts_ref[...], spread.astype(bf16))
    live = ((slot & (EPT - 1)) < count) & (keep_ref[...] == 1)
    pos = jnp.where(live, pos_ref[...], -1)
    lists_ref[:, :slots] = pos
    lane = lax.broadcasted_iota(i32, (TPR, TILE_SIDE), 1)
    k = lax.broadcasted_iota(i32, (TPR, TILE_SIDE), 0)
    lists_ref[:, slots:] = turned_times(cols_ref[...], jnp.where(lane == k, 1.0, 0.0).astype(bf16))
    target = lax.shift_right_arithmetic(pos, 7)
    ones = jnp.ones((8, slots), bf16)
    for t in range(rows):
        hot = one_hot(target[t : t + 1, :], TILE_SIDE)
        sums = lax.dot_general(ones, hot, NT, preferred_element_type=f32)
        counts_ref[t : t + 1, :] = sums[0:1, :].astype(i32)
    _, _, z, _ = grid.place(me_ref[0])
    plane = rows // DEPTH
    for dz, sent_ref in enumerate(sent_refs):
        at = pl.multiple_of((z ^ dz) * plane, 8)
        sent_ref[:, : slots + TILE_SIDE] = lists_ref[pl.ds(at, plane), :]
        for q in range(DEPTH):
            lanes = slice(slots + (q + 1) * TILE_SIDE, slots + (q + 2) * TILE_SIDE)
            sent_ref[:, lanes] = counts_ref[q * plane : (q + 1) * plane, :]


def relay_kernel(wide, *refs):
    got, (both_ref, lists_ref, counts_ref) = refs[:-3], refs[-3:]
    plane = got[0].shape[0]
    for dz, ref in enumerate(got):
        rows = slice(dz * plane, (dz + 1) * plane)
        lists_ref[rows, :] = ref[:, :wide]
        both_ref[rows, :wide] = ref[:, :wide]
    for q in range(DEPTH):
        lanes = slice(wide + q * TILE_SIDE, wide + (q + 1) * TILE_SIDE)
        count = got[0][:, lanes]
        for ref in got[1:]:
            count = count + ref[:, lanes]
        rows = slice(q * plane, (q + 1) * plane)
        counts_ref[rows, :] = count
        both_ref[rows, wide:] = count


def slot_columns(columns, first, slots):
    tile = lax.broadcasted_iota(i32, (1, slots), 1) // EPT
    spread = jnp.broadcast_to(columns[:, first : first + 1], (1, slots))
    for k in range(1, TPR):
        spread = jnp.where(tile == k, columns[:, first + k : first + k + 1], spread)
    return spread


def split_values(grid, values, both_ref, scale_of=None):
    width = values[0].shape[1]
    for g, ref in enumerate(values):
        value = ref[: grid.group, :]
        if scale_of is not None:
            value = value * scale_of(g)
        high = value.astype(bf16)
        rows = slice(g * grid.group, (g + 1) * grid.group)
        both_ref[rows, :width] = high
        both_ref[rows, width:] = (value - high.astype(f32)).astype(bf16)


def forward_kernel(grid, slots, me_ref, *refs):
    core_refs, refs = refs[:CORES], refs[CORES:]
    list_refs, refs = refs[: CORES * (grid.rows - 1)], refs[CORES * (grid.rows - 1) :]
    count_refs, refs = refs[: CORES * (grid.wide - 1)], refs[CORES * (grid.wide - 1) :]
    values, refs = refs[: grid.gathered], refs[grid.gathered :]
    scale_ref, outs, (lists_ref, root_ref, both_ref) = refs[0], refs[1:-3], refs[-3:]
    width = values[0].shape[1]
    step = pl.program_id(0)
    x, y, z, core = grid.place(me_ref[0])
    wide = slots + TILE_SIDE

    @pl.when(step == 0)
    def _():
        count = sum(ref[:, wide:] for ref in core_refs)
        for ref in count_refs:
            count = count + ref[...]
        root_ref[...] = lax.rsqrt(1.0 + count.astype(f32))
        for n, ref in enumerate(core_refs):
            lists_ref[n] = ref[:, :wide]
        for n, ref in enumerate(list_refs):
            lists_ref[CORES + n] = ref[...]

        def scale_of(g):
            at = grid.col(z ^ (g // CORES), y, core ^ (g % CORES)) * grid.per
            return spread_down([root_ref[pl.ds(at + s, 1), :] for s in range(grid.per)])

        scale_ref[...] = scale_of(0)
        split_values(grid, values, both_ref, scale_of)

    dx, dy = lax.rem(step, grid.rows), lax.div(step, grid.rows)
    to_y = lax.rem(y + dy, grid.wide)
    plane = grid.wide * CORES * grid.per
    total = jnp.zeros((grid.group, 2 * width), f32)
    for g in range(grid.gathered):
        hots = []
        for s in range(grid.per):
            at = (g // CORES) * plane + (to_y * CORES + core) * grid.per + s
            row = lists_ref[dx * CORES + g % CORES, pl.ds(at, 1), :]
            pos = row[:, :slots]
            target = lax.shift_right_arithmetic(pos, 7)
            source = slot_columns(row[:, slots:], 0, slots) * TILE_SIDE + (pos & (TILE_SIDE - 1))
            hots.append(
                lax.dot_general(
                    one_hot(target, TILE_SIDE),
                    one_hot(source - x * grid.group, grid.group),
                    NT,
                    preferred_element_type=f32,
                )
            )
        block = jnp.concatenate(hots, axis=0).astype(bf16)
        rows = slice(g * grid.group, (g + 1) * grid.group)
        total = total + jnp.dot(block, both_ref[rows, :], preferred_element_type=f32)
    total = total[:, :width] + total[:, width:]
    for k, out_ref in enumerate(outs):

        @pl.when(step == k)
        def _(out_ref=out_ref):
            out_ref[...] = total


def backward_block_kernel(grid, slots, me_ref, *refs):
    lists, block_ref = refs[:-1], refs[-1]
    g = pl.program_id(0)
    x, y, z, core = grid.place(me_ref[0])
    col = grid.col(z ^ lax.div(g, CORES), y, core ^ lax.rem(g, CORES))
    side = grid.rows * grid.group
    for k, list_ref in enumerate(lists):
        for s in range(grid.per):
            row = list_ref[pl.ds(col * grid.per + s, 1), :]
            pos = row[:, :slots]
            target = lax.shift_right_arithmetic(pos, 7)
            source = slot_columns(row[:, slots:], 0, slots) * TILE_SIDE + (pos & (TILE_SIDE - 1))
            hot = lax.dot_general(
                one_hot(source, side), one_hot(target, TILE_SIDE), NT, preferred_element_type=f32
            )
            block_ref[k * side : (k + 1) * side, s * TILE_SIDE : (s + 1) * TILE_SIDE] = hot.astype(
                bf16
            )


def spread_down(rows):
    return jnp.concatenate(
        [jnp.broadcast_to(row, (TILE_SIDE, TILE_SIDE)).T for row in rows], axis=0
    )


def backward_sum_kernel(grid, me_ref, block_ref, *refs):
    values, outs = refs[: grid.gathered], refs[grid.gathered : -2]
    shares_ref, both_ref = refs[-2:]
    width = values[0].shape[1]
    step = pl.program_id(0)

    @pl.when(step == 0)
    def _():
        x, y, z, core = grid.place(me_ref[0])
        split_values(grid, values, both_ref)
        for g, ref in enumerate(values):
            n = (z ^ (g // CORES)) * CORES + (core ^ (g % CORES))
            shares_ref[n] = ref[grid.group :, :]
        share = shares_ref[0]
        for n in range(1, grid.gathered):
            share = share + shares_ref[n]
        for out_ref in outs:
            out_ref[grid.group :, :] = share

    part = jnp.dot(block_ref[...], both_ref[...], preferred_element_type=f32)
    total = part[:, :width] + part[:, width:]
    for k, out_ref in enumerate(outs):

        @pl.when(step == k)
        def _(out_ref=out_ref):
            out_ref[: grid.group, :] = total


def finish_kernel(grid, me_ref, scale_ref, sent_ref, *refs):
    sums, (features_grad_ref, share_ref, shares_ref) = refs[:-3], refs[-3:]
    x, y, z, core = grid.place(me_ref[0])
    total = sent_ref[: grid.group, :]
    for k, ref in enumerate(sums):
        total = total + ref[: grid.group, :]
        from_x = lax.rem(x + grid.rows - k % grid.rows, grid.rows)
        from_y = lax.rem(y + grid.wide - k // grid.rows, grid.wide)
        shares_ref[from_y * grid.rows + from_x] = ref[grid.group :, :]
    features_grad_ref[...] = scale_ref[...] * total
    share = shares_ref[0]
    for n in range(1, grid.summed):
        share = share + shares_ref[n]
    share_ref[...] = share


def join_kernel(grid, me_ref, *refs):
    quarters, out_ref = refs[:-1], refs[-1]
    _, _, z, _ = grid.place(me_ref[0])
    half = quarters[0].shape[0] // 2
    for dz, ref in enumerate(quarters):
        rows = pl.ds(pl.multiple_of((z ^ dz) * half, 8), half)
        out_ref[rows, :] = jnp.concatenate([ref[:half, :], ref[half:, :]], axis=1)


def middle_kernel(
    grid,
    me_ref,
    scale_ref,
    features_ref,
    weight_ref,
    bias_ref,
    cotangent_ref,
    drop_ref,
    *refs,
):
    sums, refs = refs[: grid.summed], refs[grid.summed :]
    hidden_ref, sent_refs, weight_grad_ref = refs[0], refs[1:-1], refs[-1]
    _, _, z, _ = grid.place(me_ref[0])
    scale = scale_ref[...]
    total = scale * features_ref[...]
    for ref in sums:
        total = total + ref[...]
    mixed = scale * total
    weight = weight_ref[...]
    pre_act = jnp.dot(mixed, weight, precision=highest, preferred_element_type=f32) + bias_ref[...]
    dropout = drop_ref[...].astype(f32) / KEEP_RATE
    hidden_ref[...] = gelu_exact(pre_act) * dropout
    grad_pre = cotangent_ref[...] * dropout * gelu_slope(pre_act)
    sent = scale * lax.dot_general(
        grad_pre, weight, NT, precision=highest, preferred_element_type=f32
    )
    weight_grad_ref[...] = lax.dot_general(
        mixed, grad_pre, TN, precision=highest, preferred_element_type=f32
    )
    width = features_ref.shape[1]
    quarter = width // DEPTH
    for dz, sent_ref in enumerate(sent_refs):
        share = weight_grad_ref[pl.ds(pl.multiple_of((z ^ dz) * quarter, 8), quarter), :]
        sent_ref[: grid.group, :] = sent
        sent_ref[grid.group : grid.group + quarter, :] = share[:, :width]
        sent_ref[grid.group + quarter :, :] = share[:, width:]


def shards(
    features,
    weight,
    out_bias,
    cotangent,
    drop_keep,
    tile_cols,
    tile_edge_counts,
    edge_pos,
    edge_keep_bits,
):
    group, width = features.shape
    hidden = weight.shape[1]
    rows, slots = edge_pos.shape[2:]
    grid = Grid(lax.axis_size("row"), lax.axis_size("col"), group)
    both_axes = ("row", "col")
    me = lax.axis_index(both_axes).astype(i32)[None]
    smem = pl.BlockSpec(memory_space=pltpu.SMEM)
    vmem = pl.BlockSpec(memory_space=pltpu.VMEM)
    limit = pltpu.CompilerParams(vmem_limit_bytes=24 * MIB)

    def along_z(blocks):
        return [blocks[0]] + [
            lax.ppermute(
                blocks[dz], both_axes, grid.pairs(lambda x, y, z, c, dz=dz: (x, y, z ^ dz, c))
            )
            for dz in range(1, DEPTH)
        ]

    def to_cores(blocks):
        others = [
            lax.ppermute(block, both_axes, grid.pairs(lambda x, y, z, c: (x, y, z, c ^ 1)))
            for block in blocks
        ]
        return [block for pair in zip(blocks, others) for block in pair]

    def backward_row(k, me_ref):
        x, _, _, _ = grid.place(me_ref[0])
        to_x = lax.rem(x + lax.rem(k, grid.rows), grid.rows)
        return lax.div(k, grid.rows) * grid.rows + to_x

    sum_order = [(dx, dy) for dy in range(grid.wide) for dx in range(grid.rows)]

    def to_owners(sums):
        got = [sums[0]]
        for part, (dx, dy) in list(zip(sums, sum_order))[1:]:
            got.append(
                lax.ppermute(
                    part,
                    both_axes,
                    grid.pairs(
                        lambda x, y, z, c, dx=dx, dy=dy: (
                            (x + dx) % grid.rows,
                            (y + dy) % grid.wide,
                            z,
                            c,
                        )
                    ),
                )
            )
        return got

    wide = slots + TILE_SIDE
    plane = rows // DEPTH
    raw = [tile_cols[0, 0].T, tile_edge_counts[0, 0].T, edge_pos[0, 0], edge_keep_bits[0, 0]]
    lists, *planes = pl.pallas_call(
        functools.partial(pack_kernel, grid),
        in_specs=[smem] + [pl.BlockSpec(memory_space=pltpu.HBM)] * 4,
        out_shape=(jax.ShapeDtypeStruct((rows, wide), i32),)
        + (jax.ShapeDtypeStruct((plane, wide + DEPTH * TILE_SIDE), i32),) * DEPTH,
        scratch_shapes=[pltpu.VMEM((rows, TILE_SIDE), i32)]
        + [pltpu.VMEM(a.shape, i32) for a in raw]
        + [pltpu.SemaphoreType.DMA((4,))],
        compiler_params=limit,
        cost_estimate=pl.CostEstimate(flops=2**21, bytes_accessed=2**17, transcendentals=0),
        name="pack",
    )(me, *raw)

    def from_peer(value, move):
        return lax.ppermute(value, both_axes, [(b, a) for a, b in grid.pairs(move)])

    along = along_z([features] * DEPTH)
    both, plane_lists, counts = pl.pallas_call(
        functools.partial(relay_kernel, wide),
        out_shape=(
            jax.ShapeDtypeStruct((rows, wide + TILE_SIDE), i32),
            jax.ShapeDtypeStruct((rows, wide), i32),
            jax.ShapeDtypeStruct((rows, TILE_SIDE), i32),
        ),
        compiler_params=limit,
        cost_estimate=pl.CostEstimate(flops=2**14, bytes_accessed=2**18, transcendentals=0),
        name="relay",
    )(*along_z(planes))
    core_lists = [both, from_peer(both, lambda x, y, z, c: (x, y, z, c ^ 1))]
    row_lists = [
        from_peer(
            plane_lists, lambda x, y, z, c, dx=dx, dc=dc: ((x + dx) % grid.rows, y, z, c ^ dc)
        )
        for dx in range(1, grid.rows)
        for dc in range(CORES)
    ]
    wide_counts = [
        from_peer(counts, lambda x, y, z, c, dy=dy, dc=dc: (x, (y + dy) % grid.wide, z, c ^ dc))
        for dy in range(1, grid.wide)
        for dc in range(CORES)
    ]
    peer_lists = [lists] + [
        from_peer(lists, lambda x, y, z, c, dy=dy: (x, (y + dy) % grid.wide, z, c))
        for dy in range(1, grid.wide)
    ]
    gathered = to_cores(along)
    side, depth = grid.summed * group, grid.gathered * group

    def whole(*shape):
        return pl.BlockSpec(shape, lambda k: (0,) * len(shape))

    scale, *sums = pl.pallas_call(
        functools.partial(forward_kernel, grid, slots),
        grid=(grid.summed,),
        in_specs=[smem]
        + [whole(rows, wide + TILE_SIDE)] * CORES
        + [whole(rows, wide)] * len(row_lists)
        + [whole(rows, TILE_SIDE)] * len(wide_counts)
        + [whole(group, width)] * grid.gathered,
        out_specs=(whole(group, width),) * (1 + grid.summed),
        out_shape=(jax.ShapeDtypeStruct((group, width), f32),) * (1 + grid.summed),
        scratch_shapes=[
            pltpu.VMEM((CORES * grid.rows, rows, wide), i32),
            pltpu.VMEM((rows, TILE_SIDE), f32),
            pltpu.VMEM((depth, 2 * width), bf16),
        ],
        compiler_params=limit,
        cost_estimate=pl.CostEstimate(
            flops=8 * side * depth * width, bytes_accessed=depth * width * 4, transcendentals=0
        ),
        name="forward",
    )(me, *core_lists, *row_lists, *wide_counts, *gathered)
    sums = to_owners(sums)

    tall = group + hidden // DEPTH
    tall_shape = jax.ShapeDtypeStruct((tall, width), f32)
    hidden_out, *sent = pl.pallas_call(
        functools.partial(middle_kernel, grid),
        in_specs=[smem] + [vmem] * (6 + grid.summed),
        out_shape=(jax.ShapeDtypeStruct((group, hidden), f32),) + (tall_shape,) * DEPTH,
        scratch_shapes=[pltpu.VMEM((width, hidden), f32)],
        compiler_params=limit,
        cost_estimate=pl.CostEstimate(
            flops=36 * group * width * hidden, bytes_accessed=2**20, transcendentals=2**18
        ),
        name="middle",
    )(me, scale, features, weight, out_bias.reshape(1, hidden), cotangent, drop_keep, *sums)

    *peer_lists, sent[0] = lax.optimization_barrier((*peer_lists, sent[0]))
    backward_block = pl.pallas_call(
        functools.partial(backward_block_kernel, grid, slots),
        grid=(grid.gathered,),
        in_specs=[smem] + [pl.BlockSpec(lists.shape, lambda g: (0, 0))] * grid.wide,
        out_specs=pl.BlockSpec((side, group), lambda g: (0, g)),
        out_shape=jax.ShapeDtypeStruct((side, depth), bf16),
        compiler_params=limit,
        cost_estimate=pl.CostEstimate(
            flops=2 * rows * slots * TILE_SIDE * grid.rows * group,
            bytes_accessed=2 * side * depth,
            transcendentals=0,
        ),
        name="backward_block",
    )(me, *peer_lists)
    along = along_z(sent)
    along[-1], backward_block = lax.optimization_barrier((along[-1], backward_block))
    collected = to_cores(along)
    sums = pl.pallas_call(
        functools.partial(backward_sum_kernel, grid),
        grid_spec=pltpu.PrefetchScalarGridSpec(
            num_scalar_prefetch=1,
            grid=(grid.summed,),
            in_specs=[pl.BlockSpec((group, depth), lambda k, me_ref: (backward_row(k, me_ref), 0))]
            + [pl.BlockSpec((tall, width), lambda k, me_ref: (0, 0))] * grid.gathered,
            out_specs=(pl.BlockSpec((tall, width), lambda k, me_ref: (0, 0)),) * grid.summed,
            scratch_shapes=[
                pltpu.VMEM((grid.gathered, tall - group, width), f32),
                pltpu.VMEM((depth, 2 * width), bf16),
            ],
        ),
        out_shape=(tall_shape,) * grid.summed,
        compiler_params=limit,
        cost_estimate=pl.CostEstimate(
            flops=4 * side * depth * width, bytes_accessed=2 * side * depth, transcendentals=0
        ),
        name="backward_sum",
    )(me, backward_block, *collected)
    sums = to_owners(sums)
    grad_features, share = pl.pallas_call(
        functools.partial(finish_kernel, grid),
        in_specs=[smem] + [vmem] * (2 + grid.summed),
        out_shape=(
            jax.ShapeDtypeStruct((group, width), f32),
            jax.ShapeDtypeStruct((tall - group, width), f32),
        ),
        scratch_shapes=[pltpu.VMEM((grid.summed, tall - group, width), f32)],
        compiler_params=limit,
        cost_estimate=pl.CostEstimate(flops=2**18, bytes_accessed=2**19, transcendentals=0),
        name="finish",
    )(me, scale, sent[0], *sums)
    grad_weight = pl.pallas_call(
        functools.partial(join_kernel, grid),
        in_specs=[smem] + [vmem] * DEPTH,
        out_shape=jax.ShapeDtypeStruct((width, hidden), f32),
        compiler_params=limit,
        cost_estimate=pl.CostEstimate(flops=0, bytes_accessed=2**18, transcendentals=0),
        name="join",
    )(me, *along_z([share] * DEPTH))
    return (hidden_out, grad_features, grad_weight)


def solution(mesh):
    in_specs = (
        P(("row", "col"), None),
        P(),
        P(),
        P(("row", "col"), None),
        P(("row", "col"), None),
        P("row", "col", None, None),
        P("row", "col", None, None),
        P("row", "col", None, None),
        P("row", "col", None, None),
    )
    out_specs = (P(("row", "col"), None), P(("row", "col"), None), P())
    return jax.shard_map(shards, mesh=mesh, in_specs=in_specs, out_specs=out_specs, check_vma=False)
```

```python
import functools

import jax
import jax.numpy as jnp
from jax import lax
from jax.experimental import pallas as pl
from jax.experimental.pallas import tpu as pltpu
from jax.sharding import PartitionSpec as P

TILE_SIDE = 128
TPR = 4
EPT = 64
KEEP_RATE = 0.9
CORES = 2
DEPTH = 4

f32 = jnp.float32
bf16 = jnp.bfloat16
i32 = jnp.int32
highest = lax.Precision.HIGHEST
NT = (((1,), (1,)), ((), ()))
TN = (((0,), (0,)), ((), ()))
MIB = 1 << 20


class Grid:
    def __init__(self, rows, cols, group):
        self.rows, self.cols, self.group = rows, cols, group
        self.wide = cols // (DEPTH * CORES)
        self.count = rows * cols
        self.per = group // TILE_SIDE
        self.gathered = DEPTH * CORES
        self.summed = rows * self.wide

    def place(self, me):
        col = lax.rem(me, self.cols)
        core = lax.rem(col, CORES)
        rest = lax.div(col, CORES)
        return lax.div(me, self.cols), lax.rem(rest, self.wide), lax.div(rest, self.wide), core

    def col(self, z, y, core):
        return (z * self.wide + y) * CORES + core

    def number(self, x, y, z, core):
        return x * self.cols + self.col(z, y, core)

    def all_places(self):
        return [
            (x, y, z, core)
            for x in range(self.rows)
            for z in range(DEPTH)
            for y in range(self.wide)
            for core in range(CORES)
        ]

    def pairs(self, move):
        return [(self.number(*p), self.number(*move(*p))) for p in self.all_places()]


def gelu_exact(values):
    return 0.5 * values * (1.0 + lax.erf(values * 0.7071067811865476))


def gelu_slope(values):
    return (
        0.5 * (1.0 + lax.erf(values * 0.7071067811865476))
        + values * jnp.exp(-0.5 * values * values) * 0.3989422804014327
    )


def one_hot(index_row, size):
    places = lax.broadcasted_iota(i32, (size, index_row.shape[1]), 0)
    return jnp.where(places == index_row, 1.0, 0.0).astype(bf16)


def turned_times(values, table):
    return lax.dot_general(
        values.astype(f32).astype(bf16), table, TN, preferred_element_type=f32
    ).astype(i32)


def pack_kernel(grid, me_ref, *refs):
    hbm_refs, lists_ref, sent_refs, refs = refs[:4], refs[4], refs[5 : 5 + DEPTH], refs[5 + DEPTH :]
    counts_ref, vmem_refs, sem = refs[0], refs[1:5], refs[5]
    copies = [
        pltpu.make_async_copy(a, b, sem.at[n]) for n, (a, b) in enumerate(zip(hbm_refs, vmem_refs))
    ]
    for copy in copies:
        copy.start()
    for copy in copies:
        copy.wait()
    cols_ref, tile_counts_ref, pos_ref, keep_ref = vmem_refs
    rows, slots = pos_ref.shape
    slot = lax.broadcasted_iota(i32, (rows, slots), 1)
    tile_of = lax.broadcasted_iota(i32, (TPR, slots), 1) // EPT
    spread = jnp.where(tile_of == lax.broadcasted_iota(i32, (TPR, slots), 0), 1.0, 0.0)
    count = turned_times(tile_counts_ref[...], spread.astype(bf16))
    live = ((slot & (EPT - 1)) < count) & (keep_ref[...] == 1)
    pos = jnp.where(live, pos_ref[...], -1)
    lists_ref[:, :slots] = pos
    lane = lax.broadcasted_iota(i32, (TPR, TILE_SIDE), 1)
    k = lax.broadcasted_iota(i32, (TPR, TILE_SIDE), 0)
    lists_ref[:, slots:] = turned_times(cols_ref[...], jnp.where(lane == k, 1.0, 0.0).astype(bf16))
    target = lax.shift_right_arithmetic(pos, 7)
    ones = jnp.ones((8, slots), bf16)
    for t in range(rows):
        hot = one_hot(target[t : t + 1, :], TILE_SIDE)
        sums = lax.dot_general(ones, hot, NT, preferred_element_type=f32)
        counts_ref[t : t + 1, :] = sums[0:1, :].astype(i32)
    _, _, z, _ = grid.place(me_ref[0])
    plane = rows // DEPTH
    for dz, sent_ref in enumerate(sent_refs):
        at = pl.multiple_of((z ^ dz) * plane, 8)
        sent_ref[:, : slots + TILE_SIDE] = lists_ref[pl.ds(at, plane), :]
        for q in range(DEPTH):
            lanes = slice(slots + (q + 1) * TILE_SIDE, slots + (q + 2) * TILE_SIDE)
            sent_ref[:, lanes] = counts_ref[q * plane : (q + 1) * plane, :]


def relay_kernel(wide, *refs):
    got, (both_ref, lists_ref, counts_ref) = refs[:-3], refs[-3:]
    plane = got[0].shape[0]
    for dz, ref in enumerate(got):
        rows = slice(dz * plane, (dz + 1) * plane)
        lists_ref[rows, :] = ref[:, :wide]
        both_ref[rows, :wide] = ref[:, :wide]
    for q in range(DEPTH):
        lanes = slice(wide + q * TILE_SIDE, wide + (q + 1) * TILE_SIDE)
        count = got[0][:, lanes]
        for ref in got[1:]:
            count = count + ref[:, lanes]
        rows = slice(q * plane, (q + 1) * plane)
        counts_ref[rows, :] = count
        both_ref[rows, wide:] = count


def slot_columns(columns, first, slots):
    tile = lax.broadcasted_iota(i32, (1, slots), 1) // EPT
    spread = jnp.broadcast_to(columns[:, first : first + 1], (1, slots))
    for k in range(1, TPR):
        spread = jnp.where(tile == k, columns[:, first + k : first + k + 1], spread)
    return spread


def split_values(grid, values, both_ref, scale_of=None):
    width = values[0].shape[1]
    for g, ref in enumerate(values):
        value = ref[: grid.group, :]
        if scale_of is not None:
            value = value * scale_of(g)
        high = value.astype(bf16)
        rows = slice(g * grid.group, (g + 1) * grid.group)
        both_ref[rows, :width] = high
        both_ref[rows, width:] = (value - high.astype(f32)).astype(bf16)


def forward_block_kernel(grid, slots, me_ref, *refs):
    core_refs, refs = refs[:CORES], refs[CORES:]
    list_refs, refs = refs[: CORES * (grid.rows - 1)], refs[CORES * (grid.rows - 1) :]
    count_refs, (block_ref, root_ref, lists_ref) = refs[:-3], refs[-3:]
    step = pl.program_id(0)
    x, y, _, core = grid.place(me_ref[0])
    wide = slots + TILE_SIDE

    @pl.when(step == 0)
    def _():
        count = sum(ref[:, wide:] for ref in core_refs)
        for ref in count_refs:
            count = count + ref[...]
        root_ref[...] = lax.rsqrt(1.0 + count.astype(f32))
        for n, ref in enumerate(core_refs):
            lists_ref[n] = ref[:, :wide]
        for n, ref in enumerate(list_refs):
            lists_ref[CORES + n] = ref[...]

    dx, dy = lax.rem(step, grid.rows), lax.div(step, grid.rows)
    to_y = lax.rem(y + dy, grid.wide)
    plane = grid.wide * CORES * grid.per
    for g in range(grid.gathered):
        for s in range(grid.per):
            at = (g // CORES) * plane + (to_y * CORES + core) * grid.per + s
            row = lists_ref[dx * CORES + g % CORES, pl.ds(at, 1), :]
            pos = row[:, :slots]
            target = lax.shift_right_arithmetic(pos, 7)
            source = slot_columns(row[:, slots:], 0, slots) * TILE_SIDE + (pos & (TILE_SIDE - 1))
            hot = lax.dot_general(
                one_hot(target, TILE_SIDE),
                one_hot(source - x * grid.group, grid.group),
                NT,
                preferred_element_type=f32,
            )
            block_ref[
                s * TILE_SIDE : (s + 1) * TILE_SIDE, g * grid.group : (g + 1) * grid.group
            ] = hot.astype(bf16)


def forward_sum_kernel(grid, me_ref, root_ref, block_ref, *refs):
    values, (scale_ref, *outs, both_ref) = refs[: grid.gathered], refs[grid.gathered :]
    width = values[0].shape[1]
    step = pl.program_id(0)

    @pl.when(step == 0)
    def _():
        _, y, z, core = grid.place(me_ref[0])

        def scale_of(g):
            at = grid.col(z ^ (g // CORES), y, core ^ (g % CORES)) * grid.per
            return spread_down([root_ref[pl.ds(at + s, 1), :] for s in range(grid.per)])

        scale_ref[...] = scale_of(0)
        split_values(grid, values, both_ref, scale_of)

    part = jnp.dot(block_ref[...], both_ref[...], preferred_element_type=f32)
    total = part[:, :width] + part[:, width:]
    for k, out_ref in enumerate(outs):

        @pl.when(step == k)
        def _(out_ref=out_ref):
            out_ref[...] = total


def backward_block_kernel(grid, slots, me_ref, *refs):
    lists, block_ref = refs[:-1], refs[-1]
    g = pl.program_id(0)
    x, y, z, core = grid.place(me_ref[0])
    col = grid.col(z ^ lax.div(g, CORES), y, core ^ lax.rem(g, CORES))
    side = grid.rows * grid.group
    for k, list_ref in enumerate(lists):
        for s in range(grid.per):
            row = list_ref[pl.ds(col * grid.per + s, 1), :]
            pos = row[:, :slots]
            target = lax.shift_right_arithmetic(pos, 7)
            source = slot_columns(row[:, slots:], 0, slots) * TILE_SIDE + (pos & (TILE_SIDE - 1))
            hot = lax.dot_general(
                one_hot(source, side), one_hot(target, TILE_SIDE), NT, preferred_element_type=f32
            )
            block_ref[k * side : (k + 1) * side, s * TILE_SIDE : (s + 1) * TILE_SIDE] = hot.astype(
                bf16
            )


def spread_down(rows):
    return jnp.concatenate(
        [jnp.broadcast_to(row, (TILE_SIDE, TILE_SIDE)).T for row in rows], axis=0
    )


def backward_sum_kernel(grid, me_ref, block_ref, *refs):
    values, outs = refs[: grid.gathered], refs[grid.gathered : -2]
    shares_ref, both_ref = refs[-2:]
    width = values[0].shape[1]
    step = pl.program_id(0)

    @pl.when(step == 0)
    def _():
        x, y, z, core = grid.place(me_ref[0])
        split_values(grid, values, both_ref)
        for g, ref in enumerate(values):
            n = (z ^ (g // CORES)) * CORES + (core ^ (g % CORES))
            shares_ref[n] = ref[grid.group :, :]
        share = shares_ref[0]
        for n in range(1, grid.gathered):
            share = share + shares_ref[n]
        for out_ref in outs:
            out_ref[grid.group :, :] = share

    part = jnp.dot(block_ref[...], both_ref[...], preferred_element_type=f32)
    total = part[:, :width] + part[:, width:]
    for k, out_ref in enumerate(outs):

        @pl.when(step == k)
        def _(out_ref=out_ref):
            out_ref[: grid.group, :] = total


def finish_kernel(grid, me_ref, scale_ref, sent_ref, *refs):
    sums, (features_grad_ref, share_ref, shares_ref) = refs[:-3], refs[-3:]
    x, y, z, core = grid.place(me_ref[0])
    total = sent_ref[: grid.group, :]
    for k, ref in enumerate(sums):
        total = total + ref[: grid.group, :]
        from_x = lax.rem(x + grid.rows - k % grid.rows, grid.rows)
        from_y = lax.rem(y + grid.wide - k // grid.rows, grid.wide)
        shares_ref[from_y * grid.rows + from_x] = ref[grid.group :, :]
    features_grad_ref[...] = scale_ref[...] * total
    share = shares_ref[0]
    for n in range(1, grid.summed):
        share = share + shares_ref[n]
    share_ref[...] = share


def join_kernel(grid, me_ref, *refs):
    quarters, out_ref = refs[:-1], refs[-1]
    _, _, z, _ = grid.place(me_ref[0])
    half = quarters[0].shape[0] // 2
    for dz, ref in enumerate(quarters):
        rows = pl.ds(pl.multiple_of((z ^ dz) * half, 8), half)
        out_ref[rows, :] = jnp.concatenate([ref[:half, :], ref[half:, :]], axis=1)


def middle_kernel(
    grid,
    me_ref,
    scale_ref,
    features_ref,
    weight_ref,
    bias_ref,
    cotangent_ref,
    drop_ref,
    *refs,
):
    sums, refs = refs[: grid.summed], refs[grid.summed :]
    hidden_ref, sent_refs, weight_grad_ref = refs[0], refs[1:-1], refs[-1]
    _, _, z, _ = grid.place(me_ref[0])
    scale = scale_ref[...]
    total = scale * features_ref[...]
    for ref in sums:
        total = total + ref[...]
    mixed = scale * total
    weight = weight_ref[...]
    pre_act = jnp.dot(mixed, weight, precision=highest, preferred_element_type=f32) + bias_ref[...]
    dropout = drop_ref[...].astype(f32) / KEEP_RATE
    hidden_ref[...] = gelu_exact(pre_act) * dropout
    grad_pre = cotangent_ref[...] * dropout * gelu_slope(pre_act)
    sent = scale * lax.dot_general(
        grad_pre, weight, NT, precision=highest, preferred_element_type=f32
    )
    weight_grad_ref[...] = lax.dot_general(
        mixed, grad_pre, TN, precision=highest, preferred_element_type=f32
    )
    width = features_ref.shape[1]
    quarter = width // DEPTH
    for dz, sent_ref in enumerate(sent_refs):
        share = weight_grad_ref[pl.ds(pl.multiple_of((z ^ dz) * quarter, 8), quarter), :]
        sent_ref[: grid.group, :] = sent
        sent_ref[grid.group : grid.group + quarter, :] = share[:, :width]
        sent_ref[grid.group + quarter :, :] = share[:, width:]


def shards(
    features,
    weight,
    out_bias,
    cotangent,
    drop_keep,
    tile_cols,
    tile_edge_counts,
    edge_pos,
    edge_keep_bits,
):
    group, width = features.shape
    hidden = weight.shape[1]
    rows, slots = edge_pos.shape[2:]
    grid = Grid(lax.axis_size("row"), lax.axis_size("col"), group)
    both_axes = ("row", "col")
    me = lax.axis_index(both_axes).astype(i32)[None]
    smem = pl.BlockSpec(memory_space=pltpu.SMEM)
    vmem = pl.BlockSpec(memory_space=pltpu.VMEM)
    limit = pltpu.CompilerParams(vmem_limit_bytes=24 * MIB)

    def toward(dz):
        return grid.pairs(lambda x, y, z, c: (x, y, z ^ dz, c))

    def along_z(blocks):
        return [blocks[0]] + [
            lax.ppermute(blocks[dz], both_axes, toward(dz)) for dz in range(1, DEPTH)
        ]

    def to_cores(blocks):
        others = [
            lax.ppermute(block, both_axes, grid.pairs(lambda x, y, z, c: (x, y, z, c ^ 1)))
            for block in blocks
        ]
        return [block for pair in zip(blocks, others) for block in pair]

    def backward_row(k, me_ref):
        x, _, _, _ = grid.place(me_ref[0])
        to_x = lax.rem(x + lax.rem(k, grid.rows), grid.rows)
        return lax.div(k, grid.rows) * grid.rows + to_x

    sum_order = [(dx, dy) for dy in range(grid.wide) for dx in range(grid.rows)]

    def to_owners(sums):
        got = [sums[0]]
        for part, (dx, dy) in list(zip(sums, sum_order))[1:]:
            got.append(
                lax.ppermute(
                    part,
                    both_axes,
                    grid.pairs(
                        lambda x, y, z, c, dx=dx, dy=dy: (
                            (x + dx) % grid.rows,
                            (y + dy) % grid.wide,
                            z,
                            c,
                        )
                    ),
                )
            )
        return got

    wide = slots + TILE_SIDE
    plane = rows // DEPTH
    raw = [tile_cols[0, 0].T, tile_edge_counts[0, 0].T, edge_pos[0, 0], edge_keep_bits[0, 0]]
    lists, *planes = pl.pallas_call(
        functools.partial(pack_kernel, grid),
        in_specs=[smem] + [pl.BlockSpec(memory_space=pltpu.HBM)] * 4,
        out_shape=(jax.ShapeDtypeStruct((rows, wide), i32),)
        + (jax.ShapeDtypeStruct((plane, wide + DEPTH * TILE_SIDE), i32),) * DEPTH,
        scratch_shapes=[pltpu.VMEM((rows, TILE_SIDE), i32)]
        + [pltpu.VMEM(a.shape, i32) for a in raw]
        + [pltpu.SemaphoreType.DMA((4,))],
        compiler_params=limit,
        cost_estimate=pl.CostEstimate(flops=2**21, bytes_accessed=2**17, transcendentals=0),
        name="pack",
    )(me, *raw)

    def from_peer(value, move):
        return lax.ppermute(value, both_axes, [(b, a) for a, b in grid.pairs(move)])

    along = [features, lax.ppermute(features, both_axes, toward(1))]
    *planes, along[1] = lax.optimization_barrier((*planes, along[1]))
    got_planes = along_z(planes)
    *got_planes, later = lax.optimization_barrier((*got_planes, features))
    along += [lax.ppermute(later, both_axes, toward(dz)) for dz in range(2, DEPTH)]
    both, plane_lists, counts = pl.pallas_call(
        functools.partial(relay_kernel, wide),
        out_shape=(
            jax.ShapeDtypeStruct((rows, wide + TILE_SIDE), i32),
            jax.ShapeDtypeStruct((rows, wide), i32),
            jax.ShapeDtypeStruct((rows, TILE_SIDE), i32),
        ),
        compiler_params=limit,
        cost_estimate=pl.CostEstimate(flops=2**14, bytes_accessed=2**18, transcendentals=0),
        name="relay",
    )(*got_planes)
    core_lists = [both, from_peer(both, lambda x, y, z, c: (x, y, z, c ^ 1))]
    row_lists = [
        from_peer(
            plane_lists, lambda x, y, z, c, dx=dx, dc=dc: ((x + dx) % grid.rows, y, z, c ^ dc)
        )
        for dx in range(1, grid.rows)
        for dc in range(CORES)
    ]
    wide_counts = [
        from_peer(counts, lambda x, y, z, c, dy=dy, dc=dc: (x, (y + dy) % grid.wide, z, c ^ dc))
        for dy in range(1, grid.wide)
        for dc in range(CORES)
    ]
    peer_lists = [lists] + [
        from_peer(lists, lambda x, y, z, c, dy=dy: (x, (y + dy) % grid.wide, z, c))
        for dy in range(1, grid.wide)
    ]
    side, depth = grid.summed * group, grid.gathered * group

    formation = pl.CostEstimate(
        flops=2 * rows * slots * TILE_SIDE * grid.rows * group,
        bytes_accessed=2 * side * depth,
        transcendentals=0,
    )
    product = pl.CostEstimate(
        flops=4 * side * depth * width, bytes_accessed=2 * side * depth, transcendentals=0
    )

    def whole(*shape):
        return pl.BlockSpec(shape, lambda k: (0,) * len(shape))

    core_lists[1], *peer_lists = lax.optimization_barrier((core_lists[1], *peer_lists))
    forward_block, roots = pl.pallas_call(
        functools.partial(forward_block_kernel, grid, slots),
        grid=(grid.summed,),
        in_specs=[smem]
        + [whole(rows, wide + TILE_SIDE)] * CORES
        + [whole(rows, wide)] * len(row_lists)
        + [whole(rows, TILE_SIDE)] * len(wide_counts),
        out_specs=(pl.BlockSpec((group, depth), lambda k: (k, 0)), whole(rows, TILE_SIDE)),
        out_shape=(
            jax.ShapeDtypeStruct((side, depth), bf16),
            jax.ShapeDtypeStruct((rows, TILE_SIDE), f32),
        ),
        scratch_shapes=[pltpu.VMEM((CORES * grid.rows, rows, wide), i32)],
        compiler_params=limit,
        cost_estimate=pl.CostEstimate(flops=2**16, bytes_accessed=2**16, transcendentals=0),
        name="forward_block",
    )(me, *core_lists, *row_lists, *wide_counts)
    along[-1], forward_block = lax.optimization_barrier((along[-1], forward_block))
    gathered = to_cores(along)
    scale, *sums = pl.pallas_call(
        functools.partial(forward_sum_kernel, grid),
        grid=(grid.summed,),
        in_specs=[smem, whole(rows, TILE_SIDE), pl.BlockSpec((group, depth), lambda k: (k, 0))]
        + [whole(group, width)] * grid.gathered,
        out_specs=(whole(group, width),) * (1 + grid.summed),
        out_shape=(jax.ShapeDtypeStruct((group, width), f32),) * (1 + grid.summed),
        scratch_shapes=[pltpu.VMEM((depth, 2 * width), bf16)],
        compiler_params=limit,
        cost_estimate=product,
        name="forward_sum",
    )(me, roots, forward_block, *gathered)
    sums = to_owners(sums)

    tall = group + hidden // DEPTH
    tall_shape = jax.ShapeDtypeStruct((tall, width), f32)
    hidden_out, *sent = pl.pallas_call(
        functools.partial(middle_kernel, grid),
        in_specs=[smem] + [vmem] * (6 + grid.summed),
        out_shape=(jax.ShapeDtypeStruct((group, hidden), f32),) + (tall_shape,) * DEPTH,
        scratch_shapes=[pltpu.VMEM((width, hidden), f32)],
        compiler_params=limit,
        cost_estimate=pl.CostEstimate(
            flops=36 * group * width * hidden, bytes_accessed=2**20, transcendentals=2**18
        ),
        name="middle",
    )(me, scale, features, weight, out_bias.reshape(1, hidden), cotangent, drop_keep, *sums)

    *peer_lists, sent[0] = lax.optimization_barrier((*peer_lists, sent[0]))
    backward_block = pl.pallas_call(
        functools.partial(backward_block_kernel, grid, slots),
        grid=(grid.gathered,),
        in_specs=[smem] + [pl.BlockSpec(lists.shape, lambda g: (0, 0))] * grid.wide,
        out_specs=pl.BlockSpec((side, group), lambda g: (0, g)),
        out_shape=jax.ShapeDtypeStruct((side, depth), bf16),
        compiler_params=limit,
        cost_estimate=formation,
        name="backward_block",
    )(me, *peer_lists)
    along = along_z(sent)
    along[-1], backward_block = lax.optimization_barrier((along[-1], backward_block))
    collected = to_cores(along)
    sums = pl.pallas_call(
        functools.partial(backward_sum_kernel, grid),
        grid_spec=pltpu.PrefetchScalarGridSpec(
            num_scalar_prefetch=1,
            grid=(grid.summed,),
            in_specs=[pl.BlockSpec((group, depth), lambda k, me_ref: (backward_row(k, me_ref), 0))]
            + [pl.BlockSpec((tall, width), lambda k, me_ref: (0, 0))] * grid.gathered,
            out_specs=(pl.BlockSpec((tall, width), lambda k, me_ref: (0, 0)),) * grid.summed,
            scratch_shapes=[
                pltpu.VMEM((grid.gathered, tall - group, width), f32),
                pltpu.VMEM((depth, 2 * width), bf16),
            ],
        ),
        out_shape=(tall_shape,) * grid.summed,
        compiler_params=limit,
        cost_estimate=product,
        name="backward_sum",
    )(me, backward_block, *collected)
    sums = to_owners(sums)
    grad_features, share = pl.pallas_call(
        functools.partial(finish_kernel, grid),
        in_specs=[smem] + [vmem] * (2 + grid.summed),
        out_shape=(
            jax.ShapeDtypeStruct((group, width), f32),
            jax.ShapeDtypeStruct((tall - group, width), f32),
        ),
        scratch_shapes=[pltpu.VMEM((grid.summed, tall - group, width), f32)],
        compiler_params=limit,
        cost_estimate=pl.CostEstimate(flops=2**18, bytes_accessed=2**19, transcendentals=0),
        name="finish",
    )(me, scale, sent[0], *sums)
    grad_weight = pl.pallas_call(
        functools.partial(join_kernel, grid),
        in_specs=[smem] + [vmem] * DEPTH,
        out_shape=jax.ShapeDtypeStruct((width, hidden), f32),
        compiler_params=limit,
        cost_estimate=pl.CostEstimate(flops=0, bytes_accessed=2**18, transcendentals=0),
        name="join",
    )(me, *along_z([share] * DEPTH))
    return (hidden_out, grad_features, grad_weight)


def solution(mesh):
    in_specs = (
        P(("row", "col"), None),
        P(),
        P(),
        P(("row", "col"), None),
        P(("row", "col"), None),
        P("row", "col", None, None),
        P("row", "col", None, None),
        P("row", "col", None, None),
        P("row", "col", None, None),
    )
    out_specs = (P(("row", "col"), None), P(("row", "col"), None), P())
    return jax.shard_map(shards, mesh=mesh, in_specs=in_specs, out_specs=out_specs, check_vma=False)
```

```python
import functools

import jax
import jax.numpy as jnp
from jax import lax
from jax.experimental import pallas as pl
from jax.experimental.pallas import tpu as pltpu
from jax.sharding import PartitionSpec as P

TILE_SIDE = 128
TPR = 4
EPT = 64
KEEP_RATE = 0.9
CORES = 2
DEPTH = 4

f32 = jnp.float32
bf16 = jnp.bfloat16
i32 = jnp.int32
highest = lax.Precision.HIGHEST
NT = (((1,), (1,)), ((), ()))
TN = (((0,), (0,)), ((), ()))
MIB = 1 << 20


class Grid:
    def __init__(self, rows, cols, group):
        self.rows, self.cols, self.group = rows, cols, group
        self.wide = cols // (DEPTH * CORES)
        self.count = rows * cols
        self.per = group // TILE_SIDE
        self.gathered = DEPTH * CORES
        self.summed = rows * self.wide

    def place(self, me):
        col = lax.rem(me, self.cols)
        core = lax.rem(col, CORES)
        rest = lax.div(col, CORES)
        return lax.div(me, self.cols), lax.rem(rest, self.wide), lax.div(rest, self.wide), core

    def col(self, z, y, core):
        return (z * self.wide + y) * CORES + core

    def number(self, x, y, z, core):
        return x * self.cols + self.col(z, y, core)

    def all_places(self):
        return [
            (x, y, z, core)
            for x in range(self.rows)
            for z in range(DEPTH)
            for y in range(self.wide)
            for core in range(CORES)
        ]

    def pairs(self, move):
        return [(self.number(*p), self.number(*move(*p))) for p in self.all_places()]


def gelu_exact(values):
    return 0.5 * values * (1.0 + lax.erf(values * 0.7071067811865476))


def gelu_slope(values):
    return (
        0.5 * (1.0 + lax.erf(values * 0.7071067811865476))
        + values * jnp.exp(-0.5 * values * values) * 0.3989422804014327
    )


def one_hot(index_row, size):
    places = lax.broadcasted_iota(i32, (size, index_row.shape[1]), 0)
    return jnp.where(places == index_row, 1.0, 0.0).astype(bf16)


def turned_times(values, table):
    return lax.dot_general(
        values.astype(f32).astype(bf16), table, TN, preferred_element_type=f32
    ).astype(i32)


def pack_kernel(grid, me_ref, *refs):
    hbm_refs, lists_ref, sent_refs, refs = refs[:4], refs[4], refs[5 : 5 + DEPTH], refs[5 + DEPTH :]
    counts_ref, vmem_refs, sem = refs[0], refs[1:5], refs[5]
    copies = [
        pltpu.make_async_copy(a, b, sem.at[n]) for n, (a, b) in enumerate(zip(hbm_refs, vmem_refs))
    ]
    for copy in copies:
        copy.start()
    for copy in copies:
        copy.wait()
    cols_ref, tile_counts_ref, pos_ref, keep_ref = vmem_refs
    rows, slots = pos_ref.shape
    slot = lax.broadcasted_iota(i32, (rows, slots), 1)
    tile_of = lax.broadcasted_iota(i32, (TPR, slots), 1) // EPT
    spread = jnp.where(tile_of == lax.broadcasted_iota(i32, (TPR, slots), 0), 1.0, 0.0)
    count = turned_times(tile_counts_ref[...], spread.astype(bf16))
    live = ((slot & (EPT - 1)) < count) & (keep_ref[...] == 1)
    pos = jnp.where(live, pos_ref[...], -1)
    lists_ref[:, :slots] = pos
    lane = lax.broadcasted_iota(i32, (TPR, TILE_SIDE), 1)
    k = lax.broadcasted_iota(i32, (TPR, TILE_SIDE), 0)
    lists_ref[:, slots:] = turned_times(cols_ref[...], jnp.where(lane == k, 1.0, 0.0).astype(bf16))
    target = lax.shift_right_arithmetic(pos, 7)
    ones = jnp.ones((8, slots), bf16)
    for t in range(rows):
        hot = one_hot(target[t : t + 1, :], TILE_SIDE)
        sums = lax.dot_general(ones, hot, NT, preferred_element_type=f32)
        counts_ref[t : t + 1, :] = sums[0:1, :].astype(i32)
    _, _, z, _ = grid.place(me_ref[0])
    plane = rows // DEPTH
    for dz, sent_ref in enumerate(sent_refs):
        at = pl.multiple_of((z ^ dz) * plane, 8)
        sent_ref[:, : slots + TILE_SIDE] = lists_ref[pl.ds(at, plane), :]
        for q in range(DEPTH):
            lanes = slice(slots + (q + 1) * TILE_SIDE, slots + (q + 2) * TILE_SIDE)
            sent_ref[:, lanes] = counts_ref[q * plane : (q + 1) * plane, :]


def plane_kernel(wide, *refs):
    got, both_ref = refs[:-1], refs[-1]
    plane = got[0].shape[0]
    for dz, ref in enumerate(got):
        both_ref[dz * plane : (dz + 1) * plane, :wide] = ref[:, :wide]
    for q in range(DEPTH):
        lanes = slice(wide + q * TILE_SIDE, wide + (q + 1) * TILE_SIDE)
        count = got[0][:, lanes]
        for ref in got[1:]:
            count = count + ref[:, lanes]
        both_ref[q * plane : (q + 1) * plane, wide:] = count


def chip_kernel(wide, lists_ref, own_ref, other_ref, chip_ref, counted_ref):
    rows = own_ref.shape[0]
    chip_ref[:rows, :] = own_ref[:, :wide]
    chip_ref[rows:, :] = other_ref[:, :wide]
    counted_ref[:, :wide] = lists_ref[...]
    counted_ref[:, wide:] = own_ref[:, wide:] + other_ref[:, wide:]


def add_kernel(*refs):
    total = refs[0][...]
    for ref in refs[1:-1]:
        total = total + ref[...]
    refs[-1][...] = total


def add_along_z_kernel(grid, me_ref, *refs):
    parts, (out_ref, placed_ref) = refs[:-2], refs[-2:]
    _, _, z, _ = grid.place(me_ref[0])
    for dz, ref in enumerate(parts):
        placed_ref[z ^ dz] = ref[...]
    total = placed_ref[0]
    for n in range(1, DEPTH):
        total = total + placed_ref[n]
    out_ref[...] = total


def slot_columns(columns, first, slots):
    tile = lax.broadcasted_iota(i32, (1, slots), 1) // EPT
    spread = jnp.broadcast_to(columns[:, first : first + 1], (1, slots))
    for k in range(1, TPR):
        spread = jnp.where(tile == k, columns[:, first + k : first + k + 1], spread)
    return spread


def split_values(grid, values, both_ref, scale_of=None):
    width = values[0].shape[1]
    for g, ref in enumerate(values):
        value = ref[...]
        if scale_of is not None:
            value = value * scale_of(g)
        high = value.astype(bf16)
        rows = slice(g * grid.group, (g + 1) * grid.group)
        both_ref[rows, :width] = high
        both_ref[rows, width:] = (value - high.astype(f32)).astype(bf16)


def forward_block_kernel(grid, slots, me_ref, *refs):
    chip_refs, refs = refs[: grid.rows], refs[grid.rows :]
    counted_refs, (block_ref, root_ref, lists_ref) = refs[: grid.wide], refs[grid.wide :]
    step = pl.program_id(0)
    x, y, _, core = grid.place(me_ref[0])
    wide = slots + TILE_SIDE
    rows = counted_refs[0].shape[0]

    @pl.when(step == 0)
    def _():
        count = sum(ref[:, wide:] for ref in counted_refs)
        root_ref[...] = lax.rsqrt(1.0 + count.astype(f32))
        for n, ref in enumerate(chip_refs):
            lists_ref[n] = ref[...]

    dx, dy = lax.rem(step, grid.rows), lax.div(step, grid.rows)
    to_y = lax.rem(y + dy, grid.wide)
    plane = grid.wide * CORES * grid.per
    for g in range(grid.gathered):
        for s in range(grid.per):
            at = (g % CORES) * rows + (g // CORES) * plane + (to_y * CORES + core) * grid.per + s
            row = lists_ref[dx, pl.ds(at, 1), :]
            pos = row[:, :slots]
            target = lax.shift_right_arithmetic(pos, 7)
            source = slot_columns(row[:, slots:], 0, slots) * TILE_SIDE + (pos & (TILE_SIDE - 1))
            hot = lax.dot_general(
                one_hot(target, TILE_SIDE),
                one_hot(source - x * grid.group, grid.group),
                NT,
                preferred_element_type=f32,
            )
            block_ref[
                s * TILE_SIDE : (s + 1) * TILE_SIDE, g * grid.group : (g + 1) * grid.group
            ] = hot.astype(bf16)


def forward_sum_kernel(grid, me_ref, root_ref, block_ref, *refs):
    values, (scale_ref, *outs, both_ref) = refs[: grid.gathered], refs[grid.gathered :]
    width = values[0].shape[1]
    step = pl.program_id(0)

    @pl.when(step == 0)
    def _():
        _, y, z, core = grid.place(me_ref[0])

        def scale_of(g):
            at = grid.col(z ^ (g // CORES), y, core ^ (g % CORES)) * grid.per
            return spread_down([root_ref[pl.ds(at + s, 1), :] for s in range(grid.per)])

        scale_ref[...] = scale_of(0)
        split_values(grid, values, both_ref, scale_of)

    part = jnp.dot(block_ref[...], both_ref[...], preferred_element_type=f32)
    total = part[:, :width] + part[:, width:]
    for k, out_ref in enumerate(outs):

        @pl.when(step == k)
        def _(out_ref=out_ref):
            out_ref[...] = total


def backward_block_kernel(grid, slots, me_ref, *refs):
    lists, block_ref = refs[:-1], refs[-1]
    g = pl.program_id(0)
    x, y, z, core = grid.place(me_ref[0])
    col = grid.col(z ^ lax.div(g, CORES), y, core ^ lax.rem(g, CORES))
    side = grid.rows * grid.group
    for k, list_ref in enumerate(lists):
        for s in range(grid.per):
            row = list_ref[pl.ds(col * grid.per + s, 1), :]
            pos = row[:, :slots]
            target = lax.shift_right_arithmetic(pos, 7)
            source = slot_columns(row[:, slots:], 0, slots) * TILE_SIDE + (pos & (TILE_SIDE - 1))
            hot = lax.dot_general(
                one_hot(source, side), one_hot(target, TILE_SIDE), NT, preferred_element_type=f32
            )
            block_ref[k * side : (k + 1) * side, s * TILE_SIDE : (s + 1) * TILE_SIDE] = hot.astype(
                bf16
            )


def spread_down(rows):
    return jnp.concatenate(
        [jnp.broadcast_to(row, (TILE_SIDE, TILE_SIDE)).T for row in rows], axis=0
    )


def backward_sum_kernel(grid, me_ref, block_ref, *refs):
    values, (own_ref, other_ref, *outs, both_ref) = refs[: grid.gathered], refs[grid.gathered :]
    width = values[0].shape[1]
    step = pl.program_id(0)

    @pl.when(step == 0)
    def _():
        split_values(grid, values, both_ref)
        share = own_ref[...] + other_ref[...]
        for out_ref in outs:
            out_ref[grid.group :, :] = share

    part = jnp.dot(block_ref[...], both_ref[...], preferred_element_type=f32)
    total = part[:, :width] + part[:, width:]
    for k, out_ref in enumerate(outs):

        @pl.when(step == k)
        def _(out_ref=out_ref):
            out_ref[: grid.group, :] = total


def finish_kernel(grid, me_ref, scale_ref, sent_ref, *refs):
    sums, (features_grad_ref, weight_grad_ref, parts_ref) = refs[:-3], refs[-3:]
    x, y, z, core = grid.place(me_ref[0])
    total = sent_ref[...]
    for k, ref in enumerate(sums):
        total = total + ref[: grid.group, :]
        from_x = lax.rem(x + grid.rows - k % grid.rows, grid.rows)
        from_y = lax.rem(y + grid.wide - k // grid.rows, grid.wide)
        parts_ref[from_y * grid.rows + from_x] = ref[grid.group :, :]
    features_grad_ref[...] = scale_ref[...] * total
    high = parts_ref.shape[1] // 2
    for n in range(grid.summed):
        part = parts_ref[n]
        weight_grad_ref[n * high : (n + 1) * high, :] = jnp.concatenate(
            [part[:high, :], part[high:, :]], axis=1
        )


def middle_kernel(
    grid,
    me_ref,
    scale_ref,
    features_ref,
    weight_ref,
    bias_ref,
    cotangent_ref,
    drop_ref,
    *refs,
):
    sums, refs = refs[: grid.summed], refs[grid.summed :]
    hidden_ref, sent_ref, *part_refs, parts_ref = refs
    x, y, _, _ = grid.place(me_ref[0])
    scale = scale_ref[...]
    total = scale * features_ref[...]
    for ref in sums:
        total = total + ref[...]
    mixed = scale * total
    weight = weight_ref[...]
    pre_act = jnp.dot(mixed, weight, precision=highest, preferred_element_type=f32) + bias_ref[...]
    dropout = drop_ref[...].astype(f32) / KEEP_RATE
    hidden_ref[...] = gelu_exact(pre_act) * dropout
    grad_pre = cotangent_ref[...] * dropout * gelu_slope(pre_act)
    sent_ref[...] = scale * lax.dot_general(
        grad_pre, weight, NT, precision=highest, preferred_element_type=f32
    )
    weight_grad = lax.dot_general(
        mixed, grad_pre, TN, precision=highest, preferred_element_type=f32
    )
    width = features_ref.shape[1]
    high = width // grid.summed
    for n in range(grid.summed):
        part = weight_grad[n * high : (n + 1) * high, :]
        parts_ref[n] = jnp.concatenate([part[:, :width], part[:, width:]], axis=0)
    for k, part_ref in enumerate(part_refs):
        to_x = lax.rem(x + k % grid.rows, grid.rows)
        to_y = lax.rem(y + k // grid.rows, grid.wide)
        part_ref[...] = parts_ref[to_y * grid.rows + to_x]


def shards(
    features,
    weight,
    out_bias,
    cotangent,
    drop_keep,
    tile_cols,
    tile_edge_counts,
    edge_pos,
    edge_keep_bits,
):
    group, width = features.shape
    hidden = weight.shape[1]
    rows, slots = edge_pos.shape[2:]
    grid = Grid(lax.axis_size("row"), lax.axis_size("col"), group)
    both_axes = ("row", "col")
    me = lax.axis_index(both_axes).astype(i32)[None]
    smem = pl.BlockSpec(memory_space=pltpu.SMEM)
    vmem = pl.BlockSpec(memory_space=pltpu.VMEM)
    limit = pltpu.CompilerParams(vmem_limit_bytes=24 * MIB)

    def toward(dz):
        return grid.pairs(lambda x, y, z, c: (x, y, z ^ dz, c))

    def along_z(blocks):
        return [blocks[0]] + [
            lax.ppermute(blocks[dz], both_axes, toward(dz)) for dz in range(1, DEPTH)
        ]

    def to_cores(blocks):
        others = [
            lax.ppermute(block, both_axes, grid.pairs(lambda x, y, z, c: (x, y, z, c ^ 1)))
            for block in blocks
        ]
        return [block for pair in zip(blocks, others) for block in pair]

    def backward_row(k, me_ref):
        x, _, _, _ = grid.place(me_ref[0])
        to_x = lax.rem(x + lax.rem(k, grid.rows), grid.rows)
        return lax.div(k, grid.rows) * grid.rows + to_x

    sum_order = [(dx, dy) for dy in range(grid.wide) for dx in range(grid.rows)]

    def to_owners(sums):
        got = [sums[0]]
        for part, (dx, dy) in list(zip(sums, sum_order))[1:]:
            got.append(
                lax.ppermute(
                    part,
                    both_axes,
                    grid.pairs(
                        lambda x, y, z, c, dx=dx, dy=dy: (
                            (x + dx) % grid.rows,
                            (y + dy) % grid.wide,
                            z,
                            c,
                        )
                    ),
                )
            )
        return got

    wide = slots + TILE_SIDE
    plane = rows // DEPTH
    raw = [tile_cols[0, 0].T, tile_edge_counts[0, 0].T, edge_pos[0, 0], edge_keep_bits[0, 0]]
    lists, *planes = pl.pallas_call(
        functools.partial(pack_kernel, grid),
        in_specs=[smem] + [pl.BlockSpec(memory_space=pltpu.HBM)] * 4,
        out_shape=(jax.ShapeDtypeStruct((rows, wide), i32),)
        + (jax.ShapeDtypeStruct((plane, wide + DEPTH * TILE_SIDE), i32),) * DEPTH,
        scratch_shapes=[pltpu.VMEM((rows, TILE_SIDE), i32)]
        + [pltpu.VMEM(a.shape, i32) for a in raw]
        + [pltpu.SemaphoreType.DMA((4,))],
        compiler_params=limit,
        cost_estimate=pl.CostEstimate(flops=2**21, bytes_accessed=2**17, transcendentals=0),
        name="pack",
    )(me, *raw)

    def from_peer(value, move):
        return lax.ppermute(value, both_axes, [(b, a) for a, b in grid.pairs(move)])

    along = [features, lax.ppermute(features, both_axes, toward(1))]
    *planes, along[1] = lax.optimization_barrier((*planes, along[1]))
    got_planes = along_z(planes)
    *got_planes, later = lax.optimization_barrier((*got_planes, features))
    along += [lax.ppermute(later, both_axes, toward(dz)) for dz in range(2, DEPTH)]
    small = pl.CostEstimate(flops=2**14, bytes_accessed=2**18, transcendentals=0)
    both = pl.pallas_call(
        functools.partial(plane_kernel, wide),
        out_shape=jax.ShapeDtypeStruct((rows, wide + TILE_SIDE), i32),
        compiler_params=limit,
        cost_estimate=small,
        name="plane",
    )(*got_planes)
    chip, counted = pl.pallas_call(
        functools.partial(chip_kernel, wide),
        out_shape=(
            jax.ShapeDtypeStruct((CORES * rows, wide), i32),
            jax.ShapeDtypeStruct((rows, wide + TILE_SIDE), i32),
        ),
        compiler_params=limit,
        cost_estimate=small,
        name="chip",
    )(lists, both, from_peer(both, lambda x, y, z, c: (x, y, z, c ^ 1)))
    chips = [chip] + [
        from_peer(chip, lambda x, y, z, c, dx=dx: ((x + dx) % grid.rows, y, z, c))
        for dx in range(1, grid.rows)
    ]
    peer_lists = [counted] + [
        from_peer(counted, lambda x, y, z, c, dy=dy: (x, (y + dy) % grid.wide, z, c))
        for dy in range(1, grid.wide)
    ]
    side, depth = grid.summed * group, grid.gathered * group

    formation = pl.CostEstimate(
        flops=2 * rows * slots * TILE_SIDE * grid.rows * group,
        bytes_accessed=2 * side * depth,
        transcendentals=0,
    )
    product = pl.CostEstimate(
        flops=4 * side * depth * width, bytes_accessed=2 * side * depth, transcendentals=0
    )

    def whole(*shape):
        return pl.BlockSpec(shape, lambda k: (0,) * len(shape))

    forward_block, roots = pl.pallas_call(
        functools.partial(forward_block_kernel, grid, slots),
        grid=(grid.summed,),
        in_specs=[smem]
        + [whole(CORES * rows, wide)] * grid.rows
        + [whole(rows, wide + TILE_SIDE)] * grid.wide,
        out_specs=(pl.BlockSpec((group, depth), lambda k: (k, 0)), whole(rows, TILE_SIDE)),
        out_shape=(
            jax.ShapeDtypeStruct((side, depth), bf16),
            jax.ShapeDtypeStruct((rows, TILE_SIDE), f32),
        ),
        scratch_shapes=[pltpu.VMEM((grid.rows, CORES * rows, wide), i32)],
        compiler_params=limit,
        cost_estimate=pl.CostEstimate(flops=2**16, bytes_accessed=2**16, transcendentals=0),
        name="forward_block",
    )(me, *chips, *peer_lists)
    along[-1], forward_block = lax.optimization_barrier((along[-1], forward_block))
    gathered = to_cores(along)
    scale, *sums = pl.pallas_call(
        functools.partial(forward_sum_kernel, grid),
        grid=(grid.summed,),
        in_specs=[smem, whole(rows, TILE_SIDE), pl.BlockSpec((group, depth), lambda k: (k, 0))]
        + [whole(group, width)] * grid.gathered,
        out_specs=(whole(group, width),) * (1 + grid.summed),
        out_shape=(jax.ShapeDtypeStruct((group, width), f32),) * (1 + grid.summed),
        scratch_shapes=[pltpu.VMEM((depth, 2 * width), bf16)],
        compiler_params=limit,
        cost_estimate=product,
        name="forward_sum",
    )(me, roots, forward_block, *gathered)
    *peer_lists, sums[0] = lax.optimization_barrier((*peer_lists, sums[0]))
    backward_block = pl.pallas_call(
        functools.partial(backward_block_kernel, grid, slots),
        grid=(grid.gathered,),
        in_specs=[smem] + [pl.BlockSpec((rows, wide + TILE_SIDE), lambda g: (0, 0))] * grid.wide,
        out_specs=pl.BlockSpec((side, group), lambda g: (0, g)),
        out_shape=jax.ShapeDtypeStruct((side, depth), bf16),
        compiler_params=limit,
        cost_estimate=formation,
        name="backward_block",
    )(me, *peer_lists)
    sums = to_owners(sums)
    sums[-1], backward_block = lax.optimization_barrier((sums[-1], backward_block))

    part_shape = jax.ShapeDtypeStruct((width // grid.summed * 2, width), f32)
    tall = group + part_shape.shape[0]
    tall_shape = jax.ShapeDtypeStruct((tall, width), f32)
    hidden_out, sent, *parts = pl.pallas_call(
        functools.partial(middle_kernel, grid),
        in_specs=[smem] + [vmem] * (6 + grid.summed),
        out_shape=(
            jax.ShapeDtypeStruct((group, hidden), f32),
            jax.ShapeDtypeStruct((group, width), f32),
        )
        + (part_shape,) * grid.summed,
        scratch_shapes=[pltpu.VMEM((grid.summed, *part_shape.shape), f32)],
        compiler_params=limit,
        cost_estimate=pl.CostEstimate(
            flops=36 * group * width * hidden, bytes_accessed=2**20, transcendentals=2**18
        ),
        name="middle",
    )(me, scale, features, weight, out_bias.reshape(1, hidden), cotangent, drop_keep, *sums)

    along = along_z([sent] * DEPTH)
    share = pl.pallas_call(
        add_kernel,
        out_shape=part_shape,
        compiler_params=limit,
        cost_estimate=small,
        name="add_parts",
    )(*to_owners(parts))
    over_z = along_z([share] * DEPTH)
    along[-1], *over_z = lax.optimization_barrier((along[-1], *over_z))
    share = pl.pallas_call(
        functools.partial(add_along_z_kernel, grid),
        in_specs=[smem] + [vmem] * DEPTH,
        out_shape=part_shape,
        scratch_shapes=[pltpu.VMEM((DEPTH, *part_shape.shape), f32)],
        compiler_params=limit,
        cost_estimate=small,
        name="add_along_z",
    )(me, *over_z)
    shares = [share, from_peer(share, lambda x, y, z, c: (x, y, z, c ^ 1))]
    collected = to_cores(along)
    sums = pl.pallas_call(
        functools.partial(backward_sum_kernel, grid),
        grid_spec=pltpu.PrefetchScalarGridSpec(
            num_scalar_prefetch=1,
            grid=(grid.summed,),
            in_specs=[pl.BlockSpec((group, depth), lambda k, me_ref: (backward_row(k, me_ref), 0))]
            + [pl.BlockSpec((group, width), lambda k, me_ref: (0, 0))] * grid.gathered
            + [pl.BlockSpec(part_shape.shape, lambda k, me_ref: (0, 0))] * CORES,
            out_specs=(pl.BlockSpec((tall, width), lambda k, me_ref: (0, 0)),) * grid.summed,
            scratch_shapes=[pltpu.VMEM((depth, 2 * width), bf16)],
        ),
        out_shape=(tall_shape,) * grid.summed,
        compiler_params=limit,
        cost_estimate=product,
        name="backward_sum",
    )(me, backward_block, *collected, *shares)
    sums = to_owners(sums)
    grad_features, grad_weight = pl.pallas_call(
        functools.partial(finish_kernel, grid),
        in_specs=[smem] + [vmem] * (2 + grid.summed),
        out_shape=(
            jax.ShapeDtypeStruct((group, width), f32),
            jax.ShapeDtypeStruct((width, hidden), f32),
        ),
        scratch_shapes=[pltpu.VMEM((grid.summed, *part_shape.shape), f32)],
        compiler_params=limit,
        cost_estimate=pl.CostEstimate(flops=2**18, bytes_accessed=2**19, transcendentals=0),
        name="finish",
    )(me, scale, sent, *sums)
    return (hidden_out, grad_features, grad_weight)


def solution(mesh):
    in_specs = (
        P(("row", "col"), None),
        P(),
        P(),
        P(("row", "col"), None),
        P(("row", "col"), None),
        P("row", "col", None, None),
        P("row", "col", None, None),
        P("row", "col", None, None),
        P("row", "col", None, None),
    )
    out_specs = (P(("row", "col"), None), P(("row", "col"), None), P())
    return jax.shard_map(shards, mesh=mesh, in_specs=in_specs, out_specs=out_specs, check_vma=False)
```

```python
import functools

import jax
import jax.numpy as jnp
from jax import lax
from jax.experimental import pallas as pl
from jax.experimental.pallas import tpu as pltpu
from jax.sharding import PartitionSpec as P

TILE_SIDE = 128
TPR = 4
EPT = 64
KEEP_RATE = 0.9
CORES = 2
DEPTH = 4

f32 = jnp.float32
bf16 = jnp.bfloat16
i32 = jnp.int32
highest = lax.Precision.HIGHEST
NT = (((1,), (1,)), ((), ()))
TN = (((0,), (0,)), ((), ()))
MIB = 1 << 20


class Grid:
    def __init__(self, rows, cols, group):
        self.rows, self.cols, self.group = rows, cols, group
        self.wide = cols // (DEPTH * CORES)
        self.count = rows * cols
        self.per = group // TILE_SIDE
        self.gathered = DEPTH * CORES
        self.summed = rows * self.wide

    def place(self, me):
        col = lax.rem(me, self.cols)
        core = lax.rem(col, CORES)
        rest = lax.div(col, CORES)
        return lax.div(me, self.cols), lax.rem(rest, self.wide), lax.div(rest, self.wide), core

    def col(self, z, y, core):
        return (z * self.wide + y) * CORES + core

    def number(self, x, y, z, core):
        return x * self.cols + self.col(z, y, core)

    def all_places(self):
        return [
            (x, y, z, core)
            for x in range(self.rows)
            for z in range(DEPTH)
            for y in range(self.wide)
            for core in range(CORES)
        ]

    def pairs(self, move):
        return [(self.number(*p), self.number(*move(*p))) for p in self.all_places()]


def gelu_exact(values):
    return 0.5 * values * (1.0 + lax.erf(values * 0.7071067811865476))


def gelu_slope(values):
    return (
        0.5 * (1.0 + lax.erf(values * 0.7071067811865476))
        + values * jnp.exp(-0.5 * values * values) * 0.3989422804014327
    )


def one_hot(index_row, size):
    places = lax.broadcasted_iota(i32, (size, index_row.shape[1]), 0)
    return jnp.where(places == index_row, 1.0, 0.0).astype(bf16)


def turned_times(values, table):
    return lax.dot_general(
        values.astype(f32).astype(bf16), table, TN, preferred_element_type=f32
    ).astype(i32)


def pack_kernel(grid, me_ref, *refs):
    hbm_refs, lists_ref, sent_refs, refs = refs[:4], refs[4], refs[5 : 5 + DEPTH], refs[5 + DEPTH :]
    counts_ref, vmem_refs, sem = refs[0], refs[1:5], refs[5]
    copies = [
        pltpu.make_async_copy(a, b, sem.at[n]) for n, (a, b) in enumerate(zip(hbm_refs, vmem_refs))
    ]
    for copy in copies:
        copy.start()
    for copy in copies:
        copy.wait()
    cols_ref, tile_counts_ref, pos_ref, keep_ref = vmem_refs
    rows, slots = pos_ref.shape
    slot = lax.broadcasted_iota(i32, (rows, slots), 1)
    tile_of = lax.broadcasted_iota(i32, (TPR, slots), 1) // EPT
    spread = jnp.where(tile_of == lax.broadcasted_iota(i32, (TPR, slots), 0), 1.0, 0.0)
    count = turned_times(tile_counts_ref[...], spread.astype(bf16))
    live = ((slot & (EPT - 1)) < count) & (keep_ref[...] == 1)
    pos = jnp.where(live, pos_ref[...], -1)
    lists_ref[:, :slots] = pos
    lane = lax.broadcasted_iota(i32, (TPR, TILE_SIDE), 1)
    k = lax.broadcasted_iota(i32, (TPR, TILE_SIDE), 0)
    lists_ref[:, slots:] = turned_times(cols_ref[...], jnp.where(lane == k, 1.0, 0.0).astype(bf16))
    target = lax.shift_right_arithmetic(pos, 7)
    ones = jnp.ones((8, slots), bf16)
    for t in range(rows):
        hot = one_hot(target[t : t + 1, :], TILE_SIDE)
        sums = lax.dot_general(ones, hot, NT, preferred_element_type=f32)
        counts_ref[t : t + 1, :] = sums[0:1, :].astype(i32)
    _, _, z, _ = grid.place(me_ref[0])
    plane = rows // DEPTH
    for dz, sent_ref in enumerate(sent_refs):
        at = pl.multiple_of((z ^ dz) * plane, 8)
        sent_ref[:, : slots + TILE_SIDE] = lists_ref[pl.ds(at, plane), :]
        for q in range(DEPTH):
            lanes = slice(slots + (q + 1) * TILE_SIDE, slots + (q + 2) * TILE_SIDE)
            sent_ref[:, lanes] = counts_ref[q * plane : (q + 1) * plane, :]


def plane_kernel(wide, *refs):
    got, both_ref = refs[:-1], refs[-1]
    plane = got[0].shape[0]
    for dz, ref in enumerate(got):
        both_ref[dz * plane : (dz + 1) * plane, :wide] = ref[:, :wide]
    for q in range(DEPTH):
        lanes = slice(wide + q * TILE_SIDE, wide + (q + 1) * TILE_SIDE)
        count = got[0][:, lanes]
        for ref in got[1:]:
            count = count + ref[:, lanes]
        both_ref[q * plane : (q + 1) * plane, wide:] = count


def chip_kernel(wide, lists_ref, own_ref, other_ref, chip_ref, counted_ref):
    rows = own_ref.shape[0]
    chip_ref[:rows, :] = own_ref[:, :wide]
    chip_ref[rows:, :] = other_ref[:, :wide]
    counted_ref[:, :wide] = lists_ref[...]
    counted_ref[:, wide:] = own_ref[:, wide:] + other_ref[:, wide:]


def add_kernel(*refs):
    total = refs[0][...]
    for ref in refs[1:-1]:
        total = total + ref[...]
    refs[-1][...] = total


def add_along_z_kernel(grid, me_ref, *refs):
    parts, (out_ref, placed_ref) = refs[:-2], refs[-2:]
    _, _, z, _ = grid.place(me_ref[0])
    for dz, ref in enumerate(parts):
        placed_ref[z ^ dz] = ref[...]
    total = placed_ref[0]
    for n in range(1, DEPTH):
        total = total + placed_ref[n]
    out_ref[...] = total


def slot_columns(columns, first, slots):
    tile = lax.broadcasted_iota(i32, (1, slots), 1) // EPT
    spread = jnp.broadcast_to(columns[:, first : first + 1], (1, slots))
    for k in range(1, TPR):
        spread = jnp.where(tile == k, columns[:, first + k : first + k + 1], spread)
    return spread


def split_values(grid, values, both_ref, scale_of=None):
    width = values[0].shape[1]
    for g, ref in enumerate(values):
        value = ref[...]
        if scale_of is not None:
            value = value * scale_of(g)
        high = value.astype(bf16)
        rows = slice(g * grid.group, (g + 1) * grid.group)
        both_ref[rows, :width] = high
        both_ref[rows, width:] = (value - high.astype(f32)).astype(bf16)


def forward_block_kernel(grid, slots, me_ref, *refs):
    chip_refs, refs = refs[: grid.rows], refs[grid.rows :]
    counted_refs, (block_ref, root_ref, lists_ref) = refs[: grid.wide], refs[grid.wide :]
    step = pl.program_id(0)
    x, y, _, core = grid.place(me_ref[0])
    wide = slots + TILE_SIDE
    rows = counted_refs[0].shape[0]

    @pl.when(step == 0)
    def _():
        count = sum(ref[:, wide:] for ref in counted_refs)
        root_ref[...] = lax.rsqrt(1.0 + count.astype(f32))
        for n, ref in enumerate(chip_refs):
            lists_ref[n] = ref[...]

    dx, dy = lax.rem(step, grid.rows), lax.div(step, grid.rows)
    to_y = lax.rem(y + dy, grid.wide)
    plane = grid.wide * CORES * grid.per
    for g in range(grid.gathered):
        for s in range(grid.per):
            at = (g % CORES) * rows + (g // CORES) * plane + (to_y * CORES + core) * grid.per + s
            row = lists_ref[dx, pl.ds(at, 1), :]
            pos = row[:, :slots]
            target = lax.shift_right_arithmetic(pos, 7)
            source = slot_columns(row[:, slots:], 0, slots) * TILE_SIDE + (pos & (TILE_SIDE - 1))
            hot = lax.dot_general(
                one_hot(target, TILE_SIDE),
                one_hot(source - x * grid.group, grid.group),
                NT,
                preferred_element_type=f32,
            )
            block_ref[
                s * TILE_SIDE : (s + 1) * TILE_SIDE, g * grid.group : (g + 1) * grid.group
            ] = hot.astype(bf16)


def forward_sum_kernel(grid, me_ref, root_ref, block_ref, *refs):
    values, (scale_ref, *outs, both_ref) = refs[: grid.gathered], refs[grid.gathered :]
    width = values[0].shape[1]
    step = pl.program_id(0)

    @pl.when(step == 0)
    def _():
        _, y, z, core = grid.place(me_ref[0])

        def scale_of(g):
            at = grid.col(z ^ (g // CORES), y, core ^ (g % CORES)) * grid.per
            return spread_down([root_ref[pl.ds(at + s, 1), :] for s in range(grid.per)])

        scale_ref[...] = scale_of(0)
        split_values(grid, values, both_ref, scale_of)

    part = jnp.dot(block_ref[...], both_ref[...], preferred_element_type=f32)
    total = part[:, :width] + part[:, width:]
    for k, out_ref in enumerate(outs):

        @pl.when(step == k)
        def _(out_ref=out_ref):
            out_ref[...] = total


def backward_block_kernel(grid, slots, me_ref, *refs):
    lists, block_ref = refs[:-1], refs[-1]
    g = pl.program_id(0)
    x, y, z, core = grid.place(me_ref[0])
    col = grid.col(z ^ lax.div(g, CORES), y, core ^ lax.rem(g, CORES))
    side = grid.rows * grid.group
    for k, list_ref in enumerate(lists):
        for s in range(grid.per):
            row = list_ref[pl.ds(col * grid.per + s, 1), :]
            pos = row[:, :slots]
            target = lax.shift_right_arithmetic(pos, 7)
            source = slot_columns(row[:, slots:], 0, slots) * TILE_SIDE + (pos & (TILE_SIDE - 1))
            hot = lax.dot_general(
                one_hot(source, side), one_hot(target, TILE_SIDE), NT, preferred_element_type=f32
            )
            block_ref[k * side : (k + 1) * side, s * TILE_SIDE : (s + 1) * TILE_SIDE] = hot.astype(
                bf16
            )


def spread_down(rows):
    return jnp.concatenate(
        [jnp.broadcast_to(row, (TILE_SIDE, TILE_SIDE)).T for row in rows], axis=0
    )


def backward_sum_kernel(grid, me_ref, block_ref, *refs):
    values, (*outs, both_ref) = refs[: grid.gathered], refs[grid.gathered :]
    width = values[0].shape[1]
    step = pl.program_id(0)

    @pl.when(step == 0)
    def _():
        split_values(grid, values, both_ref)

    part = jnp.dot(block_ref[...], both_ref[...], preferred_element_type=f32)
    total = part[:, :width] + part[:, width:]
    for k, out_ref in enumerate(outs):

        @pl.when(step == k)
        def _(out_ref=out_ref):
            out_ref[...] = total


def finish_kernel(grid, me_ref, scale_ref, sent_ref, *refs):
    sums, refs = refs[: grid.summed], refs[grid.summed :]
    parts, (features_grad_ref, weight_grad_ref, parts_ref) = refs[:-3], refs[-3:]
    x, y, z, core = grid.place(me_ref[0])
    total = sent_ref[...]
    for ref in sums:
        total = total + ref[...]
    features_grad_ref[...] = scale_ref[...] * total
    for k, ref in enumerate(parts):
        from_x = lax.rem(x + grid.rows - k % grid.rows, grid.rows)
        from_y = lax.rem(y + grid.wide - k // grid.rows, grid.wide)
        parts_ref[from_y * grid.rows + from_x] = ref[...]
    high = parts_ref.shape[1] // 2
    for n in range(grid.summed):
        part = parts_ref[n]
        weight_grad_ref[n * high : (n + 1) * high, :] = jnp.concatenate(
            [part[:high, :], part[high:, :]], axis=1
        )


def middle_kernel(
    grid,
    me_ref,
    scale_ref,
    features_ref,
    weight_ref,
    bias_ref,
    cotangent_ref,
    drop_ref,
    *refs,
):
    sums, refs = refs[: grid.summed], refs[grid.summed :]
    hidden_ref, sent_ref, *part_refs, parts_ref = refs
    x, y, _, _ = grid.place(me_ref[0])
    scale = scale_ref[...]
    total = scale * features_ref[...]
    for ref in sums:
        total = total + ref[...]
    mixed = scale * total
    weight = weight_ref[...]
    pre_act = jnp.dot(mixed, weight, precision=highest, preferred_element_type=f32) + bias_ref[...]
    dropout = drop_ref[...].astype(f32) / KEEP_RATE
    hidden_ref[...] = gelu_exact(pre_act) * dropout
    grad_pre = cotangent_ref[...] * dropout * gelu_slope(pre_act)
    sent_ref[...] = scale * lax.dot_general(
        grad_pre, weight, NT, precision=highest, preferred_element_type=f32
    )
    weight_grad = lax.dot_general(
        mixed, grad_pre, TN, precision=highest, preferred_element_type=f32
    )
    width = features_ref.shape[1]
    high = width // grid.summed
    for n in range(grid.summed):
        part = weight_grad[n * high : (n + 1) * high, :]
        parts_ref[n] = jnp.concatenate([part[:, :width], part[:, width:]], axis=0)
    for k, part_ref in enumerate(part_refs):
        to_x = lax.rem(x + k % grid.rows, grid.rows)
        to_y = lax.rem(y + k // grid.rows, grid.wide)
        part_ref[...] = parts_ref[to_y * grid.rows + to_x]


def shards(
    features,
    weight,
    out_bias,
    cotangent,
    drop_keep,
    tile_cols,
    tile_edge_counts,
    edge_pos,
    edge_keep_bits,
):
    group, width = features.shape
    hidden = weight.shape[1]
    rows, slots = edge_pos.shape[2:]
    grid = Grid(lax.axis_size("row"), lax.axis_size("col"), group)
    both_axes = ("row", "col")
    me = lax.axis_index(both_axes).astype(i32)[None]
    smem = pl.BlockSpec(memory_space=pltpu.SMEM)
    vmem = pl.BlockSpec(memory_space=pltpu.VMEM)
    limit = pltpu.CompilerParams(vmem_limit_bytes=24 * MIB)

    def toward(dz):
        return grid.pairs(lambda x, y, z, c: (x, y, z ^ dz, c))

    def along_z(blocks):
        return [blocks[0]] + [
            lax.ppermute(blocks[dz], both_axes, toward(dz)) for dz in range(1, DEPTH)
        ]

    def to_cores(blocks):
        others = [
            lax.ppermute(block, both_axes, grid.pairs(lambda x, y, z, c: (x, y, z, c ^ 1)))
            for block in blocks
        ]
        return [block for pair in zip(blocks, others) for block in pair]

    def backward_row(k, me_ref):
        x, _, _, _ = grid.place(me_ref[0])
        to_x = lax.rem(x + lax.rem(k, grid.rows), grid.rows)
        return lax.div(k, grid.rows) * grid.rows + to_x

    sum_order = [(dx, dy) for dy in range(grid.wide) for dx in range(grid.rows)]

    def to_owners(sums):
        got = [sums[0]]
        for part, (dx, dy) in list(zip(sums, sum_order))[1:]:
            got.append(
                lax.ppermute(
                    part,
                    both_axes,
                    grid.pairs(
                        lambda x, y, z, c, dx=dx, dy=dy: (
                            (x + dx) % grid.rows,
                            (y + dy) % grid.wide,
                            z,
                            c,
                        )
                    ),
                )
            )
        return got

    wide = slots + TILE_SIDE
    plane = rows // DEPTH
    raw = [tile_cols[0, 0].T, tile_edge_counts[0, 0].T, edge_pos[0, 0], edge_keep_bits[0, 0]]
    lists, *planes = pl.pallas_call(
        functools.partial(pack_kernel, grid),
        in_specs=[smem] + [pl.BlockSpec(memory_space=pltpu.HBM)] * 4,
        out_shape=(jax.ShapeDtypeStruct((rows, wide), i32),)
        + (jax.ShapeDtypeStruct((plane, wide + DEPTH * TILE_SIDE), i32),) * DEPTH,
        scratch_shapes=[pltpu.VMEM((rows, TILE_SIDE), i32)]
        + [pltpu.VMEM(a.shape, i32) for a in raw]
        + [pltpu.SemaphoreType.DMA((4,))],
        compiler_params=pltpu.CompilerParams(vmem_limit_bytes=60 * MIB),
        cost_estimate=pl.CostEstimate(flops=2**31, bytes_accessed=2**23, transcendentals=0),
        name="pack",
    )(me, *raw)

    def from_peer(value, move):
        return lax.ppermute(value, both_axes, [(b, a) for a, b in grid.pairs(move)])

    along = along_z([features] * DEPTH)
    got_planes = along_z(planes)
    *along, got_planes[0] = lax.optimization_barrier((*along, got_planes[0]))
    small = pl.CostEstimate(flops=2**14, bytes_accessed=2**18, transcendentals=0)
    both = pl.pallas_call(
        functools.partial(plane_kernel, wide),
        out_shape=jax.ShapeDtypeStruct((rows, wide + TILE_SIDE), i32),
        compiler_params=limit,
        cost_estimate=small,
        name="plane",
    )(*got_planes)
    chip, counted = pl.pallas_call(
        functools.partial(chip_kernel, wide),
        out_shape=(
            jax.ShapeDtypeStruct((CORES * rows, wide), i32),
            jax.ShapeDtypeStruct((rows, wide + TILE_SIDE), i32),
        ),
        compiler_params=limit,
        cost_estimate=small,
        name="chip",
    )(lists, both, from_peer(both, lambda x, y, z, c: (x, y, z, c ^ 1)))
    chips = [chip] + [
        from_peer(chip, lambda x, y, z, c, dx=dx: ((x + dx) % grid.rows, y, z, c))
        for dx in range(1, grid.rows)
    ]
    peer_lists = [counted] + [
        from_peer(counted, lambda x, y, z, c, dy=dy: (x, (y + dy) % grid.wide, z, c))
        for dy in range(1, grid.wide)
    ]
    side, depth = grid.summed * group, grid.gathered * group

    formation = pl.CostEstimate(
        flops=2 * rows * slots * TILE_SIDE * grid.rows * group,
        bytes_accessed=2 * side * depth,
        transcendentals=0,
    )
    product = pl.CostEstimate(
        flops=4 * side * depth * width, bytes_accessed=2 * side * depth, transcendentals=0
    )

    def whole(*shape):
        return pl.BlockSpec(shape, lambda k: (0,) * len(shape))

    forward_block, roots = pl.pallas_call(
        functools.partial(forward_block_kernel, grid, slots),
        grid=(grid.summed,),
        in_specs=[smem]
        + [whole(CORES * rows, wide)] * grid.rows
        + [whole(rows, wide + TILE_SIDE)] * grid.wide,
        out_specs=(pl.BlockSpec((group, depth), lambda k: (k, 0)), whole(rows, TILE_SIDE)),
        out_shape=(
            jax.ShapeDtypeStruct((side, depth), bf16),
            jax.ShapeDtypeStruct((rows, TILE_SIDE), f32),
        ),
        scratch_shapes=[pltpu.VMEM((grid.rows, CORES * rows, wide), i32)],
        compiler_params=limit,
        cost_estimate=pl.CostEstimate(flops=2**16, bytes_accessed=2**16, transcendentals=0),
        name="forward_block",
    )(me, *chips, *peer_lists)
    along[-1], forward_block = lax.optimization_barrier((along[-1], forward_block))
    gathered = to_cores(along)
    scale, *sums = pl.pallas_call(
        functools.partial(forward_sum_kernel, grid),
        grid=(grid.summed,),
        in_specs=[smem, whole(rows, TILE_SIDE), pl.BlockSpec((group, depth), lambda k: (k, 0))]
        + [whole(group, width)] * grid.gathered,
        out_specs=(whole(group, width),) * (1 + grid.summed),
        out_shape=(jax.ShapeDtypeStruct((group, width), f32),) * (1 + grid.summed),
        scratch_shapes=[pltpu.VMEM((depth, 2 * width), bf16)],
        compiler_params=limit,
        cost_estimate=product,
        name="forward_sum",
    )(me, roots, forward_block, *gathered)
    *peer_lists, sums[0] = lax.optimization_barrier((*peer_lists, sums[0]))
    backward_block = pl.pallas_call(
        functools.partial(backward_block_kernel, grid, slots),
        grid=(grid.gathered,),
        in_specs=[smem] + [pl.BlockSpec((rows, wide + TILE_SIDE), lambda g: (0, 0))] * grid.wide,
        out_specs=pl.BlockSpec((side, group), lambda g: (0, g)),
        out_shape=jax.ShapeDtypeStruct((side, depth), bf16),
        compiler_params=limit,
        cost_estimate=formation,
        name="backward_block",
    )(me, *peer_lists)
    sums = to_owners(sums)
    sums[-1], backward_block = lax.optimization_barrier((sums[-1], backward_block))

    part_shape = jax.ShapeDtypeStruct((width // grid.summed * 2, width), f32)
    hidden_out, sent, *parts = pl.pallas_call(
        functools.partial(middle_kernel, grid),
        in_specs=[smem] + [vmem] * (6 + grid.summed),
        out_shape=(
            jax.ShapeDtypeStruct((group, hidden), f32),
            jax.ShapeDtypeStruct((group, width), f32),
        )
        + (part_shape,) * grid.summed,
        scratch_shapes=[pltpu.VMEM((grid.summed, *part_shape.shape), f32)],
        compiler_params=limit,
        cost_estimate=pl.CostEstimate(
            flops=36 * group * width * hidden, bytes_accessed=2**20, transcendentals=2**18
        ),
        name="middle",
    )(me, scale, features, weight, out_bias.reshape(1, hidden), cotangent, drop_keep, *sums)

    along = along_z([sent] * DEPTH)
    share = pl.pallas_call(
        add_kernel,
        out_shape=part_shape,
        compiler_params=limit,
        cost_estimate=small,
        name="add_parts",
    )(*to_owners(parts))
    along[-1], share = lax.optimization_barrier((along[-1], share))
    over_z = along_z([share] * DEPTH)
    collected = to_cores(along)
    sums = pl.pallas_call(
        functools.partial(backward_sum_kernel, grid),
        grid_spec=pltpu.PrefetchScalarGridSpec(
            num_scalar_prefetch=1,
            grid=(grid.summed,),
            in_specs=[pl.BlockSpec((group, depth), lambda k, me_ref: (backward_row(k, me_ref), 0))]
            + [pl.BlockSpec((group, width), lambda k, me_ref: (0, 0))] * grid.gathered,
            out_specs=(pl.BlockSpec((group, width), lambda k, me_ref: (0, 0)),) * grid.summed,
            scratch_shapes=[pltpu.VMEM((depth, 2 * width), bf16)],
        ),
        out_shape=(jax.ShapeDtypeStruct((group, width), f32),) * grid.summed,
        compiler_params=limit,
        cost_estimate=product,
        name="backward_sum",
    )(me, backward_block, *collected)
    first, *over_z = lax.optimization_barrier((sums[0], *over_z))
    sums = [first, *sums[1:]]
    share = pl.pallas_call(
        functools.partial(add_along_z_kernel, grid),
        in_specs=[smem] + [vmem] * DEPTH,
        out_shape=part_shape,
        scratch_shapes=[pltpu.VMEM((DEPTH, *part_shape.shape), f32)],
        compiler_params=limit,
        cost_estimate=small,
        name="add_along_z",
    )(me, *over_z)
    shares = [share, from_peer(share, lambda x, y, z, c: (x, y, z, c ^ 1))]
    share = pl.pallas_call(
        add_kernel,
        out_shape=part_shape,
        compiler_params=limit,
        cost_estimate=small,
        name="add_cores",
    )(*shares)
    sums = to_owners(sums)
    parts = to_owners([share] * grid.summed)
    grad_features, grad_weight = pl.pallas_call(
        functools.partial(finish_kernel, grid),
        in_specs=[smem] + [vmem] * (2 + 2 * grid.summed),
        out_shape=(
            jax.ShapeDtypeStruct((group, width), f32),
            jax.ShapeDtypeStruct((width, hidden), f32),
        ),
        scratch_shapes=[pltpu.VMEM((grid.summed, *part_shape.shape), f32)],
        compiler_params=limit,
        cost_estimate=pl.CostEstimate(flops=2**18, bytes_accessed=2**19, transcendentals=0),
        name="finish",
    )(me, scale, sent, *sums, *parts)
    return (hidden_out, grad_features, grad_weight)


def solution(mesh):
    in_specs = (
        P(("row", "col"), None),
        P(),
        P(),
        P(("row", "col"), None),
        P(("row", "col"), None),
        P("row", "col", None, None),
        P("row", "col", None, None),
        P("row", "col", None, None),
        P("row", "col", None, None),
    )
    out_specs = (P(("row", "col"), None), P(("row", "col"), None), P())
    return jax.shard_map(shards, mesh=mesh, in_specs=in_specs, out_specs=out_specs, check_vma=False)
```

```python
import functools

import jax
import jax.numpy as jnp
from jax import lax
from jax.experimental import pallas as pl
from jax.experimental.pallas import tpu as pltpu
from jax.sharding import PartitionSpec as P

TILE_SIDE = 128
TPR = 4
EPT = 64
KEEP_RATE = 0.9
CORES = 2
DEPTH = 4

f32 = jnp.float32
bf16 = jnp.bfloat16
i32 = jnp.int32
highest = lax.Precision.HIGHEST
NT = (((1,), (1,)), ((), ()))
TN = (((0,), (0,)), ((), ()))
MIB = 1 << 20


class Grid:
    def __init__(self, rows, cols, group):
        self.rows, self.cols, self.group = rows, cols, group
        self.wide = cols // (DEPTH * CORES)
        self.count = rows * cols
        self.per = group // TILE_SIDE
        self.gathered = DEPTH * CORES
        self.summed = rows * self.wide

    def place(self, me):
        col = lax.rem(me, self.cols)
        core = lax.rem(col, CORES)
        rest = lax.div(col, CORES)
        return lax.div(me, self.cols), lax.rem(rest, self.wide), lax.div(rest, self.wide), core

    def col(self, z, y, core):
        return (z * self.wide + y) * CORES + core

    def number(self, x, y, z, core):
        return x * self.cols + self.col(z, y, core)

    def all_places(self):
        return [
            (x, y, z, core)
            for x in range(self.rows)
            for z in range(DEPTH)
            for y in range(self.wide)
            for core in range(CORES)
        ]

    def pairs(self, move):
        return [(self.number(*p), self.number(*move(*p))) for p in self.all_places()]


def gelu_exact(values):
    return 0.5 * values * (1.0 + lax.erf(values * 0.7071067811865476))


def gelu_slope(values):
    return (
        0.5 * (1.0 + lax.erf(values * 0.7071067811865476))
        + values * jnp.exp(-0.5 * values * values) * 0.3989422804014327
    )


def one_hot(index_row, size):
    places = lax.broadcasted_iota(i32, (size, index_row.shape[1]), 0)
    return jnp.where(places == index_row, 1.0, 0.0).astype(bf16)


def turned_times(values, table):
    return lax.dot_general(
        values.astype(f32).astype(bf16), table, TN, preferred_element_type=f32
    ).astype(i32)


def pack_kernel(grid, me_ref, *refs):
    hbm_refs, lists_ref, sent_refs, refs = refs[:4], refs[4], refs[5 : 5 + DEPTH], refs[5 + DEPTH :]
    counts_ref, vmem_refs, sem = refs[0], refs[1:5], refs[5]
    copies = [
        pltpu.make_async_copy(a, b, sem.at[n]) for n, (a, b) in enumerate(zip(hbm_refs, vmem_refs))
    ]
    for copy in copies:
        copy.start()
    for copy in copies:
        copy.wait()
    cols_ref, tile_counts_ref, pos_ref, keep_ref = vmem_refs
    rows, slots = pos_ref.shape
    slot = lax.broadcasted_iota(i32, (rows, slots), 1)
    tile_of = lax.broadcasted_iota(i32, (TPR, slots), 1) // EPT
    spread = jnp.where(tile_of == lax.broadcasted_iota(i32, (TPR, slots), 0), 1.0, 0.0)
    count = turned_times(tile_counts_ref[...], spread.astype(bf16))
    live = ((slot & (EPT - 1)) < count) & (keep_ref[...] == 1)
    pos = jnp.where(live, pos_ref[...], -1)
    lists_ref[:, :slots] = pos
    lane = lax.broadcasted_iota(i32, (TPR, TILE_SIDE), 1)
    k = lax.broadcasted_iota(i32, (TPR, TILE_SIDE), 0)
    lists_ref[:, slots:] = turned_times(cols_ref[...], jnp.where(lane == k, 1.0, 0.0).astype(bf16))
    target = lax.shift_right_arithmetic(pos, 7)
    ones = jnp.ones((8, slots), bf16)
    for t in range(rows):
        hot = one_hot(target[t : t + 1, :], TILE_SIDE)
        sums = lax.dot_general(ones, hot, NT, preferred_element_type=f32)
        counts_ref[t : t + 1, :] = sums[0:1, :].astype(i32)
    _, _, z, _ = grid.place(me_ref[0])
    plane = rows // DEPTH
    for dz, sent_ref in enumerate(sent_refs):
        at = pl.multiple_of((z ^ dz) * plane, 8)
        sent_ref[:, : slots + TILE_SIDE] = lists_ref[pl.ds(at, plane), :]
        for q in range(DEPTH):
            lanes = slice(slots + (q + 1) * TILE_SIDE, slots + (q + 2) * TILE_SIDE)
            sent_ref[:, lanes] = counts_ref[q * plane : (q + 1) * plane, :]


def plane_kernel(wide, *refs):
    got, both_ref = refs[:-1], refs[-1]
    plane = got[0].shape[0]
    for dz, ref in enumerate(got):
        both_ref[dz * plane : (dz + 1) * plane, :wide] = ref[:, :wide]
    for q in range(DEPTH):
        lanes = slice(wide + q * TILE_SIDE, wide + (q + 1) * TILE_SIDE)
        count = got[0][:, lanes]
        for ref in got[1:]:
            count = count + ref[:, lanes]
        both_ref[q * plane : (q + 1) * plane, wide:] = count


def chip_kernel(wide, lists_ref, own_ref, other_ref, chip_ref, counted_ref):
    rows = own_ref.shape[0]
    chip_ref[:rows, :] = own_ref[:, :wide]
    chip_ref[rows:, :] = other_ref[:, :wide]
    counted_ref[:, :wide] = lists_ref[...]
    counted_ref[:, wide:] = own_ref[:, wide:] + other_ref[:, wide:]


def add_kernel(*refs):
    total = refs[0][...]
    for ref in refs[1:-1]:
        total = total + ref[...]
    refs[-1][...] = total


def add_along_z_kernel(grid, me_ref, *refs):
    parts, (out_ref, placed_ref) = refs[:-2], refs[-2:]
    _, _, z, _ = grid.place(me_ref[0])
    for dz, ref in enumerate(parts):
        placed_ref[z ^ dz] = ref[...]
    total = placed_ref[0]
    for n in range(1, DEPTH):
        total = total + placed_ref[n]
    out_ref[...] = total


def slot_columns(columns, first, slots):
    tile = lax.broadcasted_iota(i32, (1, slots), 1) // EPT
    spread = jnp.broadcast_to(columns[:, first : first + 1], (1, slots))
    for k in range(1, TPR):
        spread = jnp.where(tile == k, columns[:, first + k : first + k + 1], spread)
    return spread


def split_values(grid, values, both_ref, scale_of=None):
    width = values[0].shape[1]
    for g, ref in enumerate(values):
        value = ref[...]
        if scale_of is not None:
            value = value * scale_of(g)
        high = value.astype(bf16)
        rows = slice(g * grid.group, (g + 1) * grid.group)
        both_ref[rows, :width] = high
        both_ref[rows, width:] = (value - high.astype(f32)).astype(bf16)


def forward_block_kernel(grid, slots, me_ref, *refs):
    chip_refs, refs = refs[: grid.rows], refs[grid.rows :]
    counted_refs, (block_ref, root_ref, lists_ref) = refs[: grid.wide], refs[grid.wide :]
    step = pl.program_id(0)
    x, y, _, core = grid.place(me_ref[0])
    wide = slots + TILE_SIDE
    rows = counted_refs[0].shape[0]

    @pl.when(step == 0)
    def _():
        count = sum(ref[:, wide:] for ref in counted_refs)
        root_ref[...] = lax.rsqrt(1.0 + count.astype(f32))
        for n, ref in enumerate(chip_refs):
            lists_ref[n] = ref[...]

    dx, dy = lax.rem(step, grid.rows), lax.div(step, grid.rows)
    to_y = lax.rem(y + dy, grid.wide)
    plane = grid.wide * CORES * grid.per
    for g in range(grid.gathered):
        for s in range(grid.per):
            at = (g % CORES) * rows + (g // CORES) * plane + (to_y * CORES + core) * grid.per + s
            row = lists_ref[dx, pl.ds(at, 1), :]
            pos = row[:, :slots]
            target = lax.shift_right_arithmetic(pos, 7)
            source = slot_columns(row[:, slots:], 0, slots) * TILE_SIDE + (pos & (TILE_SIDE - 1))
            hot = lax.dot_general(
                one_hot(target, TILE_SIDE),
                one_hot(source - x * grid.group, grid.group),
                NT,
                preferred_element_type=f32,
            )
            block_ref[
                s * TILE_SIDE : (s + 1) * TILE_SIDE, g * grid.group : (g + 1) * grid.group
            ] = hot.astype(bf16)


def forward_sum_kernel(grid, me_ref, root_ref, block_ref, *refs):
    values, (scale_ref, *outs, both_ref) = refs[: grid.gathered], refs[grid.gathered :]
    width = values[0].shape[1]
    step = pl.program_id(0)

    @pl.when(step == 0)
    def _():
        _, y, z, core = grid.place(me_ref[0])

        def scale_of(g):
            at = grid.col(z ^ (g // CORES), y, core ^ (g % CORES)) * grid.per
            return spread_down([root_ref[pl.ds(at + s, 1), :] for s in range(grid.per)])

        scale_ref[...] = scale_of(0)
        split_values(grid, values, both_ref, scale_of)

    part = jnp.dot(block_ref[...], both_ref[...], preferred_element_type=f32)
    total = part[:, :width] + part[:, width:]
    for k, out_ref in enumerate(outs):

        @pl.when(step == k)
        def _(out_ref=out_ref):
            out_ref[...] = total


def backward_block_kernel(grid, slots, me_ref, *refs):
    lists, block_ref = refs[:-1], refs[-1]
    g = pl.program_id(0)
    x, y, z, core = grid.place(me_ref[0])
    col = grid.col(z ^ lax.div(g, CORES), y, core ^ lax.rem(g, CORES))
    side = grid.rows * grid.group
    for k, list_ref in enumerate(lists):
        for s in range(grid.per):
            row = list_ref[pl.ds(col * grid.per + s, 1), :]
            pos = row[:, :slots]
            target = lax.shift_right_arithmetic(pos, 7)
            source = slot_columns(row[:, slots:], 0, slots) * TILE_SIDE + (pos & (TILE_SIDE - 1))
            hot = lax.dot_general(
                one_hot(source, side), one_hot(target, TILE_SIDE), NT, preferred_element_type=f32
            )
            block_ref[k * side : (k + 1) * side, s * TILE_SIDE : (s + 1) * TILE_SIDE] = hot.astype(
                bf16
            )


def spread_down(rows):
    return jnp.concatenate(
        [jnp.broadcast_to(row, (TILE_SIDE, TILE_SIDE)).T for row in rows], axis=0
    )


def backward_sum_kernel(grid, me_ref, block_ref, *refs):
    values, (*outs, both_ref) = refs[: grid.gathered], refs[grid.gathered :]
    width = values[0].shape[1]
    step = pl.program_id(0)

    @pl.when(step == 0)
    def _():
        split_values(grid, values, both_ref)

    part = jnp.dot(block_ref[...], both_ref[...], preferred_element_type=f32)
    total = part[:, :width] + part[:, width:]
    for k, out_ref in enumerate(outs):

        @pl.when(step == k)
        def _(out_ref=out_ref):
            out_ref[...] = total


def finish_kernel(grid, me_ref, scale_ref, sent_ref, *refs):
    sums, refs = refs[: grid.summed], refs[grid.summed :]
    parts, (features_grad_ref, weight_grad_ref, parts_ref) = refs[:-3], refs[-3:]
    x, y, z, core = grid.place(me_ref[0])
    total = sent_ref[...]
    for ref in sums:
        total = total + ref[...]
    features_grad_ref[...] = scale_ref[...] * total
    for k, ref in enumerate(parts):
        from_x = lax.rem(x + grid.rows - k % grid.rows, grid.rows)
        from_y = lax.rem(y + grid.wide - k // grid.rows, grid.wide)
        parts_ref[from_y * grid.rows + from_x] = ref[...]
    high = parts_ref.shape[1] // 2
    for n in range(grid.summed):
        part = parts_ref[n]
        weight_grad_ref[n * high : (n + 1) * high, :] = jnp.concatenate(
            [part[:high, :], part[high:, :]], axis=1
        )


def middle_kernel(
    grid,
    me_ref,
    scale_ref,
    features_ref,
    weight_ref,
    bias_ref,
    cotangent_ref,
    drop_ref,
    *refs,
):
    sums, refs = refs[: grid.summed], refs[grid.summed :]
    hidden_ref, sent_ref, *part_refs, parts_ref = refs
    x, y, _, _ = grid.place(me_ref[0])
    scale = scale_ref[...]
    total = scale * features_ref[...]
    for ref in sums:
        total = total + ref[...]
    mixed = scale * total
    weight = weight_ref[...]
    pre_act = jnp.dot(mixed, weight, precision=highest, preferred_element_type=f32) + bias_ref[...]
    dropout = drop_ref[...].astype(f32) / KEEP_RATE
    hidden_ref[...] = gelu_exact(pre_act) * dropout
    grad_pre = cotangent_ref[...] * dropout * gelu_slope(pre_act)
    sent_ref[...] = scale * lax.dot_general(
        grad_pre, weight, NT, precision=highest, preferred_element_type=f32
    )
    weight_grad = lax.dot_general(
        mixed, grad_pre, TN, precision=highest, preferred_element_type=f32
    )
    width = features_ref.shape[1]
    high = width // grid.summed
    for n in range(grid.summed):
        part = weight_grad[n * high : (n + 1) * high, :]
        parts_ref[n] = jnp.concatenate([part[:, :width], part[:, width:]], axis=0)
    for k, part_ref in enumerate(part_refs):
        to_x = lax.rem(x + k % grid.rows, grid.rows)
        to_y = lax.rem(y + k // grid.rows, grid.wide)
        part_ref[...] = parts_ref[to_y * grid.rows + to_x]


def shards(
    features,
    weight,
    out_bias,
    cotangent,
    drop_keep,
    tile_cols,
    tile_edge_counts,
    edge_pos,
    edge_keep_bits,
):
    group, width = features.shape
    hidden = weight.shape[1]
    rows, slots = edge_pos.shape[2:]
    grid = Grid(lax.axis_size("row"), lax.axis_size("col"), group)
    both_axes = ("row", "col")
    me = lax.axis_index(both_axes).astype(i32)[None]
    smem = pl.BlockSpec(memory_space=pltpu.SMEM)
    vmem = pl.BlockSpec(memory_space=pltpu.VMEM)
    limit = pltpu.CompilerParams(vmem_limit_bytes=24 * MIB)

    def toward(dz):
        return grid.pairs(lambda x, y, z, c: (x, y, z ^ dz, c))

    def along_z(blocks):
        return [blocks[0]] + [
            lax.ppermute(blocks[dz], both_axes, toward(dz)) for dz in range(1, DEPTH)
        ]

    def to_cores(blocks):
        others = [
            lax.ppermute(block, both_axes, grid.pairs(lambda x, y, z, c: (x, y, z, c ^ 1)))
            for block in blocks
        ]
        return [block for pair in zip(blocks, others) for block in pair]

    def backward_row(k, me_ref):
        x, _, _, _ = grid.place(me_ref[0])
        to_x = lax.rem(x + lax.rem(k, grid.rows), grid.rows)
        return lax.div(k, grid.rows) * grid.rows + to_x

    sum_order = [(dx, dy) for dy in range(grid.wide) for dx in range(grid.rows)]

    def to_owners(sums):
        got = [sums[0]]
        for part, (dx, dy) in list(zip(sums, sum_order))[1:]:
            got.append(
                lax.ppermute(
                    part,
                    both_axes,
                    grid.pairs(
                        lambda x, y, z, c, dx=dx, dy=dy: (
                            (x + dx) % grid.rows,
                            (y + dy) % grid.wide,
                            z,
                            c,
                        )
                    ),
                )
            )
        return got

    wide = slots + TILE_SIDE
    plane = rows // DEPTH
    raw = [tile_cols[0, 0].T, tile_edge_counts[0, 0].T, edge_pos[0, 0], edge_keep_bits[0, 0]]
    lists, *planes = pl.pallas_call(
        functools.partial(pack_kernel, grid),
        in_specs=[smem] + [pl.BlockSpec(memory_space=pltpu.HBM)] * 4,
        out_shape=(jax.ShapeDtypeStruct((rows, wide), i32),)
        + (jax.ShapeDtypeStruct((plane, wide + DEPTH * TILE_SIDE), i32),) * DEPTH,
        scratch_shapes=[pltpu.VMEM((rows, TILE_SIDE), i32)]
        + [pltpu.VMEM(a.shape, i32) for a in raw]
        + [pltpu.SemaphoreType.DMA((4,))],
        compiler_params=pltpu.CompilerParams(vmem_limit_bytes=60 * MIB),
        cost_estimate=pl.CostEstimate(flops=2**31, bytes_accessed=2**23, transcendentals=0),
        name="pack",
    )(me, *raw)

    def from_peer(value, move):
        return lax.ppermute(value, both_axes, [(b, a) for a, b in grid.pairs(move)])

    along = [features] + [lax.ppermute(features, both_axes, toward(dz)) for dz in (1, 2)]
    got_planes = along_z(planes)
    *along, got_planes[0] = lax.optimization_barrier((*along, got_planes[0]))
    *got_planes, later = lax.optimization_barrier((*got_planes, features))
    along += [lax.ppermute(later, both_axes, toward(dz)) for dz in range(3, DEPTH)]
    small = pl.CostEstimate(flops=2**14, bytes_accessed=2**18, transcendentals=0)
    both = pl.pallas_call(
        functools.partial(plane_kernel, wide),
        out_shape=jax.ShapeDtypeStruct((rows, wide + TILE_SIDE), i32),
        compiler_params=limit,
        cost_estimate=small,
        name="plane",
    )(*got_planes)
    chip, counted = pl.pallas_call(
        functools.partial(chip_kernel, wide),
        out_shape=(
            jax.ShapeDtypeStruct((CORES * rows, wide), i32),
            jax.ShapeDtypeStruct((rows, wide + TILE_SIDE), i32),
        ),
        compiler_params=limit,
        cost_estimate=small,
        name="chip",
    )(lists, both, from_peer(both, lambda x, y, z, c: (x, y, z, c ^ 1)))
    chips = [chip] + [
        from_peer(chip, lambda x, y, z, c, dx=dx: ((x + dx) % grid.rows, y, z, c))
        for dx in range(1, grid.rows)
    ]
    peer_lists = [counted] + [
        from_peer(counted, lambda x, y, z, c, dy=dy: (x, (y + dy) % grid.wide, z, c))
        for dy in range(1, grid.wide)
    ]
    side, depth = grid.summed * group, grid.gathered * group

    formation = pl.CostEstimate(
        flops=2 * rows * slots * TILE_SIDE * grid.rows * group,
        bytes_accessed=2 * side * depth,
        transcendentals=0,
    )
    product = pl.CostEstimate(
        flops=4 * side * depth * width, bytes_accessed=2 * side * depth, transcendentals=0
    )

    def whole(*shape):
        return pl.BlockSpec(shape, lambda k: (0,) * len(shape))

    forward_block, roots = pl.pallas_call(
        functools.partial(forward_block_kernel, grid, slots),
        grid=(grid.summed,),
        in_specs=[smem]
        + [whole(CORES * rows, wide)] * grid.rows
        + [whole(rows, wide + TILE_SIDE)] * grid.wide,
        out_specs=(pl.BlockSpec((group, depth), lambda k: (k, 0)), whole(rows, TILE_SIDE)),
        out_shape=(
            jax.ShapeDtypeStruct((side, depth), bf16),
            jax.ShapeDtypeStruct((rows, TILE_SIDE), f32),
        ),
        scratch_shapes=[pltpu.VMEM((grid.rows, CORES * rows, wide), i32)],
        compiler_params=limit,
        cost_estimate=pl.CostEstimate(flops=2**16, bytes_accessed=2**16, transcendentals=0),
        name="forward_block",
    )(me, *chips, *peer_lists)
    along[-1], forward_block = lax.optimization_barrier((along[-1], forward_block))
    gathered = to_cores(along)
    scale, *sums = pl.pallas_call(
        functools.partial(forward_sum_kernel, grid),
        grid=(grid.summed,),
        in_specs=[smem, whole(rows, TILE_SIDE), pl.BlockSpec((group, depth), lambda k: (k, 0))]
        + [whole(group, width)] * grid.gathered,
        out_specs=(whole(group, width),) * (1 + grid.summed),
        out_shape=(jax.ShapeDtypeStruct((group, width), f32),) * (1 + grid.summed),
        scratch_shapes=[pltpu.VMEM((depth, 2 * width), bf16)],
        compiler_params=limit,
        cost_estimate=product,
        name="forward_sum",
    )(me, roots, forward_block, *gathered)
    *peer_lists, sums[0] = lax.optimization_barrier((*peer_lists, sums[0]))
    backward_block = pl.pallas_call(
        functools.partial(backward_block_kernel, grid, slots),
        grid=(grid.gathered,),
        in_specs=[smem] + [pl.BlockSpec((rows, wide + TILE_SIDE), lambda g: (0, 0))] * grid.wide,
        out_specs=pl.BlockSpec((side, group), lambda g: (0, g)),
        out_shape=jax.ShapeDtypeStruct((side, depth), bf16),
        compiler_params=limit,
        cost_estimate=formation,
        name="backward_block",
    )(me, *peer_lists)
    sums = to_owners(sums)
    sums[-1], backward_block = lax.optimization_barrier((sums[-1], backward_block))

    part_shape = jax.ShapeDtypeStruct((width // grid.summed * 2, width), f32)
    hidden_out, sent, *parts = pl.pallas_call(
        functools.partial(middle_kernel, grid),
        in_specs=[smem] + [vmem] * (6 + grid.summed),
        out_shape=(
            jax.ShapeDtypeStruct((group, hidden), f32),
            jax.ShapeDtypeStruct((group, width), f32),
        )
        + (part_shape,) * grid.summed,
        scratch_shapes=[pltpu.VMEM((grid.summed, *part_shape.shape), f32)],
        compiler_params=limit,
        cost_estimate=pl.CostEstimate(
            flops=36 * group * width * hidden, bytes_accessed=2**20, transcendentals=2**18
        ),
        name="middle",
    )(me, scale, features, weight, out_bias.reshape(1, hidden), cotangent, drop_keep, *sums)

    along = along_z([sent] * DEPTH)
    share = pl.pallas_call(
        add_kernel,
        out_shape=part_shape,
        compiler_params=limit,
        cost_estimate=small,
        name="add_parts",
    )(*to_owners(parts))
    along[-1], share = lax.optimization_barrier((along[-1], share))
    over_z = along_z([share] * DEPTH)
    collected = to_cores(along)
    sums = pl.pallas_call(
        functools.partial(backward_sum_kernel, grid),
        grid_spec=pltpu.PrefetchScalarGridSpec(
            num_scalar_prefetch=1,
            grid=(grid.summed,),
            in_specs=[pl.BlockSpec((group, depth), lambda k, me_ref: (backward_row(k, me_ref), 0))]
            + [pl.BlockSpec((group, width), lambda k, me_ref: (0, 0))] * grid.gathered,
            out_specs=(pl.BlockSpec((group, width), lambda k, me_ref: (0, 0)),) * grid.summed,
            scratch_shapes=[pltpu.VMEM((depth, 2 * width), bf16)],
        ),
        out_shape=(jax.ShapeDtypeStruct((group, width), f32),) * grid.summed,
        compiler_params=limit,
        cost_estimate=product,
        name="backward_sum",
    )(me, backward_block, *collected)
    first, *over_z = lax.optimization_barrier((sums[0], *over_z))
    sums = [first, *sums[1:]]
    share = pl.pallas_call(
        functools.partial(add_along_z_kernel, grid),
        in_specs=[smem] + [vmem] * DEPTH,
        out_shape=part_shape,
        scratch_shapes=[pltpu.VMEM((DEPTH, *part_shape.shape), f32)],
        compiler_params=limit,
        cost_estimate=small,
        name="add_along_z",
    )(me, *over_z)
    shares = [share, from_peer(share, lambda x, y, z, c: (x, y, z, c ^ 1))]
    share = pl.pallas_call(
        add_kernel,
        out_shape=part_shape,
        compiler_params=limit,
        cost_estimate=small,
        name="add_cores",
    )(*shares)
    sums = to_owners(sums)
    parts = to_owners([share] * grid.summed)
    grad_features, grad_weight = pl.pallas_call(
        functools.partial(finish_kernel, grid),
        in_specs=[smem] + [vmem] * (2 + 2 * grid.summed),
        out_shape=(
            jax.ShapeDtypeStruct((group, width), f32),
            jax.ShapeDtypeStruct((width, hidden), f32),
        ),
        scratch_shapes=[pltpu.VMEM((grid.summed, *part_shape.shape), f32)],
        compiler_params=limit,
        cost_estimate=pl.CostEstimate(flops=2**18, bytes_accessed=2**19, transcendentals=0),
        name="finish",
    )(me, scale, sent, *sums, *parts)
    return (hidden_out, grad_features, grad_weight)


def solution(mesh):
    in_specs = (
        P(("row", "col"), None),
        P(),
        P(),
        P(("row", "col"), None),
        P(("row", "col"), None),
        P("row", "col", None, None),
        P("row", "col", None, None),
        P("row", "col", None, None),
        P("row", "col", None, None),
    )
    out_specs = (P(("row", "col"), None), P(("row", "col"), None), P())
    return jax.shard_map(shards, mesh=mesh, in_specs=in_specs, out_specs=out_specs, check_vma=False)
```

```python
import functools

import jax
import jax.numpy as jnp
from jax import lax
from jax.experimental import pallas as pl
from jax.experimental.pallas import tpu as pltpu
from jax.sharding import PartitionSpec as P

TILE_SIDE = 128
TPR = 4
EPT = 64
KEEP_RATE = 0.9
CORES = 2
DEPTH = 4

f32 = jnp.float32
bf16 = jnp.bfloat16
i32 = jnp.int32
highest = lax.Precision.HIGHEST
NT = (((1,), (1,)), ((), ()))
TN = (((0,), (0,)), ((), ()))
MIB = 1 << 20


class Grid:
    def __init__(self, rows, cols, group):
        self.rows, self.cols, self.group = rows, cols, group
        self.wide = cols // (DEPTH * CORES)
        self.count = rows * cols
        self.per = group // TILE_SIDE
        self.gathered = DEPTH * CORES
        self.summed = rows * self.wide

    def place(self, me):
        col = lax.rem(me, self.cols)
        core = lax.rem(col, CORES)
        rest = lax.div(col, CORES)
        return lax.div(me, self.cols), lax.rem(rest, self.wide), lax.div(rest, self.wide), core

    def col(self, z, y, core):
        return (z * self.wide + y) * CORES + core

    def number(self, x, y, z, core):
        return x * self.cols + self.col(z, y, core)

    def all_places(self):
        return [
            (x, y, z, core)
            for x in range(self.rows)
            for z in range(DEPTH)
            for y in range(self.wide)
            for core in range(CORES)
        ]

    def pairs(self, move):
        return [(self.number(*p), self.number(*move(*p))) for p in self.all_places()]


def gelu_exact(values):
    return 0.5 * values * (1.0 + lax.erf(values * 0.7071067811865476))


def gelu_slope(values):
    return (
        0.5 * (1.0 + lax.erf(values * 0.7071067811865476))
        + values * jnp.exp(-0.5 * values * values) * 0.3989422804014327
    )


def one_hot(index_row, size):
    places = lax.broadcasted_iota(i32, (size, index_row.shape[1]), 0)
    return jnp.where(places == index_row, 1.0, 0.0).astype(bf16)


def turned_times(values, table):
    return lax.dot_general(
        values.astype(f32).astype(bf16), table, TN, preferred_element_type=f32
    ).astype(i32)


def pack_kernel(grid, me_ref, *refs):
    hbm_refs, lists_ref, sent_refs, refs = refs[:4], refs[4], refs[5 : 5 + DEPTH], refs[5 + DEPTH :]
    counts_ref, vmem_refs, sem = refs[0], refs[1:5], refs[5]
    copies = [
        pltpu.make_async_copy(a, b, sem.at[n]) for n, (a, b) in enumerate(zip(hbm_refs, vmem_refs))
    ]
    for copy in copies:
        copy.start()
    for copy in copies:
        copy.wait()
    cols_ref, tile_counts_ref, pos_ref, keep_ref = vmem_refs
    rows, slots = pos_ref.shape
    slot = lax.broadcasted_iota(i32, (rows, slots), 1)
    tile_of = lax.broadcasted_iota(i32, (TPR, slots), 1) // EPT
    spread = jnp.where(tile_of == lax.broadcasted_iota(i32, (TPR, slots), 0), 1.0, 0.0)
    count = turned_times(tile_counts_ref[...], spread.astype(bf16))
    live = ((slot & (EPT - 1)) < count) & (keep_ref[...] == 1)
    pos = jnp.where(live, pos_ref[...], -1)
    lists_ref[:, :slots] = pos
    lane = lax.broadcasted_iota(i32, (TPR, TILE_SIDE), 1)
    k = lax.broadcasted_iota(i32, (TPR, TILE_SIDE), 0)
    lists_ref[:, slots:] = turned_times(cols_ref[...], jnp.where(lane == k, 1.0, 0.0).astype(bf16))
    target = lax.shift_right_arithmetic(pos, 7)
    ones = jnp.ones((8, slots), bf16)
    for t in range(rows):
        hot = one_hot(target[t : t + 1, :], TILE_SIDE)
        sums = lax.dot_general(ones, hot, NT, preferred_element_type=f32)
        counts_ref[t : t + 1, :] = sums[0:1, :].astype(i32)
    _, _, z, _ = grid.place(me_ref[0])
    plane = rows // DEPTH
    for dz, sent_ref in enumerate(sent_refs):
        at = pl.multiple_of((z ^ dz) * plane, 8)
        sent_ref[:, : slots + TILE_SIDE] = lists_ref[pl.ds(at, plane), :]
        for q in range(DEPTH):
            lanes = slice(slots + (q + 1) * TILE_SIDE, slots + (q + 2) * TILE_SIDE)
            sent_ref[:, lanes] = counts_ref[q * plane : (q + 1) * plane, :]


def plane_kernel(wide, *refs):
    got, both_ref = refs[:-1], refs[-1]
    plane = got[0].shape[0]
    for dz, ref in enumerate(got):
        both_ref[dz * plane : (dz + 1) * plane, :wide] = ref[:, :wide]
    for q in range(DEPTH):
        lanes = slice(wide + q * TILE_SIDE, wide + (q + 1) * TILE_SIDE)
        count = got[0][:, lanes]
        for ref in got[1:]:
            count = count + ref[:, lanes]
        both_ref[q * plane : (q + 1) * plane, wide:] = count


def chip_kernel(wide, lists_ref, own_ref, other_ref, chip_ref, counted_ref):
    rows = own_ref.shape[0]
    chip_ref[:rows, :] = own_ref[:, :wide]
    chip_ref[rows:, :] = other_ref[:, :wide]
    counted_ref[:, :wide] = lists_ref[...]
    counted_ref[:, wide:] = own_ref[:, wide:] + other_ref[:, wide:]


def add_kernel(*refs):
    total = refs[0][...]
    for ref in refs[1:-1]:
        total = total + ref[...]
    refs[-1][...] = total


def add_along_z_kernel(grid, me_ref, *refs):
    parts, (out_ref, placed_ref) = refs[:-2], refs[-2:]
    _, _, z, _ = grid.place(me_ref[0])
    for dz, ref in enumerate(parts):
        placed_ref[z ^ dz] = ref[...]
    total = placed_ref[0]
    for n in range(1, DEPTH):
        total = total + placed_ref[n]
    out_ref[...] = total


def slot_columns(columns, first, slots):
    tile = lax.broadcasted_iota(i32, (1, slots), 1) // EPT
    spread = jnp.broadcast_to(columns[:, first : first + 1], (1, slots))
    for k in range(1, TPR):
        spread = jnp.where(tile == k, columns[:, first + k : first + k + 1], spread)
    return spread


def split_values(grid, values, both_ref, scale_of=None):
    width = values[0].shape[1]
    for g, ref in enumerate(values):
        value = ref[...]
        if scale_of is not None:
            value = value * scale_of(g)
        high = value.astype(bf16)
        rows = slice(g * grid.group, (g + 1) * grid.group)
        both_ref[rows, :width] = high
        both_ref[rows, width:] = (value - high.astype(f32)).astype(bf16)


def forward_block_kernel(grid, slots, me_ref, *refs):
    chip_refs, refs = refs[: grid.rows], refs[grid.rows :]
    counted_refs, (block_ref, root_ref, lists_ref) = refs[: grid.wide], refs[grid.wide :]
    step = pl.program_id(0)
    x, y, _, core = grid.place(me_ref[0])
    wide = slots + TILE_SIDE
    rows = counted_refs[0].shape[0]

    @pl.when(step == 0)
    def _():
        count = sum(ref[:, wide:] for ref in counted_refs)
        root_ref[...] = lax.rsqrt(1.0 + count.astype(f32))
        for n, ref in enumerate(chip_refs):
            lists_ref[n] = ref[...]

    dx, dy = lax.rem(step, grid.rows), lax.div(step, grid.rows)
    to_y = lax.rem(y + dy, grid.wide)
    plane = grid.wide * CORES * grid.per
    for g in range(grid.gathered):
        for s in range(grid.per):
            at = (g % CORES) * rows + (g // CORES) * plane + (to_y * CORES + core) * grid.per + s
            row = lists_ref[dx, pl.ds(at, 1), :]
            pos = row[:, :slots]
            target = lax.shift_right_arithmetic(pos, 7)
            source = slot_columns(row[:, slots:], 0, slots) * TILE_SIDE + (pos & (TILE_SIDE - 1))
            hot = lax.dot_general(
                one_hot(target, TILE_SIDE),
                one_hot(source - x * grid.group, grid.group),
                NT,
                preferred_element_type=f32,
            )
            block_ref[
                s * TILE_SIDE : (s + 1) * TILE_SIDE, g * grid.group : (g + 1) * grid.group
            ] = hot.astype(bf16)


def forward_sum_kernel(grid, me_ref, root_ref, block_ref, *refs):
    values, (scale_ref, *outs, both_ref) = refs[: grid.gathered], refs[grid.gathered :]
    width = values[0].shape[1]
    step = pl.program_id(0)

    @pl.when(step == 0)
    def _():
        _, y, z, core = grid.place(me_ref[0])

        def scale_of(g):
            at = grid.col(z ^ (g // CORES), y, core ^ (g % CORES)) * grid.per
            return spread_down([root_ref[pl.ds(at + s, 1), :] for s in range(grid.per)])

        scale_ref[...] = scale_of(0)
        split_values(grid, values, both_ref, scale_of)

    part = jnp.dot(block_ref[...], both_ref[...], preferred_element_type=f32)
    total = part[:, :width] + part[:, width:]
    for k, out_ref in enumerate(outs):

        @pl.when(step == k)
        def _(out_ref=out_ref):
            out_ref[...] = total


def backward_block_kernel(grid, slots, me_ref, *refs):
    lists, block_ref = refs[:-1], refs[-1]
    g = pl.program_id(0)
    x, y, z, core = grid.place(me_ref[0])
    col = grid.col(z ^ lax.div(g, CORES), y, core ^ lax.rem(g, CORES))
    side = grid.rows * grid.group
    for k, list_ref in enumerate(lists):
        for s in range(grid.per):
            row = list_ref[pl.ds(col * grid.per + s, 1), :]
            pos = row[:, :slots]
            target = lax.shift_right_arithmetic(pos, 7)
            source = slot_columns(row[:, slots:], 0, slots) * TILE_SIDE + (pos & (TILE_SIDE - 1))
            hot = lax.dot_general(
                one_hot(source, side), one_hot(target, TILE_SIDE), NT, preferred_element_type=f32
            )
            block_ref[k * side : (k + 1) * side, s * TILE_SIDE : (s + 1) * TILE_SIDE] = hot.astype(
                bf16
            )


def spread_down(rows):
    return jnp.concatenate(
        [jnp.broadcast_to(row, (TILE_SIDE, TILE_SIDE)).T for row in rows], axis=0
    )


def backward_sum_kernel(grid, me_ref, block_ref, *refs):
    values, (*outs, both_ref) = refs[: grid.gathered], refs[grid.gathered :]
    width = values[0].shape[1]
    step = pl.program_id(0)

    @pl.when(step == 0)
    def _():
        split_values(grid, values, both_ref)

    part = jnp.dot(block_ref[...], both_ref[...], preferred_element_type=f32)
    total = part[:, :width] + part[:, width:]
    for k, out_ref in enumerate(outs):

        @pl.when(step == k)
        def _(out_ref=out_ref):
            out_ref[...] = total


def finish_kernel(grid, me_ref, scale_ref, sent_ref, *refs):
    sums, refs = refs[: grid.summed], refs[grid.summed :]
    parts, (features_grad_ref, weight_grad_ref, parts_ref) = refs[:-3], refs[-3:]
    x, y, z, core = grid.place(me_ref[0])
    total = sent_ref[...]
    for ref in sums:
        total = total + ref[...]
    features_grad_ref[...] = scale_ref[...] * total
    for k, ref in enumerate(parts):
        from_x = lax.rem(x + grid.rows - k % grid.rows, grid.rows)
        from_y = lax.rem(y + grid.wide - k // grid.rows, grid.wide)
        parts_ref[from_y * grid.rows + from_x] = ref[...]
    high = parts_ref.shape[1] // 2
    for n in range(grid.summed):
        part = parts_ref[n]
        weight_grad_ref[n * high : (n + 1) * high, :] = jnp.concatenate(
            [part[:high, :], part[high:, :]], axis=1
        )


def middle_kernel(
    grid,
    me_ref,
    scale_ref,
    features_ref,
    weight_ref,
    bias_ref,
    cotangent_ref,
    drop_ref,
    *refs,
):
    sums, refs = refs[: grid.summed], refs[grid.summed :]
    hidden_ref, sent_ref, *part_refs, parts_ref = refs
    x, y, _, _ = grid.place(me_ref[0])
    scale = scale_ref[...]
    total = scale * features_ref[...]
    for ref in sums:
        total = total + ref[...]
    mixed = scale * total
    weight = weight_ref[...]
    pre_act = jnp.dot(mixed, weight, precision=highest, preferred_element_type=f32) + bias_ref[...]
    dropout = drop_ref[...].astype(f32) / KEEP_RATE
    hidden_ref[...] = gelu_exact(pre_act) * dropout
    grad_pre = cotangent_ref[...] * dropout * gelu_slope(pre_act)
    sent_ref[...] = scale * lax.dot_general(
        grad_pre, weight, NT, precision=highest, preferred_element_type=f32
    )
    weight_grad = lax.dot_general(
        mixed, grad_pre, TN, precision=highest, preferred_element_type=f32
    )
    width = features_ref.shape[1]
    high = width // grid.summed
    for n in range(grid.summed):
        part = weight_grad[n * high : (n + 1) * high, :]
        parts_ref[n] = jnp.concatenate([part[:, :width], part[:, width:]], axis=0)
    for k, part_ref in enumerate(part_refs):
        to_x = lax.rem(x + k % grid.rows, grid.rows)
        to_y = lax.rem(y + k // grid.rows, grid.wide)
        part_ref[...] = parts_ref[to_y * grid.rows + to_x]


def shards(
    features,
    weight,
    out_bias,
    cotangent,
    drop_keep,
    tile_cols,
    tile_edge_counts,
    edge_pos,
    edge_keep_bits,
):
    group, width = features.shape
    hidden = weight.shape[1]
    rows, slots = edge_pos.shape[2:]
    grid = Grid(lax.axis_size("row"), lax.axis_size("col"), group)
    both_axes = ("row", "col")
    me = lax.axis_index(both_axes).astype(i32)[None]
    smem = pl.BlockSpec(memory_space=pltpu.SMEM)
    vmem = pl.BlockSpec(memory_space=pltpu.VMEM)
    limit = pltpu.CompilerParams(vmem_limit_bytes=24 * MIB)

    def toward(dz):
        return grid.pairs(lambda x, y, z, c: (x, y, z ^ dz, c))

    def along_z(blocks):
        return [blocks[0]] + [
            lax.ppermute(blocks[dz], both_axes, toward(dz)) for dz in range(1, DEPTH)
        ]

    def to_core(block):
        return lax.ppermute(block, both_axes, grid.pairs(lambda x, y, z, c: (x, y, z, c ^ 1)))

    def to_cores(blocks):
        return [block for own in blocks for block in (own, to_core(own))]

    def backward_row(k, me_ref):
        x, _, _, _ = grid.place(me_ref[0])
        to_x = lax.rem(x + lax.rem(k, grid.rows), grid.rows)
        return lax.div(k, grid.rows) * grid.rows + to_x

    sum_order = [(dx, dy) for dy in range(grid.wide) for dx in range(grid.rows)]

    def to_owners(sums):
        got = [sums[0]]
        for part, (dx, dy) in list(zip(sums, sum_order))[1:]:
            got.append(
                lax.ppermute(
                    part,
                    both_axes,
                    grid.pairs(
                        lambda x, y, z, c, dx=dx, dy=dy: (
                            (x + dx) % grid.rows,
                            (y + dy) % grid.wide,
                            z,
                            c,
                        )
                    ),
                )
            )
        return got

    wide = slots + TILE_SIDE
    plane = rows // DEPTH
    raw = [tile_cols[0, 0].T, tile_edge_counts[0, 0].T, edge_pos[0, 0], edge_keep_bits[0, 0]]
    lists, *planes = pl.pallas_call(
        functools.partial(pack_kernel, grid),
        in_specs=[smem] + [pl.BlockSpec(memory_space=pltpu.HBM)] * 4,
        out_shape=(jax.ShapeDtypeStruct((rows, wide), i32),)
        + (jax.ShapeDtypeStruct((plane, wide + DEPTH * TILE_SIDE), i32),) * DEPTH,
        scratch_shapes=[pltpu.VMEM((rows, TILE_SIDE), i32)]
        + [pltpu.VMEM(a.shape, i32) for a in raw]
        + [pltpu.SemaphoreType.DMA((4,))],
        compiler_params=pltpu.CompilerParams(vmem_limit_bytes=60 * MIB),
        cost_estimate=pl.CostEstimate(flops=2**31, bytes_accessed=2**23, transcendentals=0),
        name="pack",
    )(me, *raw)

    def from_peer(value, move):
        return lax.ppermute(value, both_axes, [(b, a) for a, b in grid.pairs(move)])

    along = [features] + [lax.ppermute(features, both_axes, toward(dz)) for dz in (1, 2)]
    across = [to_core(features)]
    *planes, across[0] = lax.optimization_barrier((*planes, across[0]))
    got_planes = along_z(planes)
    merged = lax.optimization_barrier((*along, *got_planes))
    along, got_planes = list(merged[: len(along)]), merged[len(along) :]
    small = pl.CostEstimate(flops=2**14, bytes_accessed=2**18, transcendentals=0)
    both = pl.pallas_call(
        functools.partial(plane_kernel, wide),
        out_shape=jax.ShapeDtypeStruct((rows, wide + TILE_SIDE), i32),
        compiler_params=limit,
        cost_estimate=small,
        name="plane",
    )(*got_planes)
    chip, counted = pl.pallas_call(
        functools.partial(chip_kernel, wide),
        out_shape=(
            jax.ShapeDtypeStruct((CORES * rows, wide), i32),
            jax.ShapeDtypeStruct((rows, wide + TILE_SIDE), i32),
        ),
        compiler_params=limit,
        cost_estimate=small,
        name="chip",
    )(lists, both, from_peer(both, lambda x, y, z, c: (x, y, z, c ^ 1)))
    across.append(to_core(along[1]))
    chip, later, across[1] = lax.optimization_barrier((chip, features, across[1]))
    along += [lax.ppermute(later, both_axes, toward(dz)) for dz in range(3, DEPTH)]
    chips = [chip] + [
        from_peer(chip, lambda x, y, z, c, dx=dx: ((x + dx) % grid.rows, y, z, c))
        for dx in range(1, grid.rows)
    ]
    peer_lists = [counted] + [
        from_peer(counted, lambda x, y, z, c, dy=dy: (x, (y + dy) % grid.wide, z, c))
        for dy in range(1, grid.wide)
    ]
    side, depth = grid.summed * group, grid.gathered * group

    formation = pl.CostEstimate(
        flops=2 * rows * slots * TILE_SIDE * grid.rows * group,
        bytes_accessed=2 * side * depth,
        transcendentals=0,
    )
    product = pl.CostEstimate(
        flops=4 * side * depth * width, bytes_accessed=2 * side * depth, transcendentals=0
    )

    def whole(*shape):
        return pl.BlockSpec(shape, lambda k: (0,) * len(shape))

    forward_block, roots = pl.pallas_call(
        functools.partial(forward_block_kernel, grid, slots),
        grid=(grid.summed,),
        in_specs=[smem]
        + [whole(CORES * rows, wide)] * grid.rows
        + [whole(rows, wide + TILE_SIDE)] * grid.wide,
        out_specs=(pl.BlockSpec((group, depth), lambda k: (k, 0)), whole(rows, TILE_SIDE)),
        out_shape=(
            jax.ShapeDtypeStruct((side, depth), bf16),
            jax.ShapeDtypeStruct((rows, TILE_SIDE), f32),
        ),
        scratch_shapes=[pltpu.VMEM((grid.rows, CORES * rows, wide), i32)],
        compiler_params=limit,
        cost_estimate=pl.CostEstimate(flops=2**16, bytes_accessed=2**16, transcendentals=0),
        name="forward_block",
    )(me, *chips, *peer_lists)
    along[-1], forward_block = lax.optimization_barrier((along[-1], forward_block))
    across += [to_core(block) for block in along[2:]]
    gathered = [block for pair in zip(along, across) for block in pair]
    scale, *sums = pl.pallas_call(
        functools.partial(forward_sum_kernel, grid),
        grid=(grid.summed,),
        in_specs=[smem, whole(rows, TILE_SIDE), pl.BlockSpec((group, depth), lambda k: (k, 0))]
        + [whole(group, width)] * grid.gathered,
        out_specs=(whole(group, width),) * (1 + grid.summed),
        out_shape=(jax.ShapeDtypeStruct((group, width), f32),) * (1 + grid.summed),
        scratch_shapes=[pltpu.VMEM((depth, 2 * width), bf16)],
        compiler_params=limit,
        cost_estimate=product,
        name="forward_sum",
    )(me, roots, forward_block, *gathered)
    *peer_lists, sums[0] = lax.optimization_barrier((*peer_lists, sums[0]))
    backward_block = pl.pallas_call(
        functools.partial(backward_block_kernel, grid, slots),
        grid=(grid.gathered,),
        in_specs=[smem] + [pl.BlockSpec((rows, wide + TILE_SIDE), lambda g: (0, 0))] * grid.wide,
        out_specs=pl.BlockSpec((side, group), lambda g: (0, g)),
        out_shape=jax.ShapeDtypeStruct((side, depth), bf16),
        compiler_params=limit,
        cost_estimate=formation,
        name="backward_block",
    )(me, *peer_lists)
    sums = to_owners(sums)
    sums[-1], backward_block = lax.optimization_barrier((sums[-1], backward_block))

    part_shape = jax.ShapeDtypeStruct((width // grid.summed * 2, width), f32)
    hidden_out, sent, *parts = pl.pallas_call(
        functools.partial(middle_kernel, grid),
        in_specs=[smem] + [vmem] * (6 + grid.summed),
        out_shape=(
            jax.ShapeDtypeStruct((group, hidden), f32),
            jax.ShapeDtypeStruct((group, width), f32),
        )
        + (part_shape,) * grid.summed,
        scratch_shapes=[pltpu.VMEM((grid.summed, *part_shape.shape), f32)],
        compiler_params=limit,
        cost_estimate=pl.CostEstimate(
            flops=36 * group * width * hidden, bytes_accessed=2**20, transcendentals=2**18
        ),
        name="middle",
    )(me, scale, features, weight, out_bias.reshape(1, hidden), cotangent, drop_keep, *sums)

    along = along_z([sent] * DEPTH)
    share = pl.pallas_call(
        add_kernel,
        out_shape=part_shape,
        compiler_params=limit,
        cost_estimate=small,
        name="add_parts",
    )(*to_owners(parts))
    along[-1], share = lax.optimization_barrier((along[-1], share))
    over_z = along_z([share] * DEPTH)
    collected = to_cores(along)
    sums = pl.pallas_call(
        functools.partial(backward_sum_kernel, grid),
        grid_spec=pltpu.PrefetchScalarGridSpec(
            num_scalar_prefetch=1,
            grid=(grid.summed,),
            in_specs=[pl.BlockSpec((group, depth), lambda k, me_ref: (backward_row(k, me_ref), 0))]
            + [pl.BlockSpec((group, width), lambda k, me_ref: (0, 0))] * grid.gathered,
            out_specs=(pl.BlockSpec((group, width), lambda k, me_ref: (0, 0)),) * grid.summed,
            scratch_shapes=[pltpu.VMEM((depth, 2 * width), bf16)],
        ),
        out_shape=(jax.ShapeDtypeStruct((group, width), f32),) * grid.summed,
        compiler_params=limit,
        cost_estimate=product,
        name="backward_sum",
    )(me, backward_block, *collected)
    first, *over_z = lax.optimization_barrier((sums[0], *over_z))
    sums = [first, *sums[1:]]
    share = pl.pallas_call(
        functools.partial(add_along_z_kernel, grid),
        in_specs=[smem] + [vmem] * DEPTH,
        out_shape=part_shape,
        scratch_shapes=[pltpu.VMEM((DEPTH, *part_shape.shape), f32)],
        compiler_params=limit,
        cost_estimate=small,
        name="add_along_z",
    )(me, *over_z)
    shares = [share, from_peer(share, lambda x, y, z, c: (x, y, z, c ^ 1))]
    share = pl.pallas_call(
        add_kernel,
        out_shape=part_shape,
        compiler_params=limit,
        cost_estimate=small,
        name="add_cores",
    )(*shares)
    sums = to_owners(sums)
    parts = to_owners([share] * grid.summed)
    grad_features, grad_weight = pl.pallas_call(
        functools.partial(finish_kernel, grid),
        in_specs=[smem] + [vmem] * (2 + 2 * grid.summed),
        out_shape=(
            jax.ShapeDtypeStruct((group, width), f32),
            jax.ShapeDtypeStruct((width, hidden), f32),
        ),
        scratch_shapes=[pltpu.VMEM((grid.summed, *part_shape.shape), f32)],
        compiler_params=limit,
        cost_estimate=pl.CostEstimate(flops=2**18, bytes_accessed=2**19, transcendentals=0),
        name="finish",
    )(me, scale, sent, *sums, *parts)
    return (hidden_out, grad_features, grad_weight)


def solution(mesh):
    in_specs = (
        P(("row", "col"), None),
        P(),
        P(),
        P(("row", "col"), None),
        P(("row", "col"), None),
        P("row", "col", None, None),
        P("row", "col", None, None),
        P("row", "col", None, None),
        P("row", "col", None, None),
    )
    out_specs = (P(("row", "col"), None), P(("row", "col"), None), P())
    return jax.shard_map(shards, mesh=mesh, in_specs=in_specs, out_specs=out_specs, check_vma=False)
```

```python
import functools

import jax
import jax.numpy as jnp
from jax import lax
from jax.experimental import pallas as pl
from jax.experimental.pallas import tpu as pltpu
from jax.sharding import PartitionSpec as P

TILE_SIDE = 128
TPR = 4
EPT = 64
KEEP_RATE = 0.9
CORES = 2
DEPTH = 4

f32 = jnp.float32
bf16 = jnp.bfloat16
i32 = jnp.int32
highest = lax.Precision.HIGHEST
NT = (((1,), (1,)), ((), ()))
TN = (((0,), (0,)), ((), ()))
MIB = 1 << 20


class Grid:
    def __init__(self, rows, cols, group):
        self.rows, self.cols, self.group = rows, cols, group
        self.wide = cols // (DEPTH * CORES)
        self.count = rows * cols
        self.per = group // TILE_SIDE
        self.gathered = DEPTH * CORES
        self.summed = rows * self.wide

    def place(self, me):
        col = lax.rem(me, self.cols)
        core = lax.rem(col, CORES)
        rest = lax.div(col, CORES)
        return lax.div(me, self.cols), lax.rem(rest, self.wide), lax.div(rest, self.wide), core

    def col(self, z, y, core):
        return (z * self.wide + y) * CORES + core

    def number(self, x, y, z, core):
        return x * self.cols + self.col(z, y, core)

    def all_places(self):
        return [
            (x, y, z, core)
            for x in range(self.rows)
            for z in range(DEPTH)
            for y in range(self.wide)
            for core in range(CORES)
        ]

    def pairs(self, move):
        return [(self.number(*p), self.number(*move(*p))) for p in self.all_places()]


def gelu_exact(values):
    return 0.5 * values * (1.0 + lax.erf(values * 0.7071067811865476))


def gelu_slope(values):
    return (
        0.5 * (1.0 + lax.erf(values * 0.7071067811865476))
        + values * jnp.exp(-0.5 * values * values) * 0.3989422804014327
    )


def one_hot(index_row, size):
    places = lax.broadcasted_iota(i32, (size, index_row.shape[1]), 0)
    return jnp.where(places == index_row, 1.0, 0.0).astype(bf16)


def turned_times(values, table):
    return lax.dot_general(
        values.astype(f32).astype(bf16), table, TN, preferred_element_type=f32
    ).astype(i32)


def pack_kernel(grid, me_ref, *refs):
    hbm_refs, lists_ref, sent_refs, refs = refs[:4], refs[4], refs[5 : 5 + DEPTH], refs[5 + DEPTH :]
    counts_ref, vmem_refs, sem = refs[0], refs[1:5], refs[5]
    copies = [
        pltpu.make_async_copy(a, b, sem.at[n]) for n, (a, b) in enumerate(zip(hbm_refs, vmem_refs))
    ]
    for copy in copies:
        copy.start()
    for copy in copies:
        copy.wait()
    cols_ref, tile_counts_ref, pos_ref, keep_ref = vmem_refs
    rows, slots = pos_ref.shape
    slot = lax.broadcasted_iota(i32, (rows, slots), 1)
    tile_of = lax.broadcasted_iota(i32, (TPR, slots), 1) // EPT
    spread = jnp.where(tile_of == lax.broadcasted_iota(i32, (TPR, slots), 0), 1.0, 0.0)
    count = turned_times(tile_counts_ref[...], spread.astype(bf16))
    live = ((slot & (EPT - 1)) < count) & (keep_ref[...] == 1)
    pos = jnp.where(live, pos_ref[...], -1)
    lists_ref[:, :slots] = pos
    lane = lax.broadcasted_iota(i32, (TPR, TILE_SIDE), 1)
    k = lax.broadcasted_iota(i32, (TPR, TILE_SIDE), 0)
    lists_ref[:, slots:] = turned_times(cols_ref[...], jnp.where(lane == k, 1.0, 0.0).astype(bf16))
    target = lax.shift_right_arithmetic(pos, 7)
    ones = jnp.ones((8, slots), bf16)
    for t in range(rows):
        hot = one_hot(target[t : t + 1, :], TILE_SIDE)
        sums = lax.dot_general(ones, hot, NT, preferred_element_type=f32)
        counts_ref[t : t + 1, :] = sums[0:1, :].astype(i32)
    _, _, z, _ = grid.place(me_ref[0])
    plane = rows // DEPTH
    for dz, sent_ref in enumerate(sent_refs):
        at = pl.multiple_of((z ^ dz) * plane, 8)
        sent_ref[:, : slots + TILE_SIDE] = lists_ref[pl.ds(at, plane), :]
        for q in range(DEPTH):
            lanes = slice(slots + (q + 1) * TILE_SIDE, slots + (q + 2) * TILE_SIDE)
            sent_ref[:, lanes] = counts_ref[q * plane : (q + 1) * plane, :]


def plane_kernel(wide, *refs):
    got, both_ref = refs[:-1], refs[-1]
    plane = got[0].shape[0]
    for dz, ref in enumerate(got):
        both_ref[dz * plane : (dz + 1) * plane, :wide] = ref[:, :wide]
    for q in range(DEPTH):
        lanes = slice(wide + q * TILE_SIDE, wide + (q + 1) * TILE_SIDE)
        count = got[0][:, lanes]
        for ref in got[1:]:
            count = count + ref[:, lanes]
        both_ref[q * plane : (q + 1) * plane, wide:] = count


def keep_kernel(*refs):
    half = len(refs) // 2
    for ref, kept_ref in zip(refs[:half], refs[half:]):
        kept_ref[...] = ref[...]


def chip_kernel(wide, lists_ref, own_ref, other_ref, chip_ref, counted_ref):
    rows = own_ref.shape[0]
    chip_ref[:rows, :] = own_ref[:, :wide]
    chip_ref[rows:, :] = other_ref[:, :wide]
    counted_ref[:, :wide] = lists_ref[...]
    counted_ref[:, wide:] = own_ref[:, wide:] + other_ref[:, wide:]


def add_kernel(*refs):
    total = refs[0][...]
    for ref in refs[1:-1]:
        total = total + ref[...]
    refs[-1][...] = total


def add_along_z_kernel(grid, me_ref, *refs):
    parts, (out_ref, placed_ref) = refs[:-2], refs[-2:]
    _, _, z, _ = grid.place(me_ref[0])
    for dz, ref in enumerate(parts):
        placed_ref[z ^ dz] = ref[...]
    total = placed_ref[0]
    for n in range(1, DEPTH):
        total = total + placed_ref[n]
    out_ref[...] = total


def slot_columns(columns, first, slots):
    tile = lax.broadcasted_iota(i32, (1, slots), 1) // EPT
    spread = jnp.broadcast_to(columns[:, first : first + 1], (1, slots))
    for k in range(1, TPR):
        spread = jnp.where(tile == k, columns[:, first + k : first + k + 1], spread)
    return spread


def split_values(grid, values, both_ref, scale_of=None):
    width = values[0].shape[1]
    for g, ref in enumerate(values):
        value = ref[...]
        if scale_of is not None:
            value = value * scale_of(g)
        high = value.astype(bf16)
        rows = slice(g * grid.group, (g + 1) * grid.group)
        both_ref[rows, :width] = high
        both_ref[rows, width:] = (value - high.astype(f32)).astype(bf16)


def forward_block_kernel(grid, slots, me_ref, *refs):
    chip_refs, refs = refs[: grid.rows], refs[grid.rows :]
    counted_refs, (block_ref, root_ref, lists_ref) = refs[: grid.wide], refs[grid.wide :]
    step = pl.program_id(0)
    x, y, _, core = grid.place(me_ref[0])
    wide = slots + TILE_SIDE
    rows = counted_refs[0].shape[0]

    @pl.when(step == 0)
    def _():
        count = sum(ref[:, wide:] for ref in counted_refs)
        root_ref[...] = lax.rsqrt(1.0 + count.astype(f32))
        for n, ref in enumerate(chip_refs):
            lists_ref[n] = ref[...]

    dx, dy = lax.rem(step, grid.rows), lax.div(step, grid.rows)
    to_y = lax.rem(y + dy, grid.wide)
    plane = grid.wide * CORES * grid.per
    for g in range(grid.gathered):
        for s in range(grid.per):
            at = (g % CORES) * rows + (g // CORES) * plane + (to_y * CORES + core) * grid.per + s
            row = lists_ref[dx, pl.ds(at, 1), :]
            pos = row[:, :slots]
            target = lax.shift_right_arithmetic(pos, 7)
            source = slot_columns(row[:, slots:], 0, slots) * TILE_SIDE + (pos & (TILE_SIDE - 1))
            hot = lax.dot_general(
                one_hot(target, TILE_SIDE),
                one_hot(source - x * grid.group, grid.group),
                NT,
                preferred_element_type=f32,
            )
            block_ref[
                s * TILE_SIDE : (s + 1) * TILE_SIDE, g * grid.group : (g + 1) * grid.group
            ] = hot.astype(bf16)


def forward_sum_kernel(grid, me_ref, root_ref, block_ref, *refs):
    values, (scale_ref, *outs, both_ref) = refs[: grid.gathered], refs[grid.gathered :]
    width = values[0].shape[1]
    step = pl.program_id(0)

    @pl.when(step == 0)
    def _():
        _, y, z, core = grid.place(me_ref[0])

        def scale_of(g):
            at = grid.col(z ^ (g // CORES), y, core ^ (g % CORES)) * grid.per
            return spread_down([root_ref[pl.ds(at + s, 1), :] for s in range(grid.per)])

        scale_ref[...] = scale_of(0)
        split_values(grid, values, both_ref, scale_of)

    part = jnp.dot(block_ref[...], both_ref[...], preferred_element_type=f32)
    total = part[:, :width] + part[:, width:]
    for k, out_ref in enumerate(outs):

        @pl.when(step == k)
        def _(out_ref=out_ref):
            out_ref[...] = total


def backward_block_kernel(grid, slots, me_ref, *refs):
    lists, block_ref = refs[:-1], refs[-1]
    g = pl.program_id(0)
    x, y, z, core = grid.place(me_ref[0])
    col = grid.col(z ^ lax.div(g, CORES), y, core ^ lax.rem(g, CORES))
    side = grid.rows * grid.group
    for k, list_ref in enumerate(lists):
        for s in range(grid.per):
            row = list_ref[pl.ds(col * grid.per + s, 1), :]
            pos = row[:, :slots]
            target = lax.shift_right_arithmetic(pos, 7)
            source = slot_columns(row[:, slots:], 0, slots) * TILE_SIDE + (pos & (TILE_SIDE - 1))
            hot = lax.dot_general(
                one_hot(source, side), one_hot(target, TILE_SIDE), NT, preferred_element_type=f32
            )
            block_ref[k * side : (k + 1) * side, s * TILE_SIDE : (s + 1) * TILE_SIDE] = hot.astype(
                bf16
            )


def spread_down(rows):
    return jnp.concatenate(
        [jnp.broadcast_to(row, (TILE_SIDE, TILE_SIDE)).T for row in rows], axis=0
    )


def backward_sum_kernel(grid, me_ref, block_ref, *refs):
    values, (*outs, both_ref) = refs[: grid.gathered], refs[grid.gathered :]
    width = values[0].shape[1]
    step = pl.program_id(0)

    @pl.when(step == 0)
    def _():
        split_values(grid, values, both_ref)

    part = jnp.dot(block_ref[...], both_ref[...], preferred_element_type=f32)
    total = part[:, :width] + part[:, width:]
    for k, out_ref in enumerate(outs):

        @pl.when(step == k)
        def _(out_ref=out_ref):
            out_ref[...] = total


def finish_kernel(grid, me_ref, scale_ref, sent_ref, *refs):
    sums, refs = refs[: grid.summed], refs[grid.summed :]
    parts, (features_grad_ref, weight_grad_ref, parts_ref) = refs[:-3], refs[-3:]
    x, y, z, core = grid.place(me_ref[0])
    total = sent_ref[...]
    for ref in sums:
        total = total + ref[...]
    features_grad_ref[...] = scale_ref[...] * total
    for k, ref in enumerate(parts):
        from_x = lax.rem(x + grid.rows - k % grid.rows, grid.rows)
        from_y = lax.rem(y + grid.wide - k // grid.rows, grid.wide)
        parts_ref[from_y * grid.rows + from_x] = ref[...]
    high = parts_ref.shape[1] // 2
    for n in range(grid.summed):
        part = parts_ref[n]
        weight_grad_ref[n * high : (n + 1) * high, :] = jnp.concatenate(
            [part[:high, :], part[high:, :]], axis=1
        )


def middle_kernel(
    grid,
    me_ref,
    scale_ref,
    features_ref,
    weight_ref,
    bias_ref,
    cotangent_ref,
    drop_ref,
    *refs,
):
    sums, refs = refs[: grid.summed], refs[grid.summed :]
    hidden_ref, sent_ref, *part_refs, parts_ref = refs
    x, y, _, _ = grid.place(me_ref[0])
    scale = scale_ref[...]
    total = scale * features_ref[...]
    for ref in sums:
        total = total + ref[...]
    mixed = scale * total
    weight = weight_ref[...]
    pre_act = jnp.dot(mixed, weight, precision=highest, preferred_element_type=f32) + bias_ref[...]
    dropout = drop_ref[...].astype(f32) / KEEP_RATE
    hidden_ref[...] = gelu_exact(pre_act) * dropout
    grad_pre = cotangent_ref[...] * dropout * gelu_slope(pre_act)
    sent_ref[...] = scale * lax.dot_general(
        grad_pre, weight, NT, precision=highest, preferred_element_type=f32
    )
    weight_grad = lax.dot_general(
        mixed, grad_pre, TN, precision=highest, preferred_element_type=f32
    )
    width = features_ref.shape[1]
    high = width // grid.summed
    for n in range(grid.summed):
        part = weight_grad[n * high : (n + 1) * high, :]
        parts_ref[n] = jnp.concatenate([part[:, :width], part[:, width:]], axis=0)
    for k, part_ref in enumerate(part_refs):
        to_x = lax.rem(x + k % grid.rows, grid.rows)
        to_y = lax.rem(y + k // grid.rows, grid.wide)
        part_ref[...] = parts_ref[to_y * grid.rows + to_x]


def shards(
    features,
    weight,
    out_bias,
    cotangent,
    drop_keep,
    tile_cols,
    tile_edge_counts,
    edge_pos,
    edge_keep_bits,
):
    group, width = features.shape
    hidden = weight.shape[1]
    rows, slots = edge_pos.shape[2:]
    grid = Grid(lax.axis_size("row"), lax.axis_size("col"), group)
    both_axes = ("row", "col")
    me = lax.axis_index(both_axes).astype(i32)[None]
    smem = pl.BlockSpec(memory_space=pltpu.SMEM)
    vmem = pl.BlockSpec(memory_space=pltpu.VMEM)
    limit = pltpu.CompilerParams(vmem_limit_bytes=24 * MIB)

    def toward(dz):
        return grid.pairs(lambda x, y, z, c: (x, y, z ^ dz, c))

    def along_z(blocks):
        return [blocks[0]] + [
            lax.ppermute(blocks[dz], both_axes, toward(dz)) for dz in range(1, DEPTH)
        ]

    def to_cores(blocks):
        others = [
            lax.ppermute(block, both_axes, grid.pairs(lambda x, y, z, c: (x, y, z, c ^ 1)))
            for block in blocks
        ]
        return [block for pair in zip(blocks, others) for block in pair]

    def backward_row(k, me_ref):
        x, _, _, _ = grid.place(me_ref[0])
        to_x = lax.rem(x + lax.rem(k, grid.rows), grid.rows)
        return lax.div(k, grid.rows) * grid.rows + to_x

    sum_order = [(dx, dy) for dy in range(grid.wide) for dx in range(grid.rows)]

    def to_owners(sums):
        got = [sums[0]]
        for part, (dx, dy) in list(zip(sums, sum_order))[1:]:
            got.append(
                lax.ppermute(
                    part,
                    both_axes,
                    grid.pairs(
                        lambda x, y, z, c, dx=dx, dy=dy: (
                            (x + dx) % grid.rows,
                            (y + dy) % grid.wide,
                            z,
                            c,
                        )
                    ),
                )
            )
        return got

    wide = slots + TILE_SIDE
    plane = rows // DEPTH
    raw = [tile_cols[0, 0].T, tile_edge_counts[0, 0].T, edge_pos[0, 0], edge_keep_bits[0, 0]]
    lists, *planes = pl.pallas_call(
        functools.partial(pack_kernel, grid),
        in_specs=[smem] + [pl.BlockSpec(memory_space=pltpu.HBM)] * 4,
        out_shape=(jax.ShapeDtypeStruct((rows, wide), i32),)
        + (jax.ShapeDtypeStruct((plane, wide + DEPTH * TILE_SIDE), i32),) * DEPTH,
        scratch_shapes=[pltpu.VMEM((rows, TILE_SIDE), i32)]
        + [pltpu.VMEM(a.shape, i32) for a in raw]
        + [pltpu.SemaphoreType.DMA((4,))],
        compiler_params=pltpu.CompilerParams(vmem_limit_bytes=60 * MIB),
        cost_estimate=pl.CostEstimate(flops=2**31, bytes_accessed=2**23, transcendentals=0),
        name="pack",
    )(me, *raw)

    def from_peer(value, move):
        return lax.ppermute(value, both_axes, [(b, a) for a, b in grid.pairs(move)])

    along = [features] + [lax.ppermute(features, both_axes, toward(dz)) for dz in (1, 2)]
    got_planes = along_z(planes)
    lists, got_planes[0] = pl.pallas_call(
        keep_kernel,
        out_shape=tuple(jax.ShapeDtypeStruct(a.shape, i32) for a in (lists, planes[0])),
        compiler_params=limit,
        cost_estimate=pl.CostEstimate(flops=2**21, bytes_accessed=2**20, transcendentals=0),
        name="keep",
    )(lists, planes[0])
    *along, lists, got_planes[0] = lax.optimization_barrier((*along, lists, got_planes[0]))
    *got_planes, later = lax.optimization_barrier((*got_planes, features))
    along += [lax.ppermute(later, both_axes, toward(dz)) for dz in range(3, DEPTH)]
    small = pl.CostEstimate(flops=2**14, bytes_accessed=2**18, transcendentals=0)
    both = pl.pallas_call(
        functools.partial(plane_kernel, wide),
        out_shape=jax.ShapeDtypeStruct((rows, wide + TILE_SIDE), i32),
        compiler_params=limit,
        cost_estimate=small,
        name="plane",
    )(*got_planes)
    chip, counted = pl.pallas_call(
        functools.partial(chip_kernel, wide),
        out_shape=(
            jax.ShapeDtypeStruct((CORES * rows, wide), i32),
            jax.ShapeDtypeStruct((rows, wide + TILE_SIDE), i32),
        ),
        compiler_params=limit,
        cost_estimate=small,
        name="chip",
    )(lists, both, from_peer(both, lambda x, y, z, c: (x, y, z, c ^ 1)))
    chips = [chip] + [
        from_peer(chip, lambda x, y, z, c, dx=dx: ((x + dx) % grid.rows, y, z, c))
        for dx in range(1, grid.rows)
    ]
    peer_lists = [counted] + [
        from_peer(counted, lambda x, y, z, c, dy=dy: (x, (y + dy) % grid.wide, z, c))
        for dy in range(1, grid.wide)
    ]
    side, depth = grid.summed * group, grid.gathered * group

    formation = pl.CostEstimate(
        flops=2 * rows * slots * TILE_SIDE * grid.rows * group,
        bytes_accessed=2 * side * depth,
        transcendentals=0,
    )
    product = pl.CostEstimate(
        flops=4 * side * depth * width, bytes_accessed=2 * side * depth, transcendentals=0
    )

    def whole(*shape):
        return pl.BlockSpec(shape, lambda k: (0,) * len(shape))

    forward_block, roots = pl.pallas_call(
        functools.partial(forward_block_kernel, grid, slots),
        grid=(grid.summed,),
        in_specs=[smem]
        + [whole(CORES * rows, wide)] * grid.rows
        + [whole(rows, wide + TILE_SIDE)] * grid.wide,
        out_specs=(pl.BlockSpec((group, depth), lambda k: (k, 0)), whole(rows, TILE_SIDE)),
        out_shape=(
            jax.ShapeDtypeStruct((side, depth), bf16),
            jax.ShapeDtypeStruct((rows, TILE_SIDE), f32),
        ),
        scratch_shapes=[pltpu.VMEM((grid.rows, CORES * rows, wide), i32)],
        compiler_params=limit,
        cost_estimate=pl.CostEstimate(flops=2**16, bytes_accessed=2**16, transcendentals=0),
        name="forward_block",
    )(me, *chips, *peer_lists)
    along[-1], forward_block = lax.optimization_barrier((along[-1], forward_block))
    gathered = to_cores(along)
    scale, *sums = pl.pallas_call(
        functools.partial(forward_sum_kernel, grid),
        grid=(grid.summed,),
        in_specs=[smem, whole(rows, TILE_SIDE), pl.BlockSpec((group, depth), lambda k: (k, 0))]
        + [whole(group, width)] * grid.gathered,
        out_specs=(whole(group, width),) * (1 + grid.summed),
        out_shape=(jax.ShapeDtypeStruct((group, width), f32),) * (1 + grid.summed),
        scratch_shapes=[pltpu.VMEM((depth, 2 * width), bf16)],
        compiler_params=limit,
        cost_estimate=product,
        name="forward_sum",
    )(me, roots, forward_block, *gathered)
    *peer_lists, sums[0] = lax.optimization_barrier((*peer_lists, sums[0]))
    backward_block = pl.pallas_call(
        functools.partial(backward_block_kernel, grid, slots),
        grid=(grid.gathered,),
        in_specs=[smem] + [pl.BlockSpec((rows, wide + TILE_SIDE), lambda g: (0, 0))] * grid.wide,
        out_specs=pl.BlockSpec((side, group), lambda g: (0, g)),
        out_shape=jax.ShapeDtypeStruct((side, depth), bf16),
        compiler_params=limit,
        cost_estimate=formation,
        name="backward_block",
    )(me, *peer_lists)
    sums = to_owners(sums)
    sums[-1], backward_block = lax.optimization_barrier((sums[-1], backward_block))

    part_shape = jax.ShapeDtypeStruct((width // grid.summed * 2, width), f32)
    hidden_out, sent, *parts = pl.pallas_call(
        functools.partial(middle_kernel, grid),
        in_specs=[smem] + [vmem] * (6 + grid.summed),
        out_shape=(
            jax.ShapeDtypeStruct((group, hidden), f32),
            jax.ShapeDtypeStruct((group, width), f32),
        )
        + (part_shape,) * grid.summed,
        scratch_shapes=[pltpu.VMEM((grid.summed, *part_shape.shape), f32)],
        compiler_params=limit,
        cost_estimate=pl.CostEstimate(
            flops=36 * group * width * hidden, bytes_accessed=2**20, transcendentals=2**18
        ),
        name="middle",
    )(me, scale, features, weight, out_bias.reshape(1, hidden), cotangent, drop_keep, *sums)

    along = along_z([sent] * DEPTH)
    share = pl.pallas_call(
        add_kernel,
        out_shape=part_shape,
        compiler_params=limit,
        cost_estimate=small,
        name="add_parts",
    )(*to_owners(parts))
    along[-1], share = lax.optimization_barrier((along[-1], share))
    over_z = along_z([share] * DEPTH)
    collected = to_cores(along)
    sums = pl.pallas_call(
        functools.partial(backward_sum_kernel, grid),
        grid_spec=pltpu.PrefetchScalarGridSpec(
            num_scalar_prefetch=1,
            grid=(grid.summed,),
            in_specs=[pl.BlockSpec((group, depth), lambda k, me_ref: (backward_row(k, me_ref), 0))]
            + [pl.BlockSpec((group, width), lambda k, me_ref: (0, 0))] * grid.gathered,
            out_specs=(pl.BlockSpec((group, width), lambda k, me_ref: (0, 0)),) * grid.summed,
            scratch_shapes=[pltpu.VMEM((depth, 2 * width), bf16)],
        ),
        out_shape=(jax.ShapeDtypeStruct((group, width), f32),) * grid.summed,
        compiler_params=limit,
        cost_estimate=product,
        name="backward_sum",
    )(me, backward_block, *collected)
    first, *over_z = lax.optimization_barrier((sums[0], *over_z))
    sums = [first, *sums[1:]]
    share = pl.pallas_call(
        functools.partial(add_along_z_kernel, grid),
        in_specs=[smem] + [vmem] * DEPTH,
        out_shape=part_shape,
        scratch_shapes=[pltpu.VMEM((DEPTH, *part_shape.shape), f32)],
        compiler_params=limit,
        cost_estimate=small,
        name="add_along_z",
    )(me, *over_z)
    shares = [share, from_peer(share, lambda x, y, z, c: (x, y, z, c ^ 1))]
    share = pl.pallas_call(
        add_kernel,
        out_shape=part_shape,
        compiler_params=limit,
        cost_estimate=small,
        name="add_cores",
    )(*shares)
    sums = to_owners(sums)
    parts = to_owners([share] * grid.summed)
    grad_features, grad_weight = pl.pallas_call(
        functools.partial(finish_kernel, grid),
        in_specs=[smem] + [vmem] * (2 + 2 * grid.summed),
        out_shape=(
            jax.ShapeDtypeStruct((group, width), f32),
            jax.ShapeDtypeStruct((width, hidden), f32),
        ),
        scratch_shapes=[pltpu.VMEM((grid.summed, *part_shape.shape), f32)],
        compiler_params=limit,
        cost_estimate=pl.CostEstimate(flops=2**18, bytes_accessed=2**19, transcendentals=0),
        name="finish",
    )(me, scale, sent, *sums, *parts)
    return (hidden_out, grad_features, grad_weight)


def solution(mesh):
    in_specs = (
        P(("row", "col"), None),
        P(),
        P(),
        P(("row", "col"), None),
        P(("row", "col"), None),
        P("row", "col", None, None),
        P("row", "col", None, None),
        P("row", "col", None, None),
        P("row", "col", None, None),
    )
    out_specs = (P(("row", "col"), None), P(("row", "col"), None), P())
    return jax.shard_map(shards, mesh=mesh, in_specs=in_specs, out_specs=out_specs, check_vma=False)
```

```python
import functools

import jax
import jax.numpy as jnp
from jax import lax
from jax.experimental import pallas as pl
from jax.experimental.pallas import tpu as pltpu
from jax.sharding import PartitionSpec as P

TILE_SIDE = 128
TPR = 4
EPT = 64
KEEP_RATE = 0.9
CORES = 2
DEPTH = 4

f32 = jnp.float32
bf16 = jnp.bfloat16
i32 = jnp.int32
highest = lax.Precision.HIGHEST
NT = (((1,), (1,)), ((), ()))
TN = (((0,), (0,)), ((), ()))
MIB = 1 << 20


class Grid:
    def __init__(self, rows, cols, group):
        self.rows, self.cols, self.group = rows, cols, group
        self.wide = cols // (DEPTH * CORES)
        self.count = rows * cols
        self.per = group // TILE_SIDE
        self.gathered = DEPTH * CORES
        self.summed = rows * self.wide

    def place(self, me):
        col = lax.rem(me, self.cols)
        core = lax.rem(col, CORES)
        rest = lax.div(col, CORES)
        return lax.div(me, self.cols), lax.rem(rest, self.wide), lax.div(rest, self.wide), core

    def col(self, z, y, core):
        return (z * self.wide + y) * CORES + core

    def number(self, x, y, z, core):
        return x * self.cols + self.col(z, y, core)

    def all_places(self):
        return [
            (x, y, z, core)
            for x in range(self.rows)
            for z in range(DEPTH)
            for y in range(self.wide)
            for core in range(CORES)
        ]

    def pairs(self, move):
        return [(self.number(*p), self.number(*move(*p))) for p in self.all_places()]


def gelu_exact(values):
    return 0.5 * values * (1.0 + lax.erf(values * 0.7071067811865476))


def gelu_slope(values):
    return (
        0.5 * (1.0 + lax.erf(values * 0.7071067811865476))
        + values * jnp.exp(-0.5 * values * values) * 0.3989422804014327
    )


def one_hot(index_row, size):
    places = lax.broadcasted_iota(i32, (size, index_row.shape[1]), 0)
    return jnp.where(places == index_row, 1.0, 0.0).astype(bf16)


def narrow_one_hot(index_row, places):
    index = index_row.astype(f32).astype(bf16)
    return jnp.where(places == index, jnp.ones((), bf16), jnp.zeros((), bf16))


def turned_times(values, table):
    return lax.dot_general(
        values.astype(f32).astype(bf16), table, TN, preferred_element_type=f32
    ).astype(i32)


def pack_kernel(grid, me_ref, *refs):
    hbm_refs, lists_ref, sent_refs, refs = refs[:4], refs[4], refs[5 : 5 + DEPTH], refs[5 + DEPTH :]
    counts_ref, vmem_refs, sem = refs[0], refs[1:5], refs[5]
    copies = [
        pltpu.make_async_copy(a, b, sem.at[n]) for n, (a, b) in enumerate(zip(hbm_refs, vmem_refs))
    ]
    for copy in copies:
        copy.start()
    for copy in copies:
        copy.wait()
    cols_ref, tile_counts_ref, pos_ref, keep_ref = vmem_refs
    rows, slots = pos_ref.shape
    slot = lax.broadcasted_iota(i32, (rows, slots), 1)
    tile_of = lax.broadcasted_iota(i32, (TPR, slots), 1) // EPT
    spread = jnp.where(tile_of == lax.broadcasted_iota(i32, (TPR, slots), 0), 1.0, 0.0)
    count = turned_times(tile_counts_ref[...], spread.astype(bf16))
    live = ((slot & (EPT - 1)) < count) & (keep_ref[...] == 1)
    pos = jnp.where(live, pos_ref[...], -1)
    lists_ref[:, :slots] = pos
    lane = lax.broadcasted_iota(i32, (TPR, TILE_SIDE), 1)
    k = lax.broadcasted_iota(i32, (TPR, TILE_SIDE), 0)
    lists_ref[:, slots:] = turned_times(cols_ref[...], jnp.where(lane == k, 1.0, 0.0).astype(bf16))
    target = lax.shift_right_arithmetic(pos, 7)
    ones = jnp.ones((8, slots), bf16)
    for t in range(rows):
        hot = one_hot(target[t : t + 1, :], TILE_SIDE)
        sums = lax.dot_general(ones, hot, NT, preferred_element_type=f32)
        counts_ref[t : t + 1, :] = sums[0:1, :].astype(i32)
    _, _, z, _ = grid.place(me_ref[0])
    plane = rows // DEPTH
    for dz, sent_ref in enumerate(sent_refs):
        at = pl.multiple_of((z ^ dz) * plane, 8)
        sent_ref[:, : slots + TILE_SIDE] = lists_ref[pl.ds(at, plane), :]
        for q in range(DEPTH):
            lanes = slice(slots + (q + 1) * TILE_SIDE, slots + (q + 2) * TILE_SIDE)
            sent_ref[:, lanes] = counts_ref[q * plane : (q + 1) * plane, :]


def plane_kernel(wide, *refs):
    got, both_ref = refs[:-1], refs[-1]
    plane = got[0].shape[0]
    for dz, ref in enumerate(got):
        both_ref[dz * plane : (dz + 1) * plane, :wide] = ref[:, :wide]
    for q in range(DEPTH):
        lanes = slice(wide + q * TILE_SIDE, wide + (q + 1) * TILE_SIDE)
        count = got[0][:, lanes]
        for ref in got[1:]:
            count = count + ref[:, lanes]
        both_ref[q * plane : (q + 1) * plane, wide:] = count


def keep_kernel(*refs):
    half = len(refs) // 2
    for ref, kept_ref in zip(refs[:half], refs[half:]):
        kept_ref[...] = ref[...]


def chip_kernel(wide, lists_ref, own_ref, other_ref, chip_ref, counted_ref):
    rows = own_ref.shape[0]
    chip_ref[:rows, :] = own_ref[:, :wide]
    chip_ref[rows:, :] = other_ref[:, :wide]
    counted_ref[:, :wide] = lists_ref[...]
    counted_ref[:, wide:] = own_ref[:, wide:] + other_ref[:, wide:]


def add_kernel(*refs):
    total = refs[0][...]
    for ref in refs[1:-1]:
        total = total + ref[...]
    refs[-1][...] = total


def add_along_z_kernel(grid, me_ref, *refs):
    parts, (out_ref, placed_ref) = refs[:-2], refs[-2:]
    _, _, z, _ = grid.place(me_ref[0])
    for dz, ref in enumerate(parts):
        placed_ref[z ^ dz] = ref[...]
    total = placed_ref[0]
    for n in range(1, DEPTH):
        total = total + placed_ref[n]
    out_ref[...] = total


def slot_columns(columns, first, slots):
    tile = lax.broadcasted_iota(i32, (1, slots), 1) // EPT
    spread = jnp.broadcast_to(columns[:, first : first + 1], (1, slots))
    for k in range(1, TPR):
        spread = jnp.where(tile == k, columns[:, first + k : first + k + 1], spread)
    return spread


def split_values(grid, values, both_ref, scale_of=None):
    width = values[0].shape[1]
    for g, ref in enumerate(values):
        value = ref[...]
        if scale_of is not None:
            value = value * scale_of(g)
        high = value.astype(bf16)
        rows = slice(g * grid.group, (g + 1) * grid.group)
        both_ref[rows, :width] = high
        both_ref[rows, width:] = (value - high.astype(f32)).astype(bf16)


def forward_block_kernel(grid, slots, me_ref, *refs):
    chip_refs, refs = refs[: grid.rows], refs[grid.rows :]
    counted_refs, (block_ref, root_ref, lists_ref) = refs[: grid.wide], refs[grid.wide :]
    step = pl.program_id(0)
    x, y, _, core = grid.place(me_ref[0])
    wide = slots + TILE_SIDE
    rows = counted_refs[0].shape[0]

    @pl.when(step == 0)
    def _():
        count = sum(ref[:, wide:] for ref in counted_refs)
        root_ref[...] = lax.rsqrt(1.0 + count.astype(f32))
        for n, ref in enumerate(chip_refs):
            lists_ref[n] = ref[...]

    dx, dy = lax.rem(step, grid.rows), lax.div(step, grid.rows)
    to_y = lax.rem(y + dy, grid.wide)
    plane = grid.wide * CORES * grid.per
    places = lax.broadcasted_iota(i32, (grid.group, slots), 0).astype(f32).astype(bf16)
    for g in range(grid.gathered):
        for s in range(grid.per):
            at = (g % CORES) * rows + (g // CORES) * plane + (to_y * CORES + core) * grid.per + s
            row = lists_ref[dx, pl.ds(at, 1), :]
            pos = row[:, :slots]
            target = lax.shift_right_arithmetic(pos, 7)
            source = slot_columns(row[:, slots:], 0, slots) * TILE_SIDE + (pos & (TILE_SIDE - 1))
            hot = lax.dot_general(
                narrow_one_hot(target, places[:TILE_SIDE]),
                narrow_one_hot(source - x * grid.group, places),
                NT,
                preferred_element_type=f32,
            )
            block_ref[
                s * TILE_SIDE : (s + 1) * TILE_SIDE, g * grid.group : (g + 1) * grid.group
            ] = hot.astype(bf16)


def forward_sum_kernel(grid, me_ref, root_ref, block_ref, *refs):
    values, (scale_ref, *outs, both_ref) = refs[: grid.gathered], refs[grid.gathered :]
    width = values[0].shape[1]
    step = pl.program_id(0)

    @pl.when(step == 0)
    def _():
        _, y, z, core = grid.place(me_ref[0])

        def scale_of(g):
            at = grid.col(z ^ (g // CORES), y, core ^ (g % CORES)) * grid.per
            return spread_down([root_ref[pl.ds(at + s, 1), :] for s in range(grid.per)])

        scale_ref[...] = scale_of(0)
        split_values(grid, values, both_ref, scale_of)

    part = jnp.dot(block_ref[...], both_ref[...], preferred_element_type=f32)
    total = part[:, :width] + part[:, width:]
    for k, out_ref in enumerate(outs):

        @pl.when(step == k)
        def _(out_ref=out_ref):
            out_ref[...] = total


def backward_block_kernel(grid, slots, me_ref, *refs):
    lists, block_ref = refs[:-1], refs[-1]
    g = pl.program_id(0)
    x, y, z, core = grid.place(me_ref[0])
    col = grid.col(z ^ lax.div(g, CORES), y, core ^ lax.rem(g, CORES))
    side = grid.rows * grid.group
    for k, list_ref in enumerate(lists):
        for s in range(grid.per):
            row = list_ref[pl.ds(col * grid.per + s, 1), :]
            pos = row[:, :slots]
            target = lax.shift_right_arithmetic(pos, 7)
            source = slot_columns(row[:, slots:], 0, slots) * TILE_SIDE + (pos & (TILE_SIDE - 1))
            hot = lax.dot_general(
                one_hot(source, side), one_hot(target, TILE_SIDE), NT, preferred_element_type=f32
            )
            block_ref[k * side : (k + 1) * side, s * TILE_SIDE : (s + 1) * TILE_SIDE] = hot.astype(
                bf16
            )


def spread_down(rows):
    return jnp.concatenate(
        [jnp.broadcast_to(row, (TILE_SIDE, TILE_SIDE)).T for row in rows], axis=0
    )


def backward_sum_kernel(grid, me_ref, block_ref, *refs):
    values, (*outs, both_ref) = refs[: grid.gathered], refs[grid.gathered :]
    width = values[0].shape[1]
    step = pl.program_id(0)

    @pl.when(step == 0)
    def _():
        split_values(grid, values, both_ref)

    part = jnp.dot(block_ref[...], both_ref[...], preferred_element_type=f32)
    total = part[:, :width] + part[:, width:]
    for k, out_ref in enumerate(outs):

        @pl.when(step == k)
        def _(out_ref=out_ref):
            out_ref[...] = total


def finish_kernel(grid, me_ref, scale_ref, sent_ref, *refs):
    sums, refs = refs[: grid.summed], refs[grid.summed :]
    parts, (features_grad_ref, weight_grad_ref, parts_ref) = refs[:-3], refs[-3:]
    x, y, z, core = grid.place(me_ref[0])
    total = sent_ref[...]
    for ref in sums:
        total = total + ref[...]
    features_grad_ref[...] = scale_ref[...] * total
    for k, ref in enumerate(parts):
        from_x = lax.rem(x + grid.rows - k % grid.rows, grid.rows)
        from_y = lax.rem(y + grid.wide - k // grid.rows, grid.wide)
        parts_ref[from_y * grid.rows + from_x] = ref[...]
    high = parts_ref.shape[1] // 2
    for n in range(grid.summed):
        part = parts_ref[n]
        weight_grad_ref[n * high : (n + 1) * high, :] = jnp.concatenate(
            [part[:high, :], part[high:, :]], axis=1
        )


def middle_kernel(
    grid,
    me_ref,
    scale_ref,
    features_ref,
    weight_ref,
    bias_ref,
    cotangent_ref,
    drop_ref,
    *refs,
):
    sums, refs = refs[: grid.summed], refs[grid.summed :]
    hidden_ref, sent_ref, *part_refs, parts_ref = refs
    x, y, _, _ = grid.place(me_ref[0])
    scale = scale_ref[...]
    total = scale * features_ref[...]
    for ref in sums:
        total = total + ref[...]
    mixed = scale * total
    weight = weight_ref[...]
    pre_act = jnp.dot(mixed, weight, precision=highest, preferred_element_type=f32) + bias_ref[...]
    dropout = drop_ref[...].astype(f32) / KEEP_RATE
    hidden_ref[...] = gelu_exact(pre_act) * dropout
    grad_pre = cotangent_ref[...] * dropout * gelu_slope(pre_act)
    sent_ref[...] = scale * lax.dot_general(
        grad_pre, weight, NT, precision=highest, preferred_element_type=f32
    )
    weight_grad = lax.dot_general(
        mixed, grad_pre, TN, precision=highest, preferred_element_type=f32
    )
    width = features_ref.shape[1]
    high = width // grid.summed
    for n in range(grid.summed):
        part = weight_grad[n * high : (n + 1) * high, :]
        parts_ref[n] = jnp.concatenate([part[:, :width], part[:, width:]], axis=0)
    for k, part_ref in enumerate(part_refs):
        to_x = lax.rem(x + k % grid.rows, grid.rows)
        to_y = lax.rem(y + k // grid.rows, grid.wide)
        part_ref[...] = parts_ref[to_y * grid.rows + to_x]


def shards(
    features,
    weight,
    out_bias,
    cotangent,
    drop_keep,
    tile_cols,
    tile_edge_counts,
    edge_pos,
    edge_keep_bits,
):
    group, width = features.shape
    hidden = weight.shape[1]
    rows, slots = edge_pos.shape[2:]
    grid = Grid(lax.axis_size("row"), lax.axis_size("col"), group)
    both_axes = ("row", "col")
    me = lax.axis_index(both_axes).astype(i32)[None]
    smem = pl.BlockSpec(memory_space=pltpu.SMEM)
    vmem = pl.BlockSpec(memory_space=pltpu.VMEM)
    limit = pltpu.CompilerParams(vmem_limit_bytes=24 * MIB)

    def toward(dz):
        return grid.pairs(lambda x, y, z, c: (x, y, z ^ dz, c))

    def along_z(blocks):
        return [blocks[0]] + [
            lax.ppermute(blocks[dz], both_axes, toward(dz)) for dz in range(1, DEPTH)
        ]

    def to_cores(blocks):
        others = [
            lax.ppermute(block, both_axes, grid.pairs(lambda x, y, z, c: (x, y, z, c ^ 1)))
            for block in blocks
        ]
        return [block for pair in zip(blocks, others) for block in pair]

    def backward_row(k, me_ref):
        x, _, _, _ = grid.place(me_ref[0])
        to_x = lax.rem(x + lax.rem(k, grid.rows), grid.rows)
        return lax.div(k, grid.rows) * grid.rows + to_x

    sum_order = [(dx, dy) for dy in range(grid.wide) for dx in range(grid.rows)]

    def to_owners(sums):
        got = [sums[0]]
        for part, (dx, dy) in list(zip(sums, sum_order))[1:]:
            got.append(
                lax.ppermute(
                    part,
                    both_axes,
                    grid.pairs(
                        lambda x, y, z, c, dx=dx, dy=dy: (
                            (x + dx) % grid.rows,
                            (y + dy) % grid.wide,
                            z,
                            c,
                        )
                    ),
                )
            )
        return got

    wide = slots + TILE_SIDE
    plane = rows // DEPTH
    raw = [tile_cols[0, 0].T, tile_edge_counts[0, 0].T, edge_pos[0, 0], edge_keep_bits[0, 0]]
    lists, *planes = pl.pallas_call(
        functools.partial(pack_kernel, grid),
        in_specs=[smem] + [pl.BlockSpec(memory_space=pltpu.HBM)] * 4,
        out_shape=(jax.ShapeDtypeStruct((rows, wide), i32),)
        + (jax.ShapeDtypeStruct((plane, wide + DEPTH * TILE_SIDE), i32),) * DEPTH,
        scratch_shapes=[pltpu.VMEM((rows, TILE_SIDE), i32)]
        + [pltpu.VMEM(a.shape, i32) for a in raw]
        + [pltpu.SemaphoreType.DMA((4,))],
        compiler_params=pltpu.CompilerParams(vmem_limit_bytes=60 * MIB),
        cost_estimate=pl.CostEstimate(flops=2**31, bytes_accessed=2**23, transcendentals=0),
        name="pack",
    )(me, *raw)

    def from_peer(value, move):
        return lax.ppermute(value, both_axes, [(b, a) for a, b in grid.pairs(move)])

    along = [features] + [lax.ppermute(features, both_axes, toward(dz)) for dz in (1, 2)]
    got_planes = along_z(planes)
    lists, got_planes[0] = pl.pallas_call(
        keep_kernel,
        out_shape=tuple(jax.ShapeDtypeStruct(a.shape, i32) for a in (lists, planes[0])),
        compiler_params=limit,
        cost_estimate=pl.CostEstimate(flops=2**21, bytes_accessed=2**20, transcendentals=0),
        name="keep",
    )(lists, planes[0])
    *along, lists, got_planes[0] = lax.optimization_barrier((*along, lists, got_planes[0]))
    *got_planes, later = lax.optimization_barrier((*got_planes, features))
    along += [lax.ppermute(later, both_axes, toward(dz)) for dz in range(3, DEPTH)]
    small = pl.CostEstimate(flops=2**14, bytes_accessed=2**18, transcendentals=0)
    both = pl.pallas_call(
        functools.partial(plane_kernel, wide),
        out_shape=jax.ShapeDtypeStruct((rows, wide + TILE_SIDE), i32),
        compiler_params=limit,
        cost_estimate=small,
        name="plane",
    )(*got_planes)
    chip, counted = pl.pallas_call(
        functools.partial(chip_kernel, wide),
        out_shape=(
            jax.ShapeDtypeStruct((CORES * rows, wide), i32),
            jax.ShapeDtypeStruct((rows, wide + TILE_SIDE), i32),
        ),
        compiler_params=limit,
        cost_estimate=small,
        name="chip",
    )(lists, both, from_peer(both, lambda x, y, z, c: (x, y, z, c ^ 1)))
    chips = [chip] + [
        from_peer(chip, lambda x, y, z, c, dx=dx: ((x + dx) % grid.rows, y, z, c))
        for dx in range(1, grid.rows)
    ]
    peer_lists = [counted] + [
        from_peer(counted, lambda x, y, z, c, dy=dy: (x, (y + dy) % grid.wide, z, c))
        for dy in range(1, grid.wide)
    ]
    side, depth = grid.summed * group, grid.gathered * group

    formation = pl.CostEstimate(
        flops=2 * rows * slots * TILE_SIDE * grid.rows * group,
        bytes_accessed=2 * side * depth,
        transcendentals=0,
    )
    product = pl.CostEstimate(
        flops=4 * side * depth * width, bytes_accessed=2 * side * depth, transcendentals=0
    )

    def whole(*shape):
        return pl.BlockSpec(shape, lambda k: (0,) * len(shape))

    forward_block, roots = pl.pallas_call(
        functools.partial(forward_block_kernel, grid, slots),
        grid=(grid.summed,),
        in_specs=[smem]
        + [whole(CORES * rows, wide)] * grid.rows
        + [whole(rows, wide + TILE_SIDE)] * grid.wide,
        out_specs=(pl.BlockSpec((group, depth), lambda k: (k, 0)), whole(rows, TILE_SIDE)),
        out_shape=(
            jax.ShapeDtypeStruct((side, depth), bf16),
            jax.ShapeDtypeStruct((rows, TILE_SIDE), f32),
        ),
        scratch_shapes=[pltpu.VMEM((grid.rows, CORES * rows, wide), i32)],
        compiler_params=limit,
        cost_estimate=pl.CostEstimate(flops=2**16, bytes_accessed=2**16, transcendentals=0),
        name="forward_block",
    )(me, *chips, *peer_lists)
    along[-1], forward_block = lax.optimization_barrier((along[-1], forward_block))
    gathered = to_cores(along)
    scale, *sums = pl.pallas_call(
        functools.partial(forward_sum_kernel, grid),
        grid=(grid.summed,),
        in_specs=[smem, whole(rows, TILE_SIDE), pl.BlockSpec((group, depth), lambda k: (k, 0))]
        + [whole(group, width)] * grid.gathered,
        out_specs=(whole(group, width),) * (1 + grid.summed),
        out_shape=(jax.ShapeDtypeStruct((group, width), f32),) * (1 + grid.summed),
        scratch_shapes=[pltpu.VMEM((depth, 2 * width), bf16)],
        compiler_params=limit,
        cost_estimate=product,
        name="forward_sum",
    )(me, roots, forward_block, *gathered)
    *peer_lists, sums[0] = lax.optimization_barrier((*peer_lists, sums[0]))
    backward_block = pl.pallas_call(
        functools.partial(backward_block_kernel, grid, slots),
        grid=(grid.gathered,),
        in_specs=[smem] + [pl.BlockSpec((rows, wide + TILE_SIDE), lambda g: (0, 0))] * grid.wide,
        out_specs=pl.BlockSpec((side, group), lambda g: (0, g)),
        out_shape=jax.ShapeDtypeStruct((side, depth), bf16),
        compiler_params=limit,
        cost_estimate=formation,
        name="backward_block",
    )(me, *peer_lists)
    sums = to_owners(sums)
    sums[-1], backward_block = lax.optimization_barrier((sums[-1], backward_block))

    part_shape = jax.ShapeDtypeStruct((width // grid.summed * 2, width), f32)
    hidden_out, sent, *parts = pl.pallas_call(
        functools.partial(middle_kernel, grid),
        in_specs=[smem] + [vmem] * (6 + grid.summed),
        out_shape=(
            jax.ShapeDtypeStruct((group, hidden), f32),
            jax.ShapeDtypeStruct((group, width), f32),
        )
        + (part_shape,) * grid.summed,
        scratch_shapes=[pltpu.VMEM((grid.summed, *part_shape.shape), f32)],
        compiler_params=limit,
        cost_estimate=pl.CostEstimate(
            flops=36 * group * width * hidden, bytes_accessed=2**20, transcendentals=2**18
        ),
        name="middle",
    )(me, scale, features, weight, out_bias.reshape(1, hidden), cotangent, drop_keep, *sums)

    along = along_z([sent] * DEPTH)
    share = pl.pallas_call(
        add_kernel,
        out_shape=part_shape,
        compiler_params=limit,
        cost_estimate=small,
        name="add_parts",
    )(*to_owners(parts))
    along[-1], share = lax.optimization_barrier((along[-1], share))
    over_z = along_z([share] * DEPTH)
    collected = to_cores(along)
    sums = pl.pallas_call(
        functools.partial(backward_sum_kernel, grid),
        grid_spec=pltpu.PrefetchScalarGridSpec(
            num_scalar_prefetch=1,
            grid=(grid.summed,),
            in_specs=[pl.BlockSpec((group, depth), lambda k, me_ref: (backward_row(k, me_ref), 0))]
            + [pl.BlockSpec((group, width), lambda k, me_ref: (0, 0))] * grid.gathered,
            out_specs=(pl.BlockSpec((group, width), lambda k, me_ref: (0, 0)),) * grid.summed,
            scratch_shapes=[pltpu.VMEM((depth, 2 * width), bf16)],
        ),
        out_shape=(jax.ShapeDtypeStruct((group, width), f32),) * grid.summed,
        compiler_params=limit,
        cost_estimate=product,
        name="backward_sum",
    )(me, backward_block, *collected)
    first, *over_z = lax.optimization_barrier((sums[0], *over_z))
    sums = [first, *sums[1:]]
    share = pl.pallas_call(
        functools.partial(add_along_z_kernel, grid),
        in_specs=[smem] + [vmem] * DEPTH,
        out_shape=part_shape,
        scratch_shapes=[pltpu.VMEM((DEPTH, *part_shape.shape), f32)],
        compiler_params=limit,
        cost_estimate=small,
        name="add_along_z",
    )(me, *over_z)
    shares = [share, from_peer(share, lambda x, y, z, c: (x, y, z, c ^ 1))]
    share = pl.pallas_call(
        add_kernel,
        out_shape=part_shape,
        compiler_params=limit,
        cost_estimate=small,
        name="add_cores",
    )(*shares)
    sums = to_owners(sums)
    parts = to_owners([share] * grid.summed)
    grad_features, grad_weight = pl.pallas_call(
        functools.partial(finish_kernel, grid),
        in_specs=[smem] + [vmem] * (2 + 2 * grid.summed),
        out_shape=(
            jax.ShapeDtypeStruct((group, width), f32),
            jax.ShapeDtypeStruct((width, hidden), f32),
        ),
        scratch_shapes=[pltpu.VMEM((grid.summed, *part_shape.shape), f32)],
        compiler_params=limit,
        cost_estimate=pl.CostEstimate(flops=2**18, bytes_accessed=2**19, transcendentals=0),
        name="finish",
    )(me, scale, sent, *sums, *parts)
    return (hidden_out, grad_features, grad_weight)


def solution(mesh):
    in_specs = (
        P(("row", "col"), None),
        P(),
        P(),
        P(("row", "col"), None),
        P(("row", "col"), None),
        P("row", "col", None, None),
        P("row", "col", None, None),
        P("row", "col", None, None),
        P("row", "col", None, None),
    )
    out_specs = (P(("row", "col"), None), P(("row", "col"), None), P())
    return jax.shard_map(shards, mesh=mesh, in_specs=in_specs, out_specs=out_specs, check_vma=False)
```

```python
import functools

import jax
import jax.numpy as jnp
from jax import lax
from jax.experimental import pallas as pl
from jax.experimental.pallas import tpu as pltpu
from jax.sharding import PartitionSpec as P

TILE_SIDE = 128
TPR = 4
EPT = 64
KEEP_RATE = 0.9
CORES = 2
DEPTH = 4

f32 = jnp.float32
bf16 = jnp.bfloat16
i32 = jnp.int32
highest = lax.Precision.HIGHEST
NT = (((1,), (1,)), ((), ()))
TN = (((0,), (0,)), ((), ()))
MIB = 1 << 20


class Grid:
    def __init__(self, rows, cols, group):
        self.rows, self.cols, self.group = rows, cols, group
        self.wide = cols // (DEPTH * CORES)
        self.count = rows * cols
        self.per = group // TILE_SIDE
        self.gathered = DEPTH * CORES
        self.summed = rows * self.wide

    def place(self, me):
        col = lax.rem(me, self.cols)
        core = lax.rem(col, CORES)
        rest = lax.div(col, CORES)
        return lax.div(me, self.cols), lax.rem(rest, self.wide), lax.div(rest, self.wide), core

    def col(self, z, y, core):
        return (z * self.wide + y) * CORES + core

    def number(self, x, y, z, core):
        return x * self.cols + self.col(z, y, core)

    def all_places(self):
        return [
            (x, y, z, core)
            for x in range(self.rows)
            for z in range(DEPTH)
            for y in range(self.wide)
            for core in range(CORES)
        ]

    def pairs(self, move):
        return [(self.number(*p), self.number(*move(*p))) for p in self.all_places()]


def gelu_exact(values):
    return 0.5 * values * (1.0 + lax.erf(values * 0.7071067811865476))


def gelu_slope(values):
    return (
        0.5 * (1.0 + lax.erf(values * 0.7071067811865476))
        + values * jnp.exp(-0.5 * values * values) * 0.3989422804014327
    )


def one_hot(index_row, size):
    places = lax.broadcasted_iota(i32, (size, index_row.shape[1]), 0)
    return jnp.where(places == index_row, 1.0, 0.0).astype(bf16)


def turned_times(values, table):
    return lax.dot_general(
        values.astype(f32).astype(bf16), table, TN, preferred_element_type=f32
    ).astype(i32)


def pack_kernel(grid, me_ref, *refs):
    hbm_refs, lists_ref, sent_refs, refs = refs[:4], refs[4], refs[5 : 5 + DEPTH], refs[5 + DEPTH :]
    counts_ref, vmem_refs, sem = refs[0], refs[1:5], refs[5]
    copies = [
        pltpu.make_async_copy(a, b, sem.at[n]) for n, (a, b) in enumerate(zip(hbm_refs, vmem_refs))
    ]
    for copy in copies:
        copy.start()
    for copy in copies:
        copy.wait()
    cols_ref, tile_counts_ref, pos_ref, keep_ref = vmem_refs
    rows, slots = pos_ref.shape
    slot = lax.broadcasted_iota(i32, (rows, slots), 1)
    tile_of = lax.broadcasted_iota(i32, (TPR, slots), 1) // EPT
    spread = jnp.where(tile_of == lax.broadcasted_iota(i32, (TPR, slots), 0), 1.0, 0.0)
    count = turned_times(tile_counts_ref[...], spread.astype(bf16))
    live = ((slot & (EPT - 1)) < count) & (keep_ref[...] == 1)
    pos = jnp.where(live, pos_ref[...], -1)
    lists_ref[:, :slots] = pos
    lane = lax.broadcasted_iota(i32, (TPR, TILE_SIDE), 1)
    k = lax.broadcasted_iota(i32, (TPR, TILE_SIDE), 0)
    lists_ref[:, slots:] = turned_times(cols_ref[...], jnp.where(lane == k, 1.0, 0.0).astype(bf16))
    target = lax.shift_right_arithmetic(pos, 7)
    ones = jnp.ones((8, slots), bf16)
    for t in range(rows):
        hot = one_hot(target[t : t + 1, :], TILE_SIDE)
        sums = lax.dot_general(ones, hot, NT, preferred_element_type=f32)
        counts_ref[t : t + 1, :] = sums[0:1, :].astype(i32)
    _, _, z, _ = grid.place(me_ref[0])
    plane = rows // DEPTH
    for dz, sent_ref in enumerate(sent_refs):
        at = pl.multiple_of((z ^ dz) * plane, 8)
        sent_ref[:, : slots + TILE_SIDE] = lists_ref[pl.ds(at, plane), :]
        for q in range(DEPTH):
            lanes = slice(slots + (q + 1) * TILE_SIDE, slots + (q + 2) * TILE_SIDE)
            sent_ref[:, lanes] = counts_ref[q * plane : (q + 1) * plane, :]


def plane_kernel(wide, *refs):
    got, both_ref = refs[:-1], refs[-1]
    plane = got[0].shape[0]
    for dz, ref in enumerate(got):
        both_ref[dz * plane : (dz + 1) * plane, :wide] = ref[:, :wide]
    for q in range(DEPTH):
        lanes = slice(wide + q * TILE_SIDE, wide + (q + 1) * TILE_SIDE)
        count = got[0][:, lanes]
        for ref in got[1:]:
            count = count + ref[:, lanes]
        both_ref[q * plane : (q + 1) * plane, wide:] = count


def keep_kernel(*refs):
    half = len(refs) // 2
    for ref, kept_ref in zip(refs[:half], refs[half:]):
        kept_ref[...] = ref[...]


def chip_kernel(wide, lists_ref, own_ref, other_ref, chip_ref, counted_ref):
    rows = own_ref.shape[0]
    chip_ref[:rows, :] = own_ref[:, :wide]
    chip_ref[rows:, :] = other_ref[:, :wide]
    counted_ref[:, :wide] = lists_ref[...]
    counted_ref[:, wide:] = own_ref[:, wide:] + other_ref[:, wide:]


def add_kernel(*refs):
    total = refs[0][...]
    for ref in refs[1:-1]:
        total = total + ref[...]
    refs[-1][...] = total


def add_along_z_kernel(grid, me_ref, *refs):
    parts, (out_ref, placed_ref) = refs[:-2], refs[-2:]
    _, _, z, _ = grid.place(me_ref[0])
    for dz, ref in enumerate(parts):
        placed_ref[z ^ dz] = ref[...]
    total = placed_ref[0]
    for n in range(1, DEPTH):
        total = total + placed_ref[n]
    out_ref[...] = total


def slot_columns(columns, first, slots):
    tile = lax.broadcasted_iota(i32, (1, slots), 1) // EPT
    spread = jnp.broadcast_to(columns[:, first : first + 1], (1, slots))
    for k in range(1, TPR):
        spread = jnp.where(tile == k, columns[:, first + k : first + k + 1], spread)
    return spread


def split_values(grid, values, both_ref, scale_of=None):
    width = values[0].shape[1]
    for g, ref in enumerate(values):
        value = ref[...]
        if scale_of is not None:
            value = value * scale_of(g)
        high = value.astype(bf16)
        rows = slice(g * grid.group, (g + 1) * grid.group)
        both_ref[rows, :width] = high
        both_ref[rows, width:] = (value - high.astype(f32)).astype(bf16)


def forward_block_kernel(grid, slots, me_ref, *refs):
    chip_refs, refs = refs[: grid.rows], refs[grid.rows :]
    counted_refs, (block_ref, root_ref, lists_ref) = refs[: grid.wide], refs[grid.wide :]
    step = pl.program_id(0)
    x, y, _, core = grid.place(me_ref[0])
    wide = slots + TILE_SIDE
    rows = counted_refs[0].shape[0]

    @pl.when(step == 0)
    def _():
        count = sum(ref[:, wide:] for ref in counted_refs)
        root_ref[...] = lax.rsqrt(1.0 + count.astype(f32))
        for n, ref in enumerate(chip_refs):
            lists_ref[n] = ref[...]

    dx, dy = lax.rem(step, grid.rows), lax.div(step, grid.rows)
    to_y = lax.rem(y + dy, grid.wide)
    plane = grid.wide * CORES * grid.per
    for g in range(grid.gathered):
        for s in range(grid.per):
            at = (g % CORES) * rows + (g // CORES) * plane + (to_y * CORES + core) * grid.per + s
            row = lists_ref[dx, pl.ds(at, 1), :]
            pos = row[:, :slots]
            target = lax.shift_right_arithmetic(pos, 7)
            source = slot_columns(row[:, slots:], 0, slots) * TILE_SIDE + (pos & (TILE_SIDE - 1))
            hot = lax.dot_general(
                one_hot(target, TILE_SIDE),
                one_hot(source - x * grid.group, grid.group),
                NT,
                preferred_element_type=f32,
            )
            block_ref[
                s * TILE_SIDE : (s + 1) * TILE_SIDE, g * grid.group : (g + 1) * grid.group
            ] = hot.astype(bf16)


def forward_sum_kernel(grid, me_ref, root_ref, block_ref, *refs):
    values, (scale_ref, *outs, both_ref) = refs[: grid.gathered], refs[grid.gathered :]
    width = values[0].shape[1]
    step = pl.program_id(0)

    @pl.when(step == 0)
    def _():
        _, y, z, core = grid.place(me_ref[0])

        def scale_of(g):
            at = grid.col(z ^ (g // CORES), y, core ^ (g % CORES)) * grid.per
            return spread_down([root_ref[pl.ds(at + s, 1), :] for s in range(grid.per)])

        scale_ref[...] = scale_of(0)
        split_values(grid, values, both_ref, scale_of)

    part = jnp.dot(block_ref[...], both_ref[...], preferred_element_type=f32)
    total = part[:, :width] + part[:, width:]
    for k, out_ref in enumerate(outs):

        @pl.when(step == k)
        def _(out_ref=out_ref):
            out_ref[...] = total


def backward_block_kernel(grid, slots, me_ref, *refs):
    lists, block_ref = refs[:-1], refs[-1]
    g = pl.program_id(0)
    x, y, z, core = grid.place(me_ref[0])
    col = grid.col(z ^ lax.div(g, CORES), y, core ^ lax.rem(g, CORES))
    side = grid.rows * grid.group
    for k, list_ref in enumerate(lists):
        for s in range(grid.per):
            row = list_ref[pl.ds(col * grid.per + s, 1), :]
            pos = row[:, :slots]
            target = lax.shift_right_arithmetic(pos, 7)
            source = slot_columns(row[:, slots:], 0, slots) * TILE_SIDE + (pos & (TILE_SIDE - 1))
            hot = lax.dot_general(
                one_hot(source, side), one_hot(target, TILE_SIDE), NT, preferred_element_type=f32
            )
            block_ref[k * side : (k + 1) * side, s * TILE_SIDE : (s + 1) * TILE_SIDE] = hot.astype(
                bf16
            )


def spread_down(rows):
    return jnp.concatenate(
        [jnp.broadcast_to(row, (TILE_SIDE, TILE_SIDE)).T for row in rows], axis=0
    )


def backward_sum_kernel(grid, me_ref, block_ref, *refs):
    values, (*outs, both_ref) = refs[: grid.gathered], refs[grid.gathered :]
    width = values[0].shape[1]
    step = pl.program_id(0)

    @pl.when(step == 0)
    def _():
        split_values(grid, values, both_ref)

    part = jnp.dot(block_ref[...], both_ref[...], preferred_element_type=f32)
    total = part[:, :width] + part[:, width:]
    for k, out_ref in enumerate(outs):

        @pl.when(step == k)
        def _(out_ref=out_ref):
            out_ref[...] = total


def finish_kernel(grid, me_ref, scale_ref, sent_ref, *refs):
    sums, refs = refs[: grid.summed], refs[grid.summed :]
    parts, (features_grad_ref, weight_grad_ref, parts_ref) = refs[:-3], refs[-3:]
    x, y, z, core = grid.place(me_ref[0])
    total = sent_ref[...]
    for ref in sums:
        total = total + ref[...]
    features_grad_ref[...] = scale_ref[...] * total
    for k, ref in enumerate(parts):
        from_x = lax.rem(x + grid.rows - k % grid.rows, grid.rows)
        from_y = lax.rem(y + grid.wide - k // grid.rows, grid.wide)
        parts_ref[from_y * grid.rows + from_x] = ref[...]
    high = parts_ref.shape[1] // 2
    for n in range(grid.summed):
        part = parts_ref[n]
        weight_grad_ref[n * high : (n + 1) * high, :] = jnp.concatenate(
            [part[:high, :], part[high:, :]], axis=1
        )


def middle_kernel(
    grid,
    me_ref,
    scale_ref,
    features_ref,
    weight_ref,
    bias_ref,
    cotangent_ref,
    drop_ref,
    *refs,
):
    sums, refs = refs[: grid.summed], refs[grid.summed :]
    hidden_ref, sent_ref, *part_refs, parts_ref = refs
    x, y, _, _ = grid.place(me_ref[0])
    scale = scale_ref[...]
    total = scale * features_ref[...]
    for ref in sums:
        total = total + ref[...]
    mixed = scale * total
    weight = weight_ref[...]
    pre_act = jnp.dot(mixed, weight, precision=highest, preferred_element_type=f32) + bias_ref[...]
    dropout = drop_ref[...].astype(f32) / KEEP_RATE
    hidden_ref[...] = gelu_exact(pre_act) * dropout
    grad_pre = cotangent_ref[...] * dropout * gelu_slope(pre_act)
    sent_ref[...] = scale * lax.dot_general(
        grad_pre, weight, NT, precision=highest, preferred_element_type=f32
    )
    weight_grad = lax.dot_general(
        mixed, grad_pre, TN, precision=highest, preferred_element_type=f32
    )
    width = features_ref.shape[1]
    high = width // grid.summed
    for n in range(grid.summed):
        part = weight_grad[n * high : (n + 1) * high, :]
        parts_ref[n] = jnp.concatenate([part[:, :width], part[:, width:]], axis=0)
    for k, part_ref in enumerate(part_refs):
        to_x = lax.rem(x + k % grid.rows, grid.rows)
        to_y = lax.rem(y + k // grid.rows, grid.wide)
        part_ref[...] = parts_ref[to_y * grid.rows + to_x]


def shards(
    features,
    weight,
    out_bias,
    cotangent,
    drop_keep,
    tile_cols,
    tile_edge_counts,
    edge_pos,
    edge_keep_bits,
):
    group, width = features.shape
    hidden = weight.shape[1]
    rows, slots = edge_pos.shape[2:]
    grid = Grid(lax.axis_size("row"), lax.axis_size("col"), group)
    both_axes = ("row", "col")
    me = lax.axis_index(both_axes).astype(i32)[None]
    smem = pl.BlockSpec(memory_space=pltpu.SMEM)
    vmem = pl.BlockSpec(memory_space=pltpu.VMEM)
    limit = pltpu.CompilerParams(vmem_limit_bytes=24 * MIB)

    def toward(dz):
        return grid.pairs(lambda x, y, z, c: (x, y, z ^ dz, c))

    def along_z(blocks):
        return [blocks[0]] + [
            lax.ppermute(blocks[dz], both_axes, toward(dz)) for dz in range(1, DEPTH)
        ]

    def to_cores(blocks):
        others = [
            lax.ppermute(block, both_axes, grid.pairs(lambda x, y, z, c: (x, y, z, c ^ 1)))
            for block in blocks
        ]
        return [block for pair in zip(blocks, others) for block in pair]

    def backward_row(k, me_ref):
        x, _, _, _ = grid.place(me_ref[0])
        to_x = lax.rem(x + lax.rem(k, grid.rows), grid.rows)
        return lax.div(k, grid.rows) * grid.rows + to_x

    sum_order = [(dx, dy) for dy in range(grid.wide) for dx in range(grid.rows)]

    def to_owners(sums):
        got = [sums[0]]
        for part, (dx, dy) in list(zip(sums, sum_order))[1:]:
            got.append(
                lax.ppermute(
                    part,
                    both_axes,
                    grid.pairs(
                        lambda x, y, z, c, dx=dx, dy=dy: (
                            (x + dx) % grid.rows,
                            (y + dy) % grid.wide,
                            z,
                            c,
                        )
                    ),
                )
            )
        return got

    wide = slots + TILE_SIDE
    plane = rows // DEPTH
    raw = [tile_cols[0, 0].T, tile_edge_counts[0, 0].T, edge_pos[0, 0], edge_keep_bits[0, 0]]
    lists, *planes = pl.pallas_call(
        functools.partial(pack_kernel, grid),
        in_specs=[smem] + [pl.BlockSpec(memory_space=pltpu.HBM)] * 4,
        out_shape=(jax.ShapeDtypeStruct((rows, wide), i32),)
        + (jax.ShapeDtypeStruct((plane, wide + DEPTH * TILE_SIDE), i32),) * DEPTH,
        scratch_shapes=[pltpu.VMEM((rows, TILE_SIDE), i32)]
        + [pltpu.VMEM(a.shape, i32) for a in raw]
        + [pltpu.SemaphoreType.DMA((4,))],
        compiler_params=pltpu.CompilerParams(vmem_limit_bytes=60 * MIB),
        cost_estimate=pl.CostEstimate(flops=2**31, bytes_accessed=2**23, transcendentals=0),
        name="pack",
    )(me, *raw)

    def from_peer(value, move):
        return lax.ppermute(value, both_axes, [(b, a) for a, b in grid.pairs(move)])

    along = [features] + [lax.ppermute(features, both_axes, toward(dz)) for dz in (1, 2)]
    got_planes = along_z(planes)
    lists, got_planes[0] = pl.pallas_call(
        keep_kernel,
        out_shape=tuple(jax.ShapeDtypeStruct(a.shape, i32) for a in (lists, planes[0])),
        compiler_params=limit,
        cost_estimate=pl.CostEstimate(flops=2**21, bytes_accessed=2**20, transcendentals=0),
        name="keep",
    )(lists, planes[0])
    *along, lists, got_planes[0] = lax.optimization_barrier((*along, lists, got_planes[0]))
    *got_planes, later = lax.optimization_barrier((*got_planes, features))
    along += [lax.ppermute(later, both_axes, toward(dz)) for dz in range(3, DEPTH)]
    small = pl.CostEstimate(flops=2**14, bytes_accessed=2**18, transcendentals=0)
    both = pl.pallas_call(
        functools.partial(plane_kernel, wide),
        out_shape=jax.ShapeDtypeStruct((rows, wide + TILE_SIDE), i32),
        compiler_params=limit,
        cost_estimate=small,
        name="plane",
    )(*got_planes)
    chip, counted = pl.pallas_call(
        functools.partial(chip_kernel, wide),
        out_shape=(
            jax.ShapeDtypeStruct((CORES * rows, wide), i32),
            jax.ShapeDtypeStruct((rows, wide + TILE_SIDE), i32),
        ),
        compiler_params=limit,
        cost_estimate=small,
        name="chip",
    )(lists, both, from_peer(both, lambda x, y, z, c: (x, y, z, c ^ 1)))
    chips = [chip] + [
        from_peer(chip, lambda x, y, z, c, dx=dx: ((x + dx) % grid.rows, y, z, c))
        for dx in range(1, grid.rows)
    ]
    peer_lists = [counted] + [
        from_peer(counted, lambda x, y, z, c, dy=dy: (x, (y + dy) % grid.wide, z, c))
        for dy in range(1, grid.wide)
    ]
    side, depth = grid.summed * group, grid.gathered * group

    formation = pl.CostEstimate(
        flops=2 * rows * slots * TILE_SIDE * grid.rows * group,
        bytes_accessed=2 * side * depth,
        transcendentals=0,
    )
    product = pl.CostEstimate(
        flops=4 * side * depth * width, bytes_accessed=2 * side * depth, transcendentals=0
    )

    def whole(*shape):
        return pl.BlockSpec(shape, lambda k: (0,) * len(shape))

    forward_block, roots = pl.pallas_call(
        functools.partial(forward_block_kernel, grid, slots),
        grid=(grid.summed,),
        in_specs=[smem]
        + [whole(CORES * rows, wide)] * grid.rows
        + [whole(rows, wide + TILE_SIDE)] * grid.wide,
        out_specs=(pl.BlockSpec((group, depth), lambda k: (k, 0)), whole(rows, TILE_SIDE)),
        out_shape=(
            jax.ShapeDtypeStruct((side, depth), bf16),
            jax.ShapeDtypeStruct((rows, TILE_SIDE), f32),
        ),
        scratch_shapes=[pltpu.VMEM((grid.rows, CORES * rows, wide), i32)],
        compiler_params=limit,
        cost_estimate=pl.CostEstimate(flops=2**16, bytes_accessed=2**16, transcendentals=0),
        name="forward_block",
    )(me, *chips, *peer_lists)
    gathered = to_cores(along)
    scale, *sums = pl.pallas_call(
        functools.partial(forward_sum_kernel, grid),
        grid=(grid.summed,),
        in_specs=[smem, whole(rows, TILE_SIDE), pl.BlockSpec((group, depth), lambda k: (k, 0))]
        + [whole(group, width)] * grid.gathered,
        out_specs=(whole(group, width),) * (1 + grid.summed),
        out_shape=(jax.ShapeDtypeStruct((group, width), f32),) * (1 + grid.summed),
        scratch_shapes=[pltpu.VMEM((depth, 2 * width), bf16)],
        compiler_params=limit,
        cost_estimate=product,
        name="forward_sum",
    )(me, roots, forward_block, *gathered)
    *peer_lists, sums[0] = lax.optimization_barrier((*peer_lists, sums[0]))
    backward_block = pl.pallas_call(
        functools.partial(backward_block_kernel, grid, slots),
        grid=(grid.gathered,),
        in_specs=[smem] + [pl.BlockSpec((rows, wide + TILE_SIDE), lambda g: (0, 0))] * grid.wide,
        out_specs=pl.BlockSpec((side, group), lambda g: (0, g)),
        out_shape=jax.ShapeDtypeStruct((side, depth), bf16),
        compiler_params=limit,
        cost_estimate=formation,
        name="backward_block",
    )(me, *peer_lists)
    sums = to_owners(sums)
    sums[-1], backward_block = lax.optimization_barrier((sums[-1], backward_block))

    part_shape = jax.ShapeDtypeStruct((width // grid.summed * 2, width), f32)
    hidden_out, sent, *parts = pl.pallas_call(
        functools.partial(middle_kernel, grid),
        in_specs=[smem] + [vmem] * (6 + grid.summed),
        out_shape=(
            jax.ShapeDtypeStruct((group, hidden), f32),
            jax.ShapeDtypeStruct((group, width), f32),
        )
        + (part_shape,) * grid.summed,
        scratch_shapes=[pltpu.VMEM((grid.summed, *part_shape.shape), f32)],
        compiler_params=limit,
        cost_estimate=pl.CostEstimate(
            flops=36 * group * width * hidden, bytes_accessed=2**20, transcendentals=2**18
        ),
        name="middle",
    )(me, scale, features, weight, out_bias.reshape(1, hidden), cotangent, drop_keep, *sums)

    along = along_z([sent] * DEPTH)
    share = pl.pallas_call(
        add_kernel,
        out_shape=part_shape,
        compiler_params=limit,
        cost_estimate=small,
        name="add_parts",
    )(*to_owners(parts))
    along[-1], share = lax.optimization_barrier((along[-1], share))
    over_z = along_z([share] * DEPTH)
    collected = to_cores(along)
    sums = pl.pallas_call(
        functools.partial(backward_sum_kernel, grid),
        grid_spec=pltpu.PrefetchScalarGridSpec(
            num_scalar_prefetch=1,
            grid=(grid.summed,),
            in_specs=[pl.BlockSpec((group, depth), lambda k, me_ref: (backward_row(k, me_ref), 0))]
            + [pl.BlockSpec((group, width), lambda k, me_ref: (0, 0))] * grid.gathered,
            out_specs=(pl.BlockSpec((group, width), lambda k, me_ref: (0, 0)),) * grid.summed,
            scratch_shapes=[pltpu.VMEM((depth, 2 * width), bf16)],
        ),
        out_shape=(jax.ShapeDtypeStruct((group, width), f32),) * grid.summed,
        compiler_params=limit,
        cost_estimate=product,
        name="backward_sum",
    )(me, backward_block, *collected)
    first, *over_z = lax.optimization_barrier((sums[0], *over_z))
    sums = [first, *sums[1:]]
    share = pl.pallas_call(
        functools.partial(add_along_z_kernel, grid),
        in_specs=[smem] + [vmem] * DEPTH,
        out_shape=part_shape,
        scratch_shapes=[pltpu.VMEM((DEPTH, *part_shape.shape), f32)],
        compiler_params=limit,
        cost_estimate=small,
        name="add_along_z",
    )(me, *over_z)
    shares = [share, from_peer(share, lambda x, y, z, c: (x, y, z, c ^ 1))]
    share = pl.pallas_call(
        add_kernel,
        out_shape=part_shape,
        compiler_params=limit,
        cost_estimate=small,
        name="add_cores",
    )(*shares)
    sums = to_owners(sums)
    parts = to_owners([share] * grid.summed)
    grad_features, grad_weight = pl.pallas_call(
        functools.partial(finish_kernel, grid),
        in_specs=[smem] + [vmem] * (2 + 2 * grid.summed),
        out_shape=(
            jax.ShapeDtypeStruct((group, width), f32),
            jax.ShapeDtypeStruct((width, hidden), f32),
        ),
        scratch_shapes=[pltpu.VMEM((grid.summed, *part_shape.shape), f32)],
        compiler_params=limit,
        cost_estimate=pl.CostEstimate(flops=2**18, bytes_accessed=2**19, transcendentals=0),
        name="finish",
    )(me, scale, sent, *sums, *parts)
    return (hidden_out, grad_features, grad_weight)


def solution(mesh):
    in_specs = (
        P(("row", "col"), None),
        P(),
        P(),
        P(("row", "col"), None),
        P(("row", "col"), None),
        P("row", "col", None, None),
        P("row", "col", None, None),
        P("row", "col", None, None),
        P("row", "col", None, None),
    )
    out_specs = (P(("row", "col"), None), P(("row", "col"), None), P())
    return jax.shard_map(shards, mesh=mesh, in_specs=in_specs, out_specs=out_specs, check_vma=False)
```
